256 devices in a mesh: dp: 32 (over x, z), expert: 8 (over y, core).
Axes of the slice: x: 4, y: 4, z: 8, core: 2. Of those that a mesh axis runs over, the one named last changes fastest.
Arguments:
- tokens: bfloat16 [3072, 3072], P(('dp', 'expert')), may hold values from -6 to 6
- cotangent: bfloat16 [3072, 3072], P(('dp', 'expert')), may hold values from -6 to 6
- routes: int32 [3072, 2], P(('dp', 'expert')), may hold values from 0 to 7, all different within a row; in each aligned block of 12 rows (0 to 11, 12 to 23, ...) at most 4 rows name the same one
- example_ids: int32 [32, 96], P('dp', 'expert'), may hold values from 0 to 5, never falling along the last dimension, each value on 1 to 32 neighbouring positions
- w_gate: bfloat16 [8, 3072, 8192], P('expert', None, 'dp'), may hold values from -0.109375 to 0.109375
- w_up: bfloat16 [8, 3072, 8192], P('expert', None, 'dp'), may hold values from -0.109375 to 0.109375
- w_down: bfloat16 [8, 8192, 3072], P('expert', 'dp'), may hold values from -0.0625 to 0.0625
Outputs:
- mixed: bfloat16 [3072, 3072], P(('dp', 'expert'))
- example_norms: float32 [32, 6], P('dp')
- grad_gate: bfloat16 [8, 3072, 8192], P('expert', None, 'dp')
- grad_up: bfloat16 [8, 3072, 8192], P('expert', None, 'dp')
- grad_down: bfloat16 [8, 8192, 3072], P('expert', 'dp')
The draws below stay inside these ranges and needn't reach their ends.
Inputs may be any that keep to these rules, and one draw needn't show every extreme that they name: `routes`: among the tokens of one device each expert is named at most 4 times, and exactly 4 times by some expert. `example_ids`: along a row example numbers never fall and every example has at least one token.
All inputs are finite; a program needn't handle non-finite values.
Results may differ from the reference program's by a relative error of at most 0.0059.
Values may be sent and summed in bfloat16 or wider, within the bound.
No kernel may reach another device: no remote copies, remote signals or barrier semaphores. Data moves between devices by JAX's collectives and lax.ppermute only.
A program may use at most 128 MiB of HBM per device.

```python
import math
import jax
import jax.numpy as jnp
import numpy as np
from jax import lax

D = 3072
FF = 8192
CAP = 4
EX_ROW = 6
TOK_DEV = 12
EXPERTS = 8
ROW_TOK = 96
TOKENS = 3072
EXAMPLES = 192
N_DP = 32
N_EXPERT = 8


def mixed_rows(shared, own, shared_weight, own_weight):
    return jnp.clip(shared_weight * shared + own_weight * own, -6.0, 6.0)


def draw_tokens(key, part):
    key = jax.random.fold_in(key, 11)
    first, second = jax.random.split(key)
    shared = jax.random.normal(first, (1, D), jnp.float32)
    own = jax.random.normal(second, (TOKENS, D), jnp.float32)
    values = mixed_rows(shared, own, 0.7, 0.714)
    return values.astype(jnp.bfloat16)


def draw_cotangent(key, part):
    key = jax.random.fold_in(key, 23)
    first, second = jax.random.split(key)
    shared = jax.random.normal(first, (1, D), jnp.float32)
    own = jax.random.normal(second, (TOKENS, D), jnp.float32)
    values = mixed_rows(shared, own, 0.7, 0.714)
    return values.astype(jnp.bfloat16)


def steps_of(own_key, extent, shards, low, high):
    loudness, own = 1.0, jax.random.fold_in(own_key, 6)
    for position, shards_of in shards:
        draws = jnp.exp(jax.random.uniform(jax.random.fold_in(own, position), (shards_of,), jnp.float32, low / len(shards), high / len(shards)))
        loudness = loudness * jnp.repeat(draws, extent[position] // shards_of).reshape([-1 if axis == position else 1 for axis in range(len(extent))])
    return loudness


def length_profile(amount, total, reach, lean):
    weights = [(1 << 20) // math.isqrt(rank ** lean) + 1 for rank in range(2, amount + 1)]
    rest, holding = total - reach - (amount - 1), [1] * (amount - 1)
    while rest > 0:
        movable = [i for i in range(amount - 1) if holding[i] < reach]
        mass, budget = sum([weights[i] for i in movable]), rest
        for i in movable:
            more = min(reach - holding[i], max(1, budget * weights[i] // mass), rest)
            holding[i] = holding[i] + more
            rest = rest - more
    return np.array([reach] + holding)


def uneven_parts(rng, count, total, bound, skew):
    if count == 2:
        one = jax.random.randint(rng, (), max(1, total - bound), min(bound, total - 1) + 1)
        return jnp.stack([one, total - one])
    lengths = jnp.asarray(length_profile(count, total, bound, skew), jnp.int32)
    pairs = (count - 1) // 2
    giver, receiver = lengths[1:1 + 2 * pairs:2], lengths[2:2 + 2 * pairs:2]
    room = jnp.minimum(giver - 1, bound - receiver)
    shifted = jax.random.randint(jax.random.fold_in(rng, 1), (pairs,), 0, 1 << 20) % (room + 1)
    lengths = lengths.at[1:1 + 2 * pairs:2].set(giver - shifted).at[2:2 + 2 * pairs:2].set(receiver + shifted)
    return lengths[jax.random.permutation(jax.random.fold_in(rng, 2), count)]


def deal_out(rng, own, number, rows, count, top, most, lean):
    sequence = jax.random.permutation(rng, count)
    crowded, usual = portions_of(count, rows * top, most, lean, True), portions_of(count, rows * top, most, lean, False)
    places = jnp.arange(count)

    def named(lengths, offset_by):
        used = int((lengths > 0).sum())
        fixed = max(1, used // 4)
        shifted = fixed + (places - fixed + offset_by * (used - fixed)) % max(1, count - fixed)
        return jnp.zeros((count,), jnp.int32).at[sequence[jnp.where(places < fixed, places, shifted)]].set(jnp.asarray(lengths, jnp.int32))

    lengths = jnp.where(number % 4 == 0, named(crowded, number // 4), named(usual, number - number // 4 - 1))
    mixed = jax.random.permutation(jax.random.fold_in(own, 3), count)
    giver, receiver = mixed[0:count // 2 * 2:2], mixed[1:count // 2 * 2:2]
    margin = jnp.minimum(lengths[giver] - 1, most - lengths[receiver]) // 2
    margin = jnp.where((giver == sequence[0]) | (receiver == sequence[0]) | (lengths[receiver] == 0), 0, jnp.maximum(margin, 0))
    shifted = jax.random.randint(jax.random.fold_in(own, 4), (count // 2,), 0, 1 << 20) % (margin + 1)
    lengths = lengths.at[giver].add(-shifted).at[receiver].add(shifted)
    labels = jnp.searchsorted(jnp.cumsum(lengths), jnp.arange(rows * top), side="right").astype(jnp.int32)
    table = labels.reshape(top, rows).T
    table = table[jax.random.permutation(jax.random.fold_in(own, 1), rows)]
    offset_by = jax.random.randint(jax.random.fold_in(own, 2), (rows, 1), 0, top)
    return jnp.take_along_axis(table, (jnp.arange(top)[None, :] + offset_by) % top, axis=1)


def portions_of(amount, total, most, slope, full):
    weights = [(1 << 20) // math.isqrt(rank ** slope) + 1 for rank in range(1, amount + 1)]
    largest = most if full else min(most, max(-(-total // amount), total * weights[0] // sum(weights)))
    least = 1 if total - largest >= amount - 1 else 0
    holding, surplus = [largest] + [least] * (amount - 1), total - largest - least * (amount - 1)
    while surplus > 0:
        free = [i for i in range(1, amount) if holding[i] < largest] or [i for i in range(1, amount) if holding[i] < most]
        whole, left = sum([weights[i] for i in free]), surplus
        for i in free:
            more = min(most - holding[i], max(1, left * weights[i] // whole), surplus)
            holding[i] = holding[i] + more
            surplus = surplus - more
    return np.array(holding)


def noise(rng, shape, deviation, reach, pieces=(), kind=jnp.bfloat16):
    drawn = deviation * jax.random.normal(rng, shape, jnp.float32)
    if pieces:
        drawn = drawn * steps_of(rng, shape, pieces, -0.22, 0.18)
    return jnp.clip(drawn, -reach, reach).astype(kind)


def setup_inputs(seed: int = 0) -> dict:
    key_list = jax.random.split(jax.random.key(seed), 8)
    tokens = draw_tokens(jax.random.fold_in(key_list[7], 71), 0)
    cotangent = draw_cotangent(jax.random.fold_in(key_list[7], 71), 0)
    routes_keys = jax.random.split(jax.random.fold_in(key_list[2], 1), TOKENS // TOK_DEV)
    routes_turns = jax.random.permutation(jax.random.fold_in(key_list[2], 3), TOKENS // TOK_DEV)
    routes = jax.vmap(lambda own, number: deal_out(jax.random.fold_in(key_list[2], 2), own, number, TOK_DEV, EXPERTS, 2, CAP, 2))(routes_keys, routes_turns).reshape((TOKENS, 2))
    example_ids = jax.vmap(lambda own: jnp.searchsorted(jnp.cumsum(uneven_parts(own, EX_ROW, ROW_TOK, 2 * ROW_TOK // EX_ROW, 2)), jnp.arange(ROW_TOK), side="right"))(jax.random.split(key_list[3], N_DP)).reshape((N_DP, ROW_TOK)).astype(jnp.int32)
    w_gate = noise(key_list[4], (EXPERTS, D, FF), D ** -0.5, 0.109375, ((0, 8), (2, 32)))
    w_up = noise(key_list[5], (EXPERTS, D, FF), D ** -0.5, 0.109375, ((0, 8), (2, 32)))
    w_down = noise(key_list[6], (EXPERTS, FF, D), FF ** -0.5, 0.0625, ((0, 8), (1, 32)))
    return {"tokens": tokens, "cotangent": cotangent, "routes": routes, "example_ids": example_ids, "w_gate": w_gate, "w_up": w_up, "w_down": w_down}


GAMMA = 0.01

def grams(blocked):
    wide = blocked.astype(jnp.float32)
    return jnp.einsum('bid,bjd->bij', wide, wide, precision=lax.Precision.HIGHEST)

def reference(tokens, cotangent, routes, example_ids, w_gate, w_up, w_down):
    block = N_EXPERT * CAP
    row_tok = N_EXPERT * TOK_DEV
    radius = math.sqrt(3.0 * D * FF * EXPERTS / EXAMPLES)
    row_x = tokens.reshape(N_DP, row_tok, D)
    row_dy = cotangent.reshape(N_DP, row_tok, D)
    row_routes = routes.reshape(N_DP, row_tok, 2)
    row_ids = example_ids + (jnp.arange(N_DP, dtype=jnp.int32) * EX_ROW)[:, None]
    offsets = (jnp.arange(N_DP, dtype=jnp.int32) * row_tok)[:, None]
    take_rows = jax.vmap(lambda source, index: source[index])
    mixed_acc = jnp.zeros((TOKENS, D), jnp.float32)
    partial_value = jnp.zeros((EXAMPLES,), jnp.float32)
    ex_range = jnp.arange(EXAMPLES, dtype=jnp.int32)
    kept = []
    for expert in range(EXPERTS):
        hit = jnp.any(row_routes == expert, axis=2)
        where_hit = jax.vmap(lambda m: jnp.nonzero(m, size=block, fill_value=0)[0].astype(jnp.int32))(hit)
        filled = jnp.arange(block)[None, :] < lax.optimization_barrier(jnp.sum(hit.astype(jnp.int32), axis=1))[:, None]
        rows_x = jnp.where(filled[..., None], take_rows(row_x, where_hit), jnp.zeros((), tokens.dtype))
        rows_dy = jnp.where(filled[..., None], take_rows(row_dy, where_hit), jnp.zeros((), cotangent.dtype))
        ids = jnp.where(filled, take_rows(row_ids, where_hit), -1).astype(jnp.int32)
        flat_x = rows_x.reshape(-1, D)
        flat_dy = rows_dy.reshape(-1, D)
        gate = jnp.dot(flat_x, w_gate[expert], preferred_element_type=jnp.float32)
        up = jnp.dot(flat_x, w_up[expert], preferred_element_type=jnp.float32)
        sig = jax.nn.sigmoid(gate)
        swish = gate * sig
        hidden = (swish * up).astype(jnp.bfloat16)
        route_out = jnp.dot(hidden, w_down[expert], preferred_element_type=jnp.float32).astype(jnp.bfloat16)
        target = (where_hit + offsets).reshape(-1)
        mixed_acc = mixed_acc.at[target].add(jnp.where(filled.reshape(-1)[:, None], route_out.astype(jnp.float32), 0.0))
        back_hidden = jnp.dot(flat_dy, w_down[expert].T, preferred_element_type=jnp.float32)
        d_gate = (back_hidden * up * sig * (1.0 + gate * (1.0 - sig))).astype(jnp.bfloat16)
        d_up = (back_hidden * swish).astype(jnp.bfloat16)
        pair_value = grams(rows_x) * (grams(d_gate.reshape(N_DP, block, FF)) + grams(d_up.reshape(N_DP, block, FF)))
        pair_value = pair_value + grams(hidden.reshape(N_DP, block, FF)) * grams(rows_dy)
        same = (ids[:, :, None] == ids[:, None, :]) & (ids[:, :, None] >= 0)
        row_sums = lax.optimization_barrier(jnp.sum(jnp.where(same, pair_value, 0.0), axis=2)).reshape(-1)
        flat_ids = ids.reshape(-1)
        ex_hot = (flat_ids[:, None] == ex_range[None, :]).astype(jnp.float32)
        partial_value = partial_value + lax.optimization_barrier(jnp.sum(ex_hot * row_sums[:, None], axis=0))
        kept.append((flat_x, flat_dy, hidden, d_gate, d_up, flat_ids))
    norms = jnp.sqrt(partial_value)
    factors = radius / (norms + GAMMA)
    grads_gate = []
    grads_up = []
    grads_down = []
    for flat_x, flat_dy, hidden, d_gate, d_up, flat_ids in kept:
        row_factor = jnp.where(flat_ids >= 0, factors[jnp.maximum(flat_ids, 0)], 0.0)[:, None]
        gate_scaled = (row_factor * d_gate).astype(jnp.bfloat16)
        up_scaled = (row_factor * d_up).astype(jnp.bfloat16)
        cot_scaled = (row_factor * flat_dy).astype(jnp.bfloat16)
        grads_gate.append(jnp.dot(flat_x.T, gate_scaled, preferred_element_type=jnp.float32).astype(jnp.bfloat16))
        grads_up.append(jnp.dot(flat_x.T, up_scaled, preferred_element_type=jnp.float32).astype(jnp.bfloat16))
        grads_down.append(jnp.dot(hidden.T, cot_scaled, preferred_element_type=jnp.float32).astype(jnp.bfloat16))
    return (mixed_acc.astype(jnp.bfloat16), norms.reshape(N_DP, EX_ROW), jnp.stack(grads_gate), jnp.stack(grads_up), jnp.stack(grads_down))
```

```python
import math

import jax
import jax.numpy as jnp
from jax import lax
from jax.experimental import pallas as pl
from jax.experimental.pallas import tpu as pltpu
from jax.sharding import Mesh, PartitionSpec as P

D = 3072
FF = 8192
CAP = 4
EX_ROW = 6
NX, NZ, NE = 4, 8, 8
BLOCKS = NX * NZ
SLOTS = NE * CAP
ROWS = BLOCKS * SLOTS
HID = FF // BLOCKS
SIZE = {"x": NX, "z": NZ}
GAMMA = 0.01
EXPERT = ("y", "c")
BF = jnp.bfloat16
F32 = jnp.float32
MIB = 1 << 20
PER = 8
TILE = PER * SLOTS
COLS = 512


def shift(a, axis, step):
    n = SIZE[axis]
    return lax.ppermute(a, axis, [(i, (i + step) % n) for i in range(n)])


def plus(a, b):
    return (a.astype(F32) + b.astype(F32)).astype(BF)


def ring_sum(get, axis, mid):
    half = SIZE[axis] // 2
    far = get(half)
    up, down = shift(far[..., :mid, :], axis, 1), shift(far[..., mid:, :], axis, -1)
    own_up, own_down = get(half - 1), get(1 - half)
    up = jnp.concatenate([plus(up, own_up[..., :mid, :]), own_up[..., mid:, :]], axis=-2)
    down = jnp.concatenate([own_down[..., :mid, :], plus(down, own_down[..., mid:, :])], axis=-2)
    for k in range(half - 1, 0, -1):
        up, down = shift(up, axis, 1), shift(down, axis, -1)
        if k > 1:
            up, down = plus(up, get(k - 1)), plus(down, get(1 - k))
    return (up.astype(F32) + down.astype(F32) + get(0).astype(F32)).astype(BF)


def direct_sum(get, axis):
    n = SIZE[axis]
    total = get(0).astype(F32)
    for k in range(1, n):
        total = total + shift(get(k), axis, k).astype(F32)
    return total.astype(BF)


def sum_z_x(part, ix, iz):
    part = part.reshape(NX, NZ, SLOTS, -1)
    w = part.shape[-1]
    line = ring_sum(lambda k: lax.dynamic_slice(part, (0, (iz + k) % NZ, 0, 0), (NX, 1, SLOTS, w)), "z", SLOTS // 2)
    return direct_sum(lambda k: lax.dynamic_slice(line, ((ix + k) % NX, 0, 0, 0), (1, 1, SLOTS, w)), "x")[0, 0]


def sum_x_z(part, ix, iz):
    part = part.reshape(NX, NZ, SLOTS, -1)
    w = part.shape[-1]
    line = ring_sum(lambda k: lax.dynamic_slice(part, ((ix + k) % NX, 0, 0, 0), (1, NZ, SLOTS, w)), "x", SLOTS // 2)
    return direct_sum(lambda k: lax.dynamic_slice(line, (0, (iz + k) % NZ, 0, 0), (1, 1, SLOTS, w)), "z")[0, 0]


def spread(a, axes, n):
    return lax.all_to_all(jnp.broadcast_to(a[None], (n,) + a.shape), axes, 0, 0, tiled=True)


def dot(a, b, dims):
    return lax.dot_general(a, b, (dims, ((), ())), preferred_element_type=F32)


def forward_kernel(x_ref, wg_ref, wu_ref, wd_ref, gate_ref, up_ref, hidden_ref, left_ref, right_ref):
    x = x_ref[...].reshape(TILE, D)
    gate = dot(x, wg_ref[0], ((1,), (0,)))
    up = dot(x, wu_ref[0], ((1,), (0,)))
    hidden = (gate * jax.nn.sigmoid(gate) * up).astype(BF)
    gate_ref[...] = gate
    up_ref[...] = up
    hidden_ref[...] = hidden
    w = left_ref.shape[1]
    left_ref[...] = dot(hidden, wd_ref[0, :, :w], ((1,), (0,))).astype(BF)
    right_ref[...] = dot(hidden, wd_ref[0, :, w:], ((1,), (0,))).astype(BF)


def forward(both, w_gate, w_up, w_down, w):
    def whole(a):
        return pl.BlockSpec(a.shape, lambda i: (0, 0, 0), pipeline_mode=pl.Buffered(1))

    def tall(n):
        return pl.BlockSpec((TILE, n), lambda i: (i, 0))

    return pl.pallas_call(
        forward_kernel,
        grid=(BLOCKS // PER,),
        in_specs=[pl.BlockSpec((PER, SLOTS, D), lambda i: (i, 0, 0)), whole(w_gate), whole(w_up), whole(w_down)],
        out_specs=[tall(HID), tall(HID), tall(HID), tall(w), tall(D - w)],
        out_shape=[
            jax.ShapeDtypeStruct((ROWS, HID), F32),
            jax.ShapeDtypeStruct((ROWS, HID), F32),
            jax.ShapeDtypeStruct((ROWS, HID), BF),
            jax.ShapeDtypeStruct((ROWS, w), BF),
            jax.ShapeDtypeStruct((ROWS, D - w), BF),
        ],
        compiler_params=pltpu.CompilerParams(vmem_limit_bytes=40 * MIB),
        cost_estimate=pl.CostEstimate(flops=6 * ROWS * D * HID, bytes_accessed=20 * MIB, transcendentals=ROWS * HID),
        name="forward",
    )(both, w_gate, w_up, w_down)


def backward_kernel(y_ref, wd_ref, gate_ref, up_ref, hidden_ref, xx_ref, yy_ref, id_col_ref, id_row_ref, dg_ref, du_ref, sum_ref):
    back = dot(y_ref[...].reshape(TILE, D), wd_ref[0], ((1,), (1,)))
    gate, up, hidden = gate_ref[...], up_ref[...], hidden_ref[...]
    sig = jax.nn.sigmoid(gate)
    d_gate = (back * up * sig * (1.0 + gate * (1.0 - sig))).astype(BF)
    d_up = (back * (gate * sig)).astype(BF)
    dg_ref[...] = d_gate
    du_ref[...] = d_up
    last = ((1,), (1,))
    xx = jnp.concatenate([xx_ref[...]] * PER, axis=1)
    yy = jnp.concatenate([yy_ref[...]] * PER, axis=1)
    pair = xx * (dot(d_gate, d_gate, last) + dot(d_up, d_up, last)) + yy * dot(hidden, hidden, last)
    block_row = lax.broadcasted_iota(jnp.int32, (TILE, TILE), 0) // SLOTS
    block_col = lax.broadcasted_iota(jnp.int32, (TILE, TILE), 1) // SLOTS
    ids_col, ids_row = id_col_ref[...], id_row_ref[0]
    same = (block_row == block_col) & (ids_col == ids_row) & (ids_col >= 0.0)
    sum_ref[...] = jnp.sum(jnp.where(same, pair, 0.0), axis=1, keepdims=True)


def backward(both, w_down, gate, up, hidden, xx, yy, ids):
    def tall(n):
        return pl.BlockSpec((TILE, n), lambda i: (i, 0))

    steps = BLOCKS // PER
    return pl.pallas_call(
        backward_kernel,
        grid=(steps,),
        in_specs=[
            pl.BlockSpec((PER, SLOTS, D), lambda i: (i, 1, 0)),
            pl.BlockSpec(w_down.shape, lambda i: (0, 0, 0), pipeline_mode=pl.Buffered(1)),
            tall(HID),
            tall(HID),
            tall(HID),
            tall(SLOTS),
            tall(SLOTS),
            tall(1),
            pl.BlockSpec((1, 1, TILE), lambda i: (i, 0, 0)),
        ],
        out_specs=[tall(HID), tall(HID), tall(1)],
        out_shape=[
            jax.ShapeDtypeStruct((ROWS, HID), BF),
            jax.ShapeDtypeStruct((ROWS, HID), BF),
            jax.ShapeDtypeStruct((ROWS, 1), F32),
        ],
        compiler_params=pltpu.CompilerParams(vmem_limit_bytes=40 * MIB),
        cost_estimate=pl.CostEstimate(flops=3 * ROWS * D * HID, bytes_accessed=14 * MIB, transcendentals=ROWS * HID),
        name="backward",
    )(both, w_down, gate, up, hidden, xx, yy, ids.reshape(ROWS, 1), ids.reshape(steps, 1, TILE))


def grads_kernel(x_ref, y_ref, hidden_ref, dg_ref, du_ref, factor_ref, gg_ref, gu_ref, gd_ref, scaled, turned):
    @pl.when(pl.program_id(0) == 0)
    def _():
        factor = factor_ref[...]
        scaled[:, :HID] = (factor * dg_ref[...].astype(F32)).astype(BF)
        scaled[:, HID:] = (factor * du_ref[...].astype(F32)).astype(BF)
        turned[...] = hidden_ref[...].T

    x = x_ref[...].reshape(ROWS, COLS)
    both = dot(x, scaled[...], ((0,), (0,))).astype(BF)
    gg_ref[0] = both[:, :HID]
    gu_ref[0] = both[:, HID:]
    cot = (factor_ref[...] * y_ref[...].reshape(ROWS, COLS).astype(F32)).astype(BF)
    gd_ref[0] = dot(turned[...], cot, ((1,), (0,))).astype(BF)


def gradients(both, hidden, d_gate, d_up, factor):
    def whole(a):
        return pl.BlockSpec(a.shape, lambda i: (0, 0), pipeline_mode=pl.Buffered(1))

    return pl.pallas_call(
        grads_kernel,
        grid=(D // COLS,),
        in_specs=[
            pl.BlockSpec((BLOCKS, SLOTS, COLS), lambda i: (0, 0, i)),
            pl.BlockSpec((BLOCKS, SLOTS, COLS), lambda i: (0, 1, i)),
            whole(hidden),
            whole(d_gate),
            whole(d_up),
            whole(factor),
        ],
        out_specs=[
            pl.BlockSpec((1, COLS, HID), lambda i: (0, i, 0)),
            pl.BlockSpec((1, COLS, HID), lambda i: (0, i, 0)),
            pl.BlockSpec((1, HID, COLS), lambda i: (0, 0, i)),
        ],
        out_shape=[
            jax.ShapeDtypeStruct((1, D, HID), BF),
            jax.ShapeDtypeStruct((1, D, HID), BF),
            jax.ShapeDtypeStruct((1, HID, D), BF),
        ],
        scratch_shapes=[pltpu.VMEM((ROWS, 2 * HID), BF), pltpu.VMEM((HID, ROWS), BF)],
        compiler_params=pltpu.CompilerParams(vmem_limit_bytes=40 * MIB),
        cost_estimate=pl.CostEstimate(flops=6 * ROWS * D * HID, bytes_accessed=18 * MIB, transcendentals=0),
        name="gradients",
    )(both, both, hidden, d_gate, d_up, factor)


def on_device(tokens, cotangent, routes, example_ids, w_gate, w_up, w_down):
    ix, iz = lax.axis_index("x"), lax.axis_index("z")
    my_row = ix * NZ + iz
    tok_count, width = tokens.shape
    radius = math.sqrt(3.0 * D * FF * NE / (BLOCKS * EX_ROW))
    flat_routes = routes.reshape(-1)
    owner_hot = (flat_routes[:, None] == jnp.arange(NE)[None, :]).astype(jnp.int32)
    before = jnp.cumsum(owner_hot, axis=0) - owner_hot
    slot_of = flat_routes * CAP + jnp.sum(before * owner_hot, axis=1)
    placed = (jnp.arange(SLOTS)[:, None] == slot_of[None, :]).astype(jnp.int32)
    placed = jnp.sum(placed.reshape(SLOTS, tok_count, 2), axis=2)
    placed_bf = placed.astype(BF)
    filled = jnp.sum(placed, axis=1) > 0
    send_ids = jnp.where(filled, jnp.sum(placed * example_ids.reshape(-1)[None, :], axis=1), -1)
    send_x = jnp.dot(placed_bf, tokens, preferred_element_type=F32).astype(BF)
    send_dy = jnp.dot(placed_bf, cotangent, preferred_element_type=F32).astype(BF)
    id_cols = jnp.broadcast_to(send_ids.astype(BF)[:, None], (SLOTS, 128))
    send = jnp.concatenate(
        [
            jnp.concatenate([send_x, id_cols], axis=1).reshape(NE, CAP, width + 128),
            jnp.concatenate([send_dy, id_cols], axis=1).reshape(NE, CAP, width + 128),
        ],
        axis=1,
    )
    got = lax.all_to_all(send, EXPERT, split_axis=0, concat_axis=0, tiled=True)
    local_x = got[:, :CAP, :width].reshape(SLOTS, width)
    local_dy = got[:, CAP:, :width].reshape(SLOTS, width)
    local_ids = got[:, :CAP, width].reshape(SLOTS, 1).astype(F32)
    both = lax.all_gather(jnp.concatenate([local_x, local_dy], axis=0), ("x", "z"), axis=0)
    last = ((1,), (1,))
    notes = jnp.concatenate(
        [dot(local_x, local_x, last), dot(local_dy, local_dy, last), jnp.broadcast_to(local_ids, (SLOTS, 64))], axis=1
    )
    notes = spread(notes, ("x", "z"), BLOCKS).reshape(BLOCKS, SLOTS, 128)
    xx = notes[:, :, :SLOTS].reshape(ROWS, SLOTS)
    yy = notes[:, :, SLOTS : 2 * SLOTS].reshape(ROWS, SLOTS)
    ids = notes[:, :, 2 * SLOTS]
    gate, up, hidden, left, right = forward(both, w_gate, w_up, w_down, D // 2)
    own_out = jnp.concatenate([sum_z_x(left, ix, iz), sum_x_z(right, ix, iz)], axis=1)
    returned = lax.all_to_all(own_out.reshape(NE, CAP, width), EXPERT, split_axis=0, concat_axis=0, tiled=True)
    mixed = jnp.dot(placed_bf.T, returned.reshape(SLOTS, width), preferred_element_type=F32).astype(BF)
    d_gate, d_up, row_sums = backward(both, w_down, gate, up, hidden, xx, yy, ids)
    ex_hot = (ids[:, :, None] == jnp.arange(EX_ROW, dtype=F32)[None, None, :]).astype(F32)
    partial_value = jnp.sum(ex_hot * row_sums.reshape(BLOCKS, SLOTS, 1), axis=1)
    squares = jnp.sum(spread(partial_value, ("x", "z"), BLOCKS).reshape(BLOCKS, BLOCKS, EX_ROW), axis=0)
    squares = jnp.sum(spread(squares, EXPERT, NE).reshape(NE, BLOCKS, EX_ROW), axis=0)
    norms_all = jnp.sqrt(squares)
    factors = radius / (norms_all + GAMMA)
    own_norms = lax.dynamic_slice_in_dim(norms_all, my_row, 1, 0)
    row_factor = jnp.sum(ex_hot * factors[:, None, :], axis=2).reshape(ROWS, 1)
    grad_gate, grad_up, grad_down = gradients(both, hidden, d_gate, d_up, row_factor)
    return (mixed, own_norms, grad_gate, grad_up, grad_down)


def solution(mesh):
    mesh = Mesh(mesh.devices.reshape(NX, NZ, 4, 2), ("x", "z", "y", "c"))
    data, every = ("x", "z"), ("x", "z", "y", "c")
    return jax.shard_map(
        on_device,
        mesh=mesh,
        in_specs=(
            P(every, None),
            P(every, None),
            P(every, None),
            P(data, EXPERT),
            P(EXPERT, None, data),
            P(EXPERT, None, data),
            P(EXPERT, data, None),
        ),
        out_specs=(
            P(every, None),
            P(data, None),
            P(EXPERT, None, data),
            P(EXPERT, None, data),
            P(EXPERT, data, None),
        ),
        check_vma=False,
    )
```

```python
import math

import jax
import jax.numpy as jnp
from jax import lax
from jax.experimental import pallas as pl
from jax.experimental.pallas import tpu as pltpu
from jax.sharding import Mesh, PartitionSpec as P

D = 3072
FF = 8192
CAP = 4
EX_ROW = 6
NX, NZ, NE = 4, 8, 8
BLOCKS = NX * NZ
SLOTS = NE * CAP
ROWS = BLOCKS * SLOTS
HID = FF // BLOCKS
SIZE = {"x": NX, "z": NZ}
ORDER = {"x": (0, -1, 1, 2), "z": (0, -1, 1, -2, 2, -3, 3, 4)}
GAMMA = 0.01
RADIUS = math.sqrt(3.0 * D * FF * NE / (BLOCKS * EX_ROW))
EXPERT = ("y", "c")
BF = jnp.bfloat16
F32 = jnp.float32
MIB = 1 << 20
LANES = 128
TILE = NZ * SLOTS
MID = SLOTS // 2
COLS = 512
LEFT = D // 2


def shift(a, axis, step):
    n = SIZE[axis]
    return lax.ppermute(a, axis, [(i, (i + step) % n) for i in range(n)])


def ring_gather(a, axis):
    half = SIZE[axis] // 2
    mid = a.shape[-2] // 2
    pieces = [a]
    up = down = a
    for _ in range(1, half):
        up, down = shift(up, axis, 1), shift(down, axis, -1)
        pieces += [up, down]
    return pieces + [shift(up[..., :mid, :], axis, 1), shift(down[..., mid:, :], axis, -1)]


def line_of(pieces):
    return jnp.stack(pieces[:-2] + [jnp.concatenate(pieces[-2:], axis=-2)], axis=0)


def plus(a, b):
    return (a.astype(F32) + b.astype(F32)).astype(BF)


def ring_sum(parts, axis):
    half = SIZE[axis] // 2
    place = ORDER[axis].index

    def get(k):
        return parts[place(k)]

    far = get(half)
    mid = far.shape[0] // 2
    first = up = shift(far[:mid], axis, 1)
    down = shift(far[mid:], axis, -1)
    own_up, own_down = get(half - 1), get(1 - half)
    up = jnp.concatenate([plus(up, own_up[:mid]), own_up[mid:]], axis=0)
    down = jnp.concatenate([own_down[:mid], plus(down, own_down[mid:])], axis=0)
    for k in range(half - 1, 0, -1):
        up, down = shift(up, axis, 1), shift(down, axis, -1)
        if k > 1:
            up, down = plus(up, get(k - 1)), plus(down, get(1 - k))
    return (up.astype(F32) + down.astype(F32) + get(0).astype(F32)).astype(BF), first


def direct_sum(parts, axis):
    total = parts[0].astype(F32)
    for place, k in enumerate(ORDER[axis]):
        if k:
            total = total + shift(parts[place], axis, k).astype(F32)
    return total.astype(BF)


def spread(a, axes, n):
    return lax.all_to_all(jnp.broadcast_to(a[None], (n,) + a.shape), axes, 0, 0, tiled=True)


def dot(a, b, dims):
    return lax.dot_general(a, b, (dims, ((), ())), preferred_element_type=F32)


def forward_kernel(where_ref, *refs):
    a_refs, refs = refs[: NZ + 1], refs[NZ + 1 :]
    b_refs, refs = refs[: NX + 1], refs[NX + 1 :]
    wg_ref, wu_ref, wd_ref, x_ref, gate_ref, up_ref, hidden_ref, left_ref, right_ref, sems = refs
    quarter = MID // 2
    copies = []
    for i in range(NX):
        moves = [(a_refs[j].at[i], x_ref.at[i, j, pl.ds(0, MID)]) for j in range(NZ - 1)]
        moves += [(a_refs[NZ - 1 + h].at[i], x_ref.at[i, NZ - 1, pl.ds(h * quarter, quarter)]) for h in range(2)]
        if i < NX - 1:
            moves += [(b_refs[i], x_ref.at[i, :, pl.ds(MID, MID)])]
        else:
            moves += [(b_refs[i + h], x_ref.at[i, :, pl.ds(MID + h * quarter, quarter)]) for h in range(2)]
        copies.append([pltpu.make_async_copy(s, d, sems.at[i, n]) for n, (s, d) in enumerate(moves)])
    for group in copies:
        for copy in group:
            copy.start()
    for i in range(NX):
        for copy in copies[i]:
            copy.wait()
        x = x_ref[i].reshape(TILE, D)
        gate = dot(x, wg_ref[0], ((1,), (0,)))
        up = dot(x, wu_ref[0], ((1,), (0,)))
        hidden = (gate * jax.nn.sigmoid(gate) * up).astype(BF)
        rows = pl.ds(i * TILE, TILE)
        gate_ref[rows, :] = gate
        up_ref[rows, :] = up
        hidden_ref[rows, :] = hidden
        out = dot(hidden, wd_ref[0, :, :LEFT], ((1,), (0,))).astype(BF)
        for j in range(NZ):
            left_ref[j, i] = out[j * SLOTS : (j + 1) * SLOTS]
        out = dot(hidden, wd_ref[0, :, LEFT:], ((1,), (0,))).astype(BF)
        right_ref[where_ref[i]] = out


def forward(where, a_pieces, b_pieces, w_gate, w_up, w_down):
    anywhere = pl.BlockSpec(memory_space=pl.ANY)
    inside = pl.BlockSpec(memory_space=pltpu.VMEM)
    return pl.pallas_call(
        forward_kernel,
        in_specs=[pl.BlockSpec(memory_space=pltpu.SMEM)] + [anywhere] * (NZ + NX + 2) + [inside] * 3,
        out_specs=[inside] * 6,
        out_shape=[
            jax.ShapeDtypeStruct((NX, NZ, SLOTS, D), BF),
            jax.ShapeDtypeStruct((ROWS, HID), F32),
            jax.ShapeDtypeStruct((ROWS, HID), F32),
            jax.ShapeDtypeStruct((ROWS, HID), BF),
            jax.ShapeDtypeStruct((NZ, NX, SLOTS, LEFT), BF),
            jax.ShapeDtypeStruct((NX, TILE, D - LEFT), BF),
        ],
        scratch_shapes=[pltpu.SemaphoreType.DMA((NX, NZ + 3))],
        compiler_params=pltpu.CompilerParams(vmem_limit_bytes=44 * MIB),
        cost_estimate=pl.CostEstimate(flops=6 * ROWS * D * HID, bytes_accessed=20 * MIB, transcendentals=ROWS * HID),
        name="forward",
    )(where, *a_pieces, *b_pieces, w_gate, w_up, w_down)


def backward_kernel(where_ref, y_ref, id_ref, x_ref, wd_ref, gate_ref, up_ref, hidden_ref, y_out, dg_ref, du_ref, spot_ref, sum_ref):
    i = pl.program_id(0)
    at_x = where_ref[i]
    spots = []
    ids = []
    for j in range(NZ):
        at_z = where_ref[NX + j]
        y_out[0, j] = y_ref[at_z]
        block_id = id_ref[at_z].astype(F32)
        ids.append(block_id)
        start = ((at_x * NZ + at_z) * 8).astype(F32)
        spots.append(jnp.where(block_id >= 0.0, block_id + start, -1.0))
    ids = jnp.concatenate(ids, axis=0)
    spot = jnp.concatenate(spots, axis=0)
    spot_ref[...] = spot[:, :1]
    y = y_out[0].reshape(TILE, D)
    x = x_ref[0].reshape(TILE, D)
    back = dot(y, wd_ref[0], ((1,), (1,)))
    gate, up, hidden = gate_ref[...], up_ref[...], hidden_ref[...]
    sig = jax.nn.sigmoid(gate)
    d_gate = (back * up * sig * (1.0 + gate * (1.0 - sig))).astype(BF)
    d_up = (back * (gate * sig)).astype(BF)
    dg_ref[...] = d_gate
    du_ref[...] = d_up
    last = ((1,), (1,))
    pair = dot(x, x, last) * (dot(d_gate, d_gate, last) + dot(d_up, d_up, last))
    pair = pair + dot(y, y, last) * dot(hidden, hidden, last)
    same = (spot[:, :1] == spot.T[:1, :]) & (spot[:, :1] >= 0.0)
    row_sums = jnp.sum(jnp.where(same, pair, 0.0), axis=1, keepdims=True)
    lane = lax.broadcasted_iota(jnp.int32, (TILE, LANES), 1).astype(F32)

    @pl.when(i == 0)
    def _():
        sum_ref[...] = jnp.zeros_like(sum_ref)

    for half in range(2):
        hot = spot == lane + half * LANES
        sum_ref[half : half + 1, :] += jnp.sum(jnp.where(hot, row_sums, 0.0), axis=0, keepdims=True)


def backward(where, wide_y, x, w_down, gate, up, hidden):
    def tall(n):
        return pl.BlockSpec((TILE, n), lambda i, where: (i, 0))

    rows = pl.BlockSpec((1, NZ, SLOTS, D), lambda i, where: (i, 0, 0, 0))
    return pl.pallas_call(
        backward_kernel,
        grid_spec=pltpu.PrefetchScalarGridSpec(
            num_scalar_prefetch=1,
            grid=(NX,),
            in_specs=[
                pl.BlockSpec((NZ, SLOTS, D), lambda i, where: (where[i], 0, 0)),
                pl.BlockSpec((NZ, SLOTS, LANES), lambda i, where: (where[i], 0, D // LANES)),
                rows,
                pl.BlockSpec(w_down.shape, lambda i, where: (0, 0, 0), pipeline_mode=pl.Buffered(1)),
                tall(HID),
                tall(HID),
                tall(HID),
            ],
            out_specs=[rows, tall(HID), tall(HID), tall(1), pl.BlockSpec((2, LANES), lambda i, where: (0, 0))],
        ),
        out_shape=[
            jax.ShapeDtypeStruct((NX, NZ, SLOTS, D), BF),
            jax.ShapeDtypeStruct((ROWS, HID), BF),
            jax.ShapeDtypeStruct((ROWS, HID), BF),
            jax.ShapeDtypeStruct((ROWS, 1), F32),
            jax.ShapeDtypeStruct((2, LANES), F32),
        ],
        compiler_params=pltpu.CompilerParams(vmem_limit_bytes=40 * MIB),
        cost_estimate=pl.CostEstimate(flops=5 * ROWS * D * HID, bytes_accessed=20 * MIB, transcendentals=ROWS * HID),
        name="backward",
    )(where, wide_y, wide_y, x, w_down, gate, up, hidden)


def grads_kernel(x_ref, y_ref, hidden_ref, dg_ref, du_ref, spot_ref, factor_ref, gg_ref, gu_ref, gd_ref, scaled, turned, by_row):
    @pl.when(pl.program_id(0) == 0)
    def _():
        spot = spot_ref[...]
        lane = lax.broadcasted_iota(jnp.int32, (ROWS, LANES), 1).astype(F32)
        factor = jnp.zeros((ROWS, 1), F32)
        for half in range(2):
            chosen = jnp.where(spot == lane + half * LANES, factor_ref[half : half + 1, :], 0.0)
            factor = factor + jnp.sum(chosen, axis=1, keepdims=True)
        by_row[...] = factor
        scaled[:, :HID] = (factor * dg_ref[...].astype(F32)).astype(BF)
        scaled[:, HID:] = (factor * du_ref[...].astype(F32)).astype(BF)
        turned[...] = hidden_ref[...].T

    x = x_ref[...].reshape(ROWS, COLS)
    both = dot(x, scaled[...], ((0,), (0,))).astype(BF)
    gg_ref[0] = both[:, :HID]
    gu_ref[0] = both[:, HID:]
    cot = (by_row[...] * y_ref[...].reshape(ROWS, COLS).astype(F32)).astype(BF)
    gd_ref[0] = dot(turned[...], cot, ((1,), (0,))).astype(BF)


def gradients(x, y, hidden, d_gate, d_up, spot, factors):
    def whole(a):
        return pl.BlockSpec(a.shape, lambda i: (0, 0), pipeline_mode=pl.Buffered(1))

    part = pl.BlockSpec((NX, NZ, SLOTS, COLS), lambda i: (0, 0, 0, i))
    return pl.pallas_call(
        grads_kernel,
        grid=(D // COLS,),
        in_specs=[part, part, whole(hidden), whole(d_gate), whole(d_up), whole(spot), whole(factors)],
        out_specs=[
            pl.BlockSpec((1, COLS, HID), lambda i: (0, i, 0)),
            pl.BlockSpec((1, COLS, HID), lambda i: (0, i, 0)),
            pl.BlockSpec((1, HID, COLS), lambda i: (0, 0, i)),
        ],
        out_shape=[
            jax.ShapeDtypeStruct((1, D, HID), BF),
            jax.ShapeDtypeStruct((1, D, HID), BF),
            jax.ShapeDtypeStruct((1, HID, D), BF),
        ],
        scratch_shapes=[pltpu.VMEM((ROWS, 2 * HID), BF), pltpu.VMEM((HID, ROWS), BF), pltpu.VMEM((ROWS, 1), F32)],
        compiler_params=pltpu.CompilerParams(vmem_limit_bytes=40 * MIB),
        cost_estimate=pl.CostEstimate(flops=6 * ROWS * D * HID, bytes_accessed=18 * MIB, transcendentals=0),
        name="gradients",
    )(x, y, hidden, d_gate, d_up, spot, factors)


def on_device(tokens, cotangent, routes, example_ids, w_gate, w_up, w_down):
    ix, iz = lax.axis_index("x"), lax.axis_index("z")
    where = jnp.concatenate([(ix + jnp.array(ORDER["x"])) % NX, (iz + jnp.array(ORDER["z"])) % NZ]).astype(jnp.int32)
    tok_count, width = tokens.shape
    flat_routes = routes.reshape(-1)
    owner_hot = (flat_routes[:, None] == jnp.arange(NE)[None, :]).astype(jnp.int32)
    before = jnp.cumsum(owner_hot, axis=0) - owner_hot
    slot_of = flat_routes * CAP + jnp.sum(before * owner_hot, axis=1)
    placed = (jnp.arange(SLOTS)[:, None] == slot_of[None, :]).astype(jnp.int32)
    placed = jnp.sum(placed.reshape(SLOTS, tok_count, 2), axis=2)
    placed_bf = placed.astype(BF)
    filled = jnp.sum(placed, axis=1) > 0
    send_ids = jnp.where(filled, jnp.sum(placed * example_ids.reshape(-1)[None, :], axis=1), -1)
    send_x = jnp.dot(placed_bf, tokens, preferred_element_type=F32).astype(BF)
    send_dy = jnp.dot(placed_bf, cotangent, preferred_element_type=F32).astype(BF)
    id_cols = jnp.broadcast_to(send_ids.astype(BF)[:, None], (SLOTS, LANES))
    send = jnp.concatenate(
        [
            jnp.concatenate([send_x, id_cols], axis=1).reshape(NE, CAP, width + LANES),
            jnp.concatenate([send_dy, id_cols], axis=1).reshape(NE, CAP, width + LANES),
        ],
        axis=1,
    )
    got = lax.all_to_all(send, EXPERT, split_axis=0, concat_axis=0, tiled=True)
    local_x = got[:, :CAP, :width].reshape(SLOTS, width)
    local_dy = got[:, CAP:].reshape(SLOTS, width + LANES)
    wide_y = lax.all_gather(local_dy, ("x", "z"), axis=0)
    line_x = line_of(ring_gather(local_x[:MID], "x"))
    line_z = line_of(ring_gather(local_x[MID:], "z"))
    a_pieces = ring_gather(line_x, "z")
    b_pieces = ring_gather(line_z, "x")
    x, gate, up, hidden, left, right = forward(where, a_pieces, b_pieces, w_gate, w_up, w_down)
    right, wide_y = lax.optimization_barrier((right, wide_y))
    left_line, first = ring_sum(left, "z")
    right_line = lax.psum_scatter(right.reshape(ROWS, D - LEFT), "x", scatter_dimension=0, tiled=True)
    left_out = direct_sum(left_line, "x")
    right_out = direct_sum(right_line.reshape(NZ, SLOTS, D - LEFT), "z")
    own_out = jnp.concatenate([left_out, right_out], axis=1)
    returned = lax.all_to_all(own_out.reshape(NE, CAP, width), EXPERT, split_axis=0, concat_axis=0, tiled=True)
    mixed = jnp.dot(placed_bf.T, returned.reshape(SLOTS, width), preferred_element_type=F32).astype(BF)
    gate, _ = lax.optimization_barrier((gate, first))
    y, d_gate, d_up, spot, partial_value = backward(where, wide_y, x, w_down, gate, up, hidden)
    squares = jnp.sum(spread(partial_value, ("x", "z"), BLOCKS).reshape(BLOCKS, 2, LANES), axis=0)
    squares = jnp.sum(spread(squares, EXPERT, NE).reshape(NE, 2, LANES), axis=0)
    norms = jnp.sqrt(squares)
    factors = RADIUS / (norms + GAMMA)
    own_norms = lax.dynamic_slice(norms.reshape(BLOCKS, 8), (ix * NZ + iz, 0), (1, EX_ROW))
    grad_gate, grad_up, grad_down = gradients(x, y, hidden, d_gate, d_up, spot, factors)
    return (mixed, own_norms, grad_gate, grad_up, grad_down)


def solution(mesh):
    mesh = Mesh(mesh.devices.reshape(NX, NZ, 4, 2), ("x", "z", "y", "c"))
    data, every = ("x", "z"), ("x", "z", "y", "c")
    return jax.shard_map(
        on_device,
        mesh=mesh,
        in_specs=(
            P(every, None),
            P(every, None),
            P(every, None),
            P(data, EXPERT),
            P(EXPERT, None, data),
            P(EXPERT, None, data),
            P(EXPERT, data, None),
        ),
        out_specs=(
            P(every, None),
            P(data, None),
            P(EXPERT, None, data),
            P(EXPERT, None, data),
            P(EXPERT, data, None),
        ),
        check_vma=False,
    )
```

```python
import math

import jax
import jax.numpy as jnp
from jax import lax
from jax.experimental import pallas as pl
from jax.experimental.pallas import tpu as pltpu
from jax.sharding import Mesh, PartitionSpec as P

D = 3072
FF = 8192
CAP = 4
EX_ROW = 6
NX, NZ, NE = 4, 8, 8
BLOCKS = NX * NZ
SLOTS = NE * CAP
ROWS = BLOCKS * SLOTS
HID = FF // BLOCKS
SIZE = {"x": NX, "z": NZ}
ORDER = {"x": (0, -1, 1, 2), "z": (0, -1, 1, -2, 2, -3, 3, 4)}
GAMMA = 0.01
RADIUS = math.sqrt(3.0 * D * FF * NE / (BLOCKS * EX_ROW))
EXPERT = ("y", "c")
BF = jnp.bfloat16
F32 = jnp.float32
MIB = 1 << 20
LANES = 128
TILE = NZ * SLOTS
MID = SLOTS // 2
COLS = 512
LEFT = D // 2


def shift(a, axis, step):
    n = SIZE[axis]
    return lax.ppermute(a, axis, [(i, (i + step) % n) for i in range(n)])


def ring_gather(a, axis):
    half = SIZE[axis] // 2
    mid = a.shape[-2] // 2
    pieces = [a]
    up = down = a
    for _ in range(1, half):
        up, down = shift(up, axis, 1), shift(down, axis, -1)
        pieces += [up, down]
    return pieces + [shift(up[..., :mid, :], axis, 1), shift(down[..., mid:, :], axis, -1)]


def line_of(pieces):
    return jnp.stack(pieces[:-2] + [jnp.concatenate(pieces[-2:], axis=-2)], axis=0)


def plus(a, b):
    return (a.astype(F32) + b.astype(F32)).astype(BF)


def ring_sum(parts, axis, hook):
    half = SIZE[axis] // 2
    place = ORDER[axis].index

    def get(k):
        return parts[place(k)]

    far = get(half)
    mid = far.shape[0] // 2
    up, down = shift(far[:mid], axis, 1), shift(far[mid:], axis, -1)
    own_up, own_down = get(half - 1), get(1 - half)
    up = jnp.concatenate([plus(up, own_up[:mid]), own_up[mid:]], axis=0)
    down = jnp.concatenate([own_down[:mid], plus(down, own_down[mid:])], axis=0)
    for k in range(half - 1, 0, -1):
        up, down = hook(half - k, (up, down))
        up, down = shift(up, axis, 1), shift(down, axis, -1)
        if k > 1:
            up, down = plus(up, get(k - 1)), plus(down, get(1 - k))
    up, down = hook(half, (up, down))
    return (up.astype(F32) + down.astype(F32) + get(0).astype(F32)).astype(BF)


def direct_sum(parts, axis):
    total = parts[0].astype(F32)
    for place, k in enumerate(ORDER[axis]):
        if k:
            total = total + shift(parts[place], axis, k).astype(F32)
    return total.astype(BF)


def spread(a, axes, n):
    return lax.all_to_all(jnp.broadcast_to(a[None], (n,) + a.shape), axes, 0, 0, tiled=True)


def dot(a, b, dims):
    return lax.dot_general(a, b, (dims, ((), ())), preferred_element_type=F32)


def forward_kernel(where_ref, *refs):
    a_refs, refs = refs[: NZ + 1], refs[NZ + 1 :]
    b_refs, refs = refs[: NX + 1], refs[NX + 1 :]
    wg_ref, wu_ref, wd_ref, x_out, gate_ref, up_ref, hidden_ref, left_ref, right_ref, rows_ref, in_sems, out_sems = refs
    step = pl.program_id(0)
    quarter = MID // 2
    arrivals = []
    for i in range(NX):
        moves = [(a_refs[j].at[i], rows_ref.at[i, j, pl.ds(0, MID)]) for j in range(NZ - 1)]
        moves += [(a_refs[NZ - 1 + h].at[i], rows_ref.at[i, NZ - 1, pl.ds(h * quarter, quarter)]) for h in range(2)]
        if i < NX - 1:
            moves += [(b_refs[i], rows_ref.at[i, :, pl.ds(MID, MID)])]
        else:
            moves += [(b_refs[i + h], rows_ref.at[i, :, pl.ds(MID + h * quarter, quarter)]) for h in range(2)]
        arrivals.append([pltpu.make_async_copy(s, d, in_sems.at[i, n]) for n, (s, d) in enumerate(moves)])
    leaving = [pltpu.make_async_copy(rows_ref.at[i], x_out.at[i], out_sems.at[i]) for i in range(NX)]

    @pl.when(step == 0)
    def _():
        for group in arrivals:
            for copy in group:
                copy.start()

    for i in range(NX):

        @pl.when(step == i)
        def _():
            for copy in arrivals[i]:
                copy.wait()
            leaving[i].start()

    x = rows_ref[step].reshape(TILE, D)
    gate = dot(x, wg_ref[0], ((1,), (0,)))
    up = dot(x, wu_ref[0], ((1,), (0,)))
    hidden = (gate * jax.nn.sigmoid(gate) * up).astype(BF)
    gate_ref[...] = gate
    up_ref[...] = up
    hidden_ref[...] = hidden
    out = dot(hidden, wd_ref[0, :, :LEFT], ((1,), (0,))).astype(BF)
    left_ref[...] = out.reshape(NZ, 1, SLOTS, LEFT)
    out = dot(hidden, wd_ref[0, :, LEFT:], ((1,), (0,))).astype(BF)
    for j in range(NZ):
        right_ref[0, where_ref[NX + j]] = out[j * SLOTS : (j + 1) * SLOTS]

    @pl.when(step == NX - 1)
    def _():
        for copy in leaving:
            copy.wait()


def forward(where, a_pieces, b_pieces, w_gate, w_up, w_down):
    outside = pl.BlockSpec(memory_space=pltpu.HBM)

    def whole(a):
        return pl.BlockSpec(a.shape, lambda i, where: (0, 0, 0), pipeline_mode=pl.Buffered(1))

    def tall(n):
        return pl.BlockSpec((TILE, n), lambda i, where: (i, 0))

    return pl.pallas_call(
        forward_kernel,
        grid_spec=pltpu.PrefetchScalarGridSpec(
            num_scalar_prefetch=1,
            grid=(NX,),
            in_specs=[outside] * (NZ + NX + 2) + [whole(w_gate), whole(w_up), whole(w_down)],
            out_specs=[
                outside,
                tall(HID),
                tall(HID),
                tall(HID),
                pl.BlockSpec((NZ, 1, SLOTS, LEFT), lambda i, where: (0, i, 0, 0)),
                pl.BlockSpec((1, NZ, SLOTS, D - LEFT), lambda i, where: (where[i], 0, 0, 0)),
            ],
            scratch_shapes=[
                pltpu.VMEM((NX, NZ, SLOTS, D), BF),
                pltpu.SemaphoreType.DMA((NX, NZ + 3)),
                pltpu.SemaphoreType.DMA((NX,)),
            ],
        ),
        out_shape=[
            jax.ShapeDtypeStruct((NX, NZ, SLOTS, D), BF),
            jax.ShapeDtypeStruct((ROWS, HID), F32),
            jax.ShapeDtypeStruct((ROWS, HID), F32),
            jax.ShapeDtypeStruct((ROWS, HID), BF),
            jax.ShapeDtypeStruct((NZ, NX, SLOTS, LEFT), BF),
            jax.ShapeDtypeStruct((NX, NZ, SLOTS, D - LEFT), BF),
        ],
        compiler_params=pltpu.CompilerParams(vmem_limit_bytes=40 * MIB),
        cost_estimate=pl.CostEstimate(flops=6 * ROWS * D * HID, bytes_accessed=20 * MIB, transcendentals=ROWS * HID),
        name="forward",
    )(where, *a_pieces, *b_pieces, w_gate, w_up, w_down)


def backward_kernel(where_ref, y_ref, id_ref, x_ref, wd_ref, gate_ref, up_ref, hidden_ref, dg_ref, du_ref, spot_ref, sum_ref, y_rows):
    i = pl.program_id(0)
    at_x = where_ref[i]
    spots = []
    for j in range(NZ):
        at_z = where_ref[NX + j]
        y_rows[j] = y_ref[at_z]
        block_id = id_ref[at_z].astype(F32)
        start = ((at_x * NZ + at_z) * 8).astype(F32)
        spots.append(jnp.where(block_id >= 0.0, block_id + start, -1.0))
    spot = jnp.concatenate(spots, axis=0)
    spot_ref[...] = spot[:, :1]
    y = y_rows[...].reshape(TILE, D)
    x = x_ref[0].reshape(TILE, D)
    back = dot(y, wd_ref[0], ((1,), (1,)))
    gate, up, hidden = gate_ref[...], up_ref[...], hidden_ref[...]
    sig = jax.nn.sigmoid(gate)
    d_gate = (back * up * sig * (1.0 + gate * (1.0 - sig))).astype(BF)
    d_up = (back * (gate * sig)).astype(BF)
    dg_ref[...] = d_gate
    du_ref[...] = d_up
    last = ((1,), (1,))
    pair = dot(x, x, last) * (dot(d_gate, d_gate, last) + dot(d_up, d_up, last))
    pair = pair + dot(y, y, last) * dot(hidden, hidden, last)
    same = (spot[:, :1] == spot.T[:1, :]) & (spot[:, :1] >= 0.0)
    row_sums = jnp.sum(jnp.where(same, pair, 0.0), axis=1, keepdims=True)
    lane = lax.broadcasted_iota(jnp.int32, (TILE, LANES), 1).astype(F32)

    @pl.when(i == 0)
    def _():
        sum_ref[...] = jnp.zeros_like(sum_ref)

    for half in range(2):
        hot = spot == lane + half * LANES
        sum_ref[half : half + 1, :] += jnp.sum(jnp.where(hot, row_sums, 0.0), axis=0, keepdims=True)


def backward(where, wide_y, x, w_down, gate, up, hidden):
    def tall(n):
        return pl.BlockSpec((TILE, n), lambda i, where: (i, 0))

    rows = pl.BlockSpec((1, NZ, SLOTS, D), lambda i, where: (i, 0, 0, 0))
    return pl.pallas_call(
        backward_kernel,
        grid_spec=pltpu.PrefetchScalarGridSpec(
            num_scalar_prefetch=1,
            grid=(NX,),
            in_specs=[
                pl.BlockSpec((NZ, SLOTS, D), lambda i, where: (where[i], 0, 0)),
                pl.BlockSpec((NZ, SLOTS, LANES), lambda i, where: (where[i], 0, D // LANES)),
                rows,
                pl.BlockSpec(w_down.shape, lambda i, where: (0, 0, 0), pipeline_mode=pl.Buffered(1)),
                tall(HID),
                tall(HID),
                tall(HID),
            ],
            out_specs=[tall(HID), tall(HID), tall(1), pl.BlockSpec((2, LANES), lambda i, where: (0, 0))],
            scratch_shapes=[pltpu.VMEM((NZ, SLOTS, D), BF)],
        ),
        out_shape=[
            jax.ShapeDtypeStruct((ROWS, HID), BF),
            jax.ShapeDtypeStruct((ROWS, HID), BF),
            jax.ShapeDtypeStruct((ROWS, 1), F32),
            jax.ShapeDtypeStruct((2, LANES), F32),
        ],
        compiler_params=pltpu.CompilerParams(vmem_limit_bytes=40 * MIB),
        cost_estimate=pl.CostEstimate(flops=5 * ROWS * D * HID, bytes_accessed=20 * MIB, transcendentals=ROWS * HID),
        name="backward",
    )(where, wide_y, wide_y, x, w_down, gate, up, hidden)


def grads_kernel(
    where_ref, x_ref, y_ref, hidden_ref, dg_ref, du_ref, spot_ref, factor_ref, gg_ref, gu_ref, gd_ref, scaled, turned, moved, by_row
):
    @pl.when(pl.program_id(0) == 0)
    def _():
        spot = spot_ref[...]
        lane = lax.broadcasted_iota(jnp.int32, (ROWS, LANES), 1).astype(F32)
        factor = jnp.zeros((ROWS, 1), F32)
        for half in range(2):
            chosen = jnp.where(spot == lane + half * LANES, factor_ref[half : half + 1, :], 0.0)
            factor = factor + jnp.sum(chosen, axis=1, keepdims=True)
        scaled[:, :HID] = (factor * dg_ref[...].astype(F32)).astype(BF)
        scaled[:, HID:] = (factor * du_ref[...].astype(F32)).astype(BF)
        for i in range(NX):
            for j in range(NZ):
                block = where_ref[i] * NZ + where_ref[NX + j]
                first = (i * NZ + j) * SLOTS
                moved[block] = hidden_ref[first : first + SLOTS]
                by_row[block] = factor[first : first + SLOTS]
        turned[...] = moved[...].reshape(ROWS, HID).T

    x = x_ref[...].reshape(ROWS, COLS)
    both = dot(x, scaled[...], ((0,), (0,))).astype(BF)
    gg_ref[0] = both[:, :HID]
    gu_ref[0] = both[:, HID:]
    cot = (by_row[...] * y_ref[...].astype(F32)).astype(BF).reshape(ROWS, COLS)
    gd_ref[0] = dot(turned[...], cot, ((1,), (0,))).astype(BF)


def gradients(where, x, wide_y, hidden, d_gate, d_up, spot, factors):
    def whole(a):
        return pl.BlockSpec(a.shape, lambda i, where: (0, 0), pipeline_mode=pl.Buffered(1))

    return pl.pallas_call(
        grads_kernel,
        grid_spec=pltpu.PrefetchScalarGridSpec(
            num_scalar_prefetch=1,
            grid=(D // COLS,),
            in_specs=[
                pl.BlockSpec((NX, NZ, SLOTS, COLS), lambda i, where: (0, 0, 0, i)),
                pl.BlockSpec((BLOCKS, SLOTS, COLS), lambda i, where: (0, 0, i)),
                whole(hidden),
                whole(d_gate),
                whole(d_up),
                whole(spot),
                whole(factors),
            ],
            out_specs=[
                pl.BlockSpec((1, COLS, HID), lambda i, where: (0, i, 0)),
                pl.BlockSpec((1, COLS, HID), lambda i, where: (0, i, 0)),
                pl.BlockSpec((1, HID, COLS), lambda i, where: (0, 0, i)),
            ],
            scratch_shapes=[
                pltpu.VMEM((ROWS, 2 * HID), BF),
                pltpu.VMEM((HID, ROWS), BF),
                pltpu.VMEM((BLOCKS, SLOTS, HID), BF),
                pltpu.VMEM((BLOCKS, SLOTS, 1), F32),
            ],
        ),
        out_shape=[
            jax.ShapeDtypeStruct((1, D, HID), BF),
            jax.ShapeDtypeStruct((1, D, HID), BF),
            jax.ShapeDtypeStruct((1, HID, D), BF),
        ],
        compiler_params=pltpu.CompilerParams(vmem_limit_bytes=40 * MIB),
        cost_estimate=pl.CostEstimate(flops=6 * ROWS * D * HID, bytes_accessed=18 * MIB, transcendentals=0),
        name="gradients",
    )(where, x, wide_y, hidden, d_gate, d_up, spot, factors)


def on_device(tokens, cotangent, routes, example_ids, w_gate, w_up, w_down):
    ix, iz = lax.axis_index("x"), lax.axis_index("z")
    where = jnp.concatenate([(ix + jnp.array(ORDER["x"])) % NX, (iz + jnp.array(ORDER["z"])) % NZ]).astype(jnp.int32)
    tok_count, width = tokens.shape
    flat_routes = routes.reshape(-1)
    owner_hot = (flat_routes[:, None] == jnp.arange(NE)[None, :]).astype(jnp.int32)
    before = jnp.cumsum(owner_hot, axis=0) - owner_hot
    slot_of = flat_routes * CAP + jnp.sum(before * owner_hot, axis=1)
    placed = (jnp.arange(SLOTS)[:, None] == slot_of[None, :]).astype(jnp.int32)
    placed = jnp.sum(placed.reshape(SLOTS, tok_count, 2), axis=2)
    placed_bf = placed.astype(BF)
    filled = jnp.sum(placed, axis=1) > 0
    send_ids = jnp.where(filled, jnp.sum(placed * example_ids.reshape(-1)[None, :], axis=1), -1)
    send_x = jnp.dot(placed_bf, tokens, preferred_element_type=F32).astype(BF)
    send_dy = jnp.dot(placed_bf, cotangent, preferred_element_type=F32).astype(BF)
    id_cols = jnp.broadcast_to(send_ids.astype(BF)[:, None], (SLOTS, LANES))
    send = jnp.concatenate(
        [
            jnp.concatenate([send_x, id_cols], axis=1).reshape(NE, CAP, width + LANES),
            jnp.concatenate([send_dy, id_cols], axis=1).reshape(NE, CAP, width + LANES),
        ],
        axis=1,
    )
    got = lax.all_to_all(send, EXPERT, split_axis=0, concat_axis=0, tiled=True)
    local_x = got[:, :CAP, :width].reshape(SLOTS, width)
    local_dy = got[:, CAP:].reshape(SLOTS, width + LANES)
    wide_y = lax.all_gather(local_dy, ("x", "z"), axis=0)
    line_x = line_of(ring_gather(local_x[:MID], "x"))
    line_z = line_of(ring_gather(local_x[MID:], "z"))
    a_pieces = ring_gather(line_x, "z")
    b_pieces = ring_gather(line_z, "x")
    x, gate, up_part, hidden, left, right = forward(where, a_pieces, b_pieces, w_gate, w_up, w_down)
    right, wide_y = lax.optimization_barrier((right, wide_y))
    right_line = lax.psum_scatter(right.reshape(ROWS, D - LEFT), "x", scatter_dimension=0, tiled=True)
    kept = {}

    def hook(step, pair):
        if step == 1:
            kept["back"] = backward(where, wide_y, x, w_down, gate, up_part, hidden)
            pair, kept["sum"] = lax.optimization_barrier((pair, kept["back"][3]))
        elif step == 2:
            total = jnp.sum(spread(kept["sum"], ("x", "z"), BLOCKS).reshape(BLOCKS, 2, LANES), axis=0)
            pair, kept["sum"] = lax.optimization_barrier((pair, total))
        elif step == 3:
            total = jnp.sum(spread(kept["sum"], EXPERT, NE).reshape(NE, 2, LANES), axis=0)
            pair, norms, line = lax.optimization_barrier((pair, jnp.sqrt(total), right_line.astype(F32)))
            kept["norms"], kept["line"] = norms, line
        else:
            d_gate, d_up, spot, _ = kept["back"]
            factors = RADIUS / (kept["norms"] + GAMMA)
            grads = gradients(where, x, wide_y, hidden, d_gate, d_up, spot, factors)
            pair, kept["grads"] = lax.optimization_barrier((pair, grads))
        return pair

    left_line = ring_sum(left, "z", hook)
    right_out = lax.psum_scatter(kept["line"], "z", scatter_dimension=0, tiled=True).astype(BF)
    left_out = direct_sum(left_line, "x")
    own_out = jnp.concatenate([left_out, right_out], axis=1)
    returned = lax.all_to_all(own_out.reshape(NE, CAP, width), EXPERT, split_axis=0, concat_axis=0, tiled=True)
    mixed = jnp.dot(placed_bf.T, returned.reshape(SLOTS, width), preferred_element_type=F32).astype(BF)
    norms = kept["norms"]
    own_norms = lax.dynamic_slice(norms.reshape(BLOCKS, 8), (ix * NZ + iz, 0), (1, EX_ROW))
    return (mixed, own_norms, *kept["grads"])


def solution(mesh):
    mesh = Mesh(mesh.devices.reshape(NX, NZ, 4, 2), ("x", "z", "y", "c"))
    data, every = ("x", "z"), ("x", "z", "y", "c")
    return jax.shard_map(
        on_device,
        mesh=mesh,
        in_specs=(
            P(every, None),
            P(every, None),
            P(every, None),
            P(data, EXPERT),
            P(EXPERT, None, data),
            P(EXPERT, None, data),
            P(EXPERT, data, None),
        ),
        out_specs=(
            P(every, None),
            P(data, None),
            P(EXPERT, None, data),
            P(EXPERT, None, data),
            P(EXPERT, data, None),
        ),
        check_vma=False,
    )
```

```python
import math

import jax
import jax.numpy as jnp
from jax import lax
from jax.experimental import pallas as pl
from jax.experimental.pallas import tpu as pltpu
from jax.sharding import Mesh, PartitionSpec as P

D = 3072
FF = 8192
CAP = 4
EX_ROW = 6
NX, NZ, NE = 4, 8, 8
BLOCKS = NX * NZ
SLOTS = NE * CAP
ROWS = BLOCKS * SLOTS
HID = FF // BLOCKS
SIZE = {"x": NX, "z": NZ}
ORDER = {"x": (0, -1, 1, 2), "z": (0, -1, 1, -2, 2, -3, 3, 4)}
GAMMA = 0.01
RADIUS = math.sqrt(3.0 * D * FF * NE / (BLOCKS * EX_ROW))
EXPERT = ("y", "c")
BF = jnp.bfloat16
F32 = jnp.float32
MIB = 1 << 20
LANES = 128
TILE = NZ * SLOTS
MID = SLOTS // 2
COLS = 512
LEFT = D // 2


def shift(a, axis, step):
    n = SIZE[axis]
    return lax.ppermute(a, axis, [(i, (i + step) % n) for i in range(n)])


def ring_gather(a, axis):
    half = SIZE[axis] // 2
    mid = a.shape[-2] // 2
    pieces = [a]
    up = down = a
    for _ in range(1, half):
        up, down = shift(up, axis, 1), shift(down, axis, -1)
        pieces += [up, down]
    return pieces + [shift(up[..., :mid, :], axis, 1), shift(down[..., mid:, :], axis, -1)]


def line_of(pieces):
    return jnp.stack(pieces[:-2] + [jnp.concatenate(pieces[-2:], axis=-2)], axis=0)


def plus(a, b):
    return (a.astype(F32) + b.astype(F32)).astype(BF)


def ring_sum(far_up, far_down, parts, axis, hook):
    half = SIZE[axis] // 2
    place = ORDER[axis].index

    def get(k):
        return parts[place(k)]

    mid = far_up.shape[0]
    up, down = shift(far_up, axis, 1), shift(far_down, axis, -1)
    own_up, own_down = hook(1, (get(half - 1), get(1 - half)))
    up = jnp.concatenate([plus(up, own_up[:mid]), own_up[mid:]], axis=0)
    down = jnp.concatenate([own_down[:mid], plus(down, own_down[mid:])], axis=0)
    for k in range(half - 1, 0, -1):
        up, down = shift(up, axis, 1), shift(down, axis, -1)
        if k > 1:
            own_up, own_down = hook(half - k + 1, (get(k - 1), get(1 - k)))
            up, down = plus(up, own_up), plus(down, own_down)
    own = hook(half, get(0))
    return (up.astype(F32) + down.astype(F32) + own.astype(F32)).astype(BF)


def direct_sum(parts, axis):
    total = parts[0].astype(F32)
    for place, k in enumerate(ORDER[axis]):
        if k:
            total = total + shift(parts[place], axis, k).astype(F32)
    return total.astype(BF)


def spread(a, axes, n):
    return lax.all_to_all(jnp.broadcast_to(a[None], (n,) + a.shape), axes, 0, 0, tiled=True)


def dot(a, b, dims):
    return lax.dot_general(a, b, (dims, ((), ())), preferred_element_type=F32)


def forward_kernel(where_ref, *refs):
    a_refs, refs = refs[: NZ + 1], refs[NZ + 1 :]
    b_refs, refs = refs[: NX + 1], refs[NX + 1 :]
    wg_ref, wu_ref, wd_ref, x_out, gate_ref, up_ref, hidden_ref, far_up, far_down, left_ref, right_ref, rows_ref, in_sems, out_sems = refs
    step = pl.program_id(0)
    quarter = MID // 2
    arrivals = []
    for i in range(NX):
        moves = [(a_refs[j].at[i], rows_ref.at[i, j, pl.ds(0, MID)]) for j in range(NZ - 1)]
        moves += [(a_refs[NZ - 1 + h].at[i], rows_ref.at[i, NZ - 1, pl.ds(h * quarter, quarter)]) for h in range(2)]
        if i < NX - 1:
            moves += [(b_refs[i], rows_ref.at[i, :, pl.ds(MID, MID)])]
        else:
            moves += [(b_refs[i + h], rows_ref.at[i, :, pl.ds(MID + h * quarter, quarter)]) for h in range(2)]
        arrivals.append([pltpu.make_async_copy(s, d, in_sems.at[i, n]) for n, (s, d) in enumerate(moves)])
    leaving = [pltpu.make_async_copy(rows_ref.at[i], x_out.at[i], out_sems.at[i]) for i in range(NX)]

    @pl.when(step == 0)
    def _():
        for group in arrivals:
            for copy in group:
                copy.start()

    for i in range(NX):

        @pl.when(step == i)
        def _():
            for copy in arrivals[i]:
                copy.wait()
            leaving[i].start()

    x = rows_ref[step].reshape(TILE, D)
    gate = dot(x, wg_ref[0], ((1,), (0,)))
    up = dot(x, wu_ref[0], ((1,), (0,)))
    hidden = (gate * jax.nn.sigmoid(gate) * up).astype(BF)
    gate_ref[...] = gate
    up_ref[...] = up
    hidden_ref[...] = hidden
    out = dot(hidden, wd_ref[0, :, :LEFT], ((1,), (0,))).astype(BF)
    left_ref[...] = out[: TILE - SLOTS].reshape(NZ - 1, 1, SLOTS, LEFT)

    @pl.when(step < NX // 2)
    def _():
        far_up[0] = out[TILE - SLOTS :]

    @pl.when(step >= NX // 2)
    def _():
        far_down[0] = out[TILE - SLOTS :]

    out = dot(hidden, wd_ref[0, :, LEFT:], ((1,), (0,))).astype(BF)
    for j in range(NZ):
        right_ref[0, where_ref[NX + j]] = out[j * SLOTS : (j + 1) * SLOTS]

    @pl.when(step == NX - 1)
    def _():
        for copy in leaving:
            copy.wait()


def forward(where, a_pieces, b_pieces, w_gate, w_up, w_down):
    outside = pl.BlockSpec(memory_space=pltpu.HBM)

    def whole(a):
        return pl.BlockSpec(a.shape, lambda i, where: (0, 0, 0), pipeline_mode=pl.Buffered(1))

    def tall(n):
        return pl.BlockSpec((TILE, n), lambda i, where: (i, 0))

    return pl.pallas_call(
        forward_kernel,
        grid_spec=pltpu.PrefetchScalarGridSpec(
            num_scalar_prefetch=1,
            grid=(NX,),
            in_specs=[outside] * (NZ + NX + 2) + [whole(w_gate), whole(w_up), whole(w_down)],
            out_specs=[
                outside,
                tall(HID),
                tall(HID),
                tall(HID),
                pl.BlockSpec((1, SLOTS, LEFT), lambda i, where: (jnp.minimum(i, NX // 2 - 1), 0, 0)),
                pl.BlockSpec((1, SLOTS, LEFT), lambda i, where: (jnp.maximum(i - NX // 2, 0), 0, 0)),
                pl.BlockSpec((NZ - 1, 1, SLOTS, LEFT), lambda i, where: (0, i, 0, 0)),
                pl.BlockSpec((1, NZ, SLOTS, D - LEFT), lambda i, where: (where[i], 0, 0, 0)),
            ],
            scratch_shapes=[
                pltpu.VMEM((NX, NZ, SLOTS, D), BF),
                pltpu.SemaphoreType.DMA((NX, NZ + 3)),
                pltpu.SemaphoreType.DMA((NX,)),
            ],
        ),
        out_shape=[
            jax.ShapeDtypeStruct((NX, NZ, SLOTS, D), BF),
            jax.ShapeDtypeStruct((ROWS, HID), F32),
            jax.ShapeDtypeStruct((ROWS, HID), F32),
            jax.ShapeDtypeStruct((ROWS, HID), BF),
            jax.ShapeDtypeStruct((NX // 2, SLOTS, LEFT), BF),
            jax.ShapeDtypeStruct((NX // 2, SLOTS, LEFT), BF),
            jax.ShapeDtypeStruct((NZ - 1, NX, SLOTS, LEFT), BF),
            jax.ShapeDtypeStruct((NX, NZ, SLOTS, D - LEFT), BF),
        ],
        compiler_params=pltpu.CompilerParams(vmem_limit_bytes=60 * MIB),
        cost_estimate=pl.CostEstimate(flops=6 * ROWS * D * HID, bytes_accessed=20 * MIB, transcendentals=ROWS * HID),
        name="forward",
    )(where, *a_pieces, *b_pieces, w_gate, w_up, w_down)


def backward_kernel(where_ref, y_ref, id_ref, x_ref, wd_ref, gate_ref, up_ref, hidden_ref, dg_ref, du_ref, spot_ref, sum_ref, y_rows):
    i = pl.program_id(0)
    at_x = where_ref[i]
    spots = []
    for j in range(NZ):
        at_z = where_ref[NX + j]
        y_rows[j] = y_ref[at_z]
        block_id = id_ref[at_z].astype(F32)
        start = ((at_x * NZ + at_z) * 8).astype(F32)
        spots.append(jnp.where(block_id >= 0.0, block_id + start, -1.0))
    spot = jnp.concatenate(spots, axis=0)
    spot_ref[...] = spot[:, :1]
    y = y_rows[...].reshape(TILE, D)
    x = x_ref[0].reshape(TILE, D)
    back = dot(y, wd_ref[0], ((1,), (1,)))
    gate, up, hidden = gate_ref[...], up_ref[...], hidden_ref[...]
    sig = jax.nn.sigmoid(gate)
    d_gate = (back * up * sig * (1.0 + gate * (1.0 - sig))).astype(BF)
    d_up = (back * (gate * sig)).astype(BF)
    dg_ref[...] = d_gate
    du_ref[...] = d_up
    last = ((1,), (1,))
    pair = dot(x, x, last) * (dot(d_gate, d_gate, last) + dot(d_up, d_up, last))
    pair = pair + dot(y, y, last) * dot(hidden, hidden, last)
    same = (spot[:, :1] == spot.T[:1, :]) & (spot[:, :1] >= 0.0)
    row_sums = jnp.sum(jnp.where(same, pair, 0.0), axis=1, keepdims=True)
    lane = lax.broadcasted_iota(jnp.int32, (TILE, LANES), 1).astype(F32)

    @pl.when(i == 0)
    def _():
        sum_ref[...] = jnp.zeros_like(sum_ref)

    for half in range(2):
        hot = spot == lane + half * LANES
        sum_ref[half : half + 1, :] += jnp.sum(jnp.where(hot, row_sums, 0.0), axis=0, keepdims=True)


def backward(where, wide_y, x, w_down, gate, up, hidden):
    def tall(n):
        return pl.BlockSpec((TILE, n), lambda i, where: (i, 0))

    rows = pl.BlockSpec((1, NZ, SLOTS, D), lambda i, where: (i, 0, 0, 0))
    return pl.pallas_call(
        backward_kernel,
        grid_spec=pltpu.PrefetchScalarGridSpec(
            num_scalar_prefetch=1,
            grid=(NX,),
            in_specs=[
                pl.BlockSpec((NZ, SLOTS, D), lambda i, where: (where[i], 0, 0)),
                pl.BlockSpec((NZ, SLOTS, LANES), lambda i, where: (where[i], 0, D // LANES)),
                rows,
                pl.BlockSpec(w_down.shape, lambda i, where: (0, 0, 0), pipeline_mode=pl.Buffered(1)),
                tall(HID),
                tall(HID),
                tall(HID),
            ],
            out_specs=[tall(HID), tall(HID), tall(1), pl.BlockSpec((2, LANES), lambda i, where: (0, 0))],
            scratch_shapes=[pltpu.VMEM((NZ, SLOTS, D), BF)],
        ),
        out_shape=[
            jax.ShapeDtypeStruct((ROWS, HID), BF),
            jax.ShapeDtypeStruct((ROWS, HID), BF),
            jax.ShapeDtypeStruct((ROWS, 1), F32),
            jax.ShapeDtypeStruct((2, LANES), F32),
        ],
        compiler_params=pltpu.CompilerParams(vmem_limit_bytes=60 * MIB),
        cost_estimate=pl.CostEstimate(flops=5 * ROWS * D * HID, bytes_accessed=20 * MIB, transcendentals=ROWS * HID),
        name="backward",
    )(where, wide_y, wide_y, x, w_down, gate, up, hidden)


def grads_kernel(
    where_ref, x_ref, y_ref, hidden_ref, dg_ref, du_ref, spot_ref, factor_ref, gg_ref, gu_ref, gd_ref, scaled, turned, moved, by_row
):
    @pl.when(pl.program_id(0) == 0)
    def _():
        spot = spot_ref[...]
        lane = lax.broadcasted_iota(jnp.int32, (ROWS, LANES), 1).astype(F32)
        factor = jnp.zeros((ROWS, 1), F32)
        for half in range(2):
            chosen = jnp.where(spot == lane + half * LANES, factor_ref[half : half + 1, :], 0.0)
            factor = factor + jnp.sum(chosen, axis=1, keepdims=True)
        scaled[:, :HID] = (factor * dg_ref[...].astype(F32)).astype(BF)
        scaled[:, HID:] = (factor * du_ref[...].astype(F32)).astype(BF)
        for i in range(NX):
            for j in range(NZ):
                block = where_ref[i] * NZ + where_ref[NX + j]
                first = (i * NZ + j) * SLOTS
                moved[block] = hidden_ref[first : first + SLOTS]
                by_row[block] = factor[first : first + SLOTS]
        turned[...] = moved[...].reshape(ROWS, HID).T

    x = x_ref[...].reshape(ROWS, COLS)
    both = dot(x, scaled[...], ((0,), (0,))).astype(BF)
    gg_ref[0] = both[:, :HID]
    gu_ref[0] = both[:, HID:]
    cot = (by_row[...] * y_ref[...].astype(F32)).astype(BF).reshape(ROWS, COLS)
    gd_ref[0] = dot(turned[...], cot, ((1,), (0,))).astype(BF)


def gradients(where, x, wide_y, hidden, d_gate, d_up, spot, factors):
    def whole(a):
        return pl.BlockSpec(a.shape, lambda i, where: (0, 0), pipeline_mode=pl.Buffered(1))

    return pl.pallas_call(
        grads_kernel,
        grid_spec=pltpu.PrefetchScalarGridSpec(
            num_scalar_prefetch=1,
            grid=(D // COLS,),
            in_specs=[
                pl.BlockSpec((NX, NZ, SLOTS, COLS), lambda i, where: (0, 0, 0, i)),
                pl.BlockSpec((BLOCKS, SLOTS, COLS), lambda i, where: (0, 0, i)),
                whole(hidden),
                whole(d_gate),
                whole(d_up),
                whole(spot),
                whole(factors),
            ],
            out_specs=[
                pl.BlockSpec((1, COLS, HID), lambda i, where: (0, i, 0)),
                pl.BlockSpec((1, COLS, HID), lambda i, where: (0, i, 0)),
                pl.BlockSpec((1, HID, COLS), lambda i, where: (0, 0, i)),
            ],
            scratch_shapes=[
                pltpu.VMEM((ROWS, 2 * HID), BF),
                pltpu.VMEM((HID, ROWS), BF),
                pltpu.VMEM((BLOCKS, SLOTS, HID), BF),
                pltpu.VMEM((BLOCKS, SLOTS, 1), F32),
            ],
        ),
        out_shape=[
            jax.ShapeDtypeStruct((1, D, HID), BF),
            jax.ShapeDtypeStruct((1, D, HID), BF),
            jax.ShapeDtypeStruct((1, HID, D), BF),
        ],
        compiler_params=pltpu.CompilerParams(vmem_limit_bytes=60 * MIB),
        cost_estimate=pl.CostEstimate(flops=6 * ROWS * D * HID, bytes_accessed=18 * MIB, transcendentals=0),
        name="gradients",
    )(where, x, wide_y, hidden, d_gate, d_up, spot, factors)


def on_device(tokens, cotangent, routes, example_ids, w_gate, w_up, w_down):
    ix, iz = lax.axis_index("x"), lax.axis_index("z")
    where = jnp.concatenate([(ix + jnp.array(ORDER["x"])) % NX, (iz + jnp.array(ORDER["z"])) % NZ]).astype(jnp.int32)
    tok_count, width = tokens.shape
    flat_routes = routes.reshape(-1)
    owner_hot = (flat_routes[:, None] == jnp.arange(NE)[None, :]).astype(jnp.int32)
    before = jnp.cumsum(owner_hot, axis=0) - owner_hot
    slot_of = flat_routes * CAP + jnp.sum(before * owner_hot, axis=1)
    placed = (jnp.arange(SLOTS)[:, None] == slot_of[None, :]).astype(jnp.int32)
    placed = jnp.sum(placed.reshape(SLOTS, tok_count, 2), axis=2)
    placed_bf = placed.astype(BF)
    filled = jnp.sum(placed, axis=1) > 0
    send_ids = jnp.where(filled, jnp.sum(placed * example_ids.reshape(-1)[None, :], axis=1), -1)
    send_x = jnp.dot(placed_bf, tokens, preferred_element_type=F32).astype(BF)
    send_dy = jnp.dot(placed_bf, cotangent, preferred_element_type=F32).astype(BF)
    id_cols = jnp.broadcast_to(send_ids.astype(BF)[:, None], (SLOTS, LANES))
    send = jnp.concatenate(
        [
            jnp.concatenate([send_x, id_cols], axis=1).reshape(NE, CAP, width + LANES),
            jnp.concatenate([send_dy, id_cols], axis=1).reshape(NE, CAP, width + LANES),
        ],
        axis=1,
    )
    got = lax.all_to_all(send, EXPERT, split_axis=0, concat_axis=0, tiled=True)
    local_x = got[:, :CAP, :width].reshape(SLOTS, width)
    local_dy = got[:, CAP:].reshape(SLOTS, width + LANES)
    wide_y = lax.all_gather(local_dy, ("x", "z"), axis=0)
    line_x = line_of(ring_gather(local_x[:MID], "x"))
    line_z = line_of(ring_gather(local_x[MID:], "z"))
    a_pieces = ring_gather(line_x, "z")
    b_pieces = ring_gather(line_z, "x")
    x, gate, up_part, hidden, far_up, far_down, left, right = forward(
        where, a_pieces, b_pieces, w_gate, w_up, w_down
    )
    right, wide_y = lax.optimization_barrier((right, wide_y))
    right_line = lax.psum_scatter(right.reshape(ROWS, D - LEFT), "x", scatter_dimension=0, tiled=True)
    kept = {}

    def hook(step, sent):
        if step == 1:
            kept["back"] = backward(where, wide_y, x, w_down, gate, up_part, hidden)
            sent, kept["sum"] = lax.optimization_barrier((sent, kept["back"][3]))
        elif step == 2:
            total = jnp.sum(spread(kept["sum"], ("x", "z"), BLOCKS).reshape(BLOCKS, 2, LANES), axis=0)
            sent, kept["sum"], line = lax.optimization_barrier((sent, total, right_line))
            kept["line"] = lax.psum_scatter(line.astype(F32), "z", scatter_dimension=0, tiled=True)
        elif step == 3:
            total = jnp.sum(spread(kept["sum"], EXPERT, NE).reshape(NE, 2, LANES), axis=0)
            sent, kept["norms"] = lax.optimization_barrier((sent, jnp.sqrt(total)))
        else:
            d_gate, d_up, spot, _ = kept["back"]
            factors = RADIUS / (kept["norms"] + GAMMA)
            grads = gradients(where, x, wide_y, hidden, d_gate, d_up, spot, factors)
            sent, kept["grads"] = lax.optimization_barrier((sent, grads))
        return sent

    left_line = ring_sum(far_up, far_down, left, "z", hook)
    right_out = kept["line"].astype(BF)
    left_out = direct_sum(left_line, "x")
    own_out = jnp.concatenate([left_out, right_out], axis=1)
    returned = lax.all_to_all(own_out.reshape(NE, CAP, width), EXPERT, split_axis=0, concat_axis=0, tiled=True)
    mixed = jnp.dot(placed_bf.T, returned.reshape(SLOTS, width), preferred_element_type=F32).astype(BF)
    norms = kept["norms"]
    own_norms = lax.dynamic_slice(norms.reshape(BLOCKS, 8), (ix * NZ + iz, 0), (1, EX_ROW))
    return (mixed, own_norms, *kept["grads"])


def solution(mesh):
    mesh = Mesh(mesh.devices.reshape(NX, NZ, 4, 2), ("x", "z", "y", "c"))
    data, every = ("x", "z"), ("x", "z", "y", "c")
    return jax.shard_map(
        on_device,
        mesh=mesh,
        in_specs=(
            P(every, None),
            P(every, None),
            P(every, None),
            P(data, EXPERT),
            P(EXPERT, None, data),
            P(EXPERT, None, data),
            P(EXPERT, data, None),
        ),
        out_specs=(
            P(every, None),
            P(data, None),
            P(EXPERT, None, data),
            P(EXPERT, None, data),
            P(EXPERT, data, None),
        ),
        check_vma=False,
    )
```

```python
import math

import jax
import jax.numpy as jnp
from jax import lax
from jax.experimental import pallas as pl
from jax.experimental.pallas import tpu as pltpu
from jax.sharding import Mesh, PartitionSpec as P

D = 3072
FF = 8192
CAP = 4
EX_ROW = 6
NX, NZ, NE = 4, 8, 8
BLOCKS = NX * NZ
SLOTS = NE * CAP
ROWS = BLOCKS * SLOTS
HID = FF // BLOCKS
SIZE = {"x": NX, "z": NZ}
ORDER = {"x": (0, -1, 1, 2), "z": (0, -1, 1, -2, 2, -3, 3, 4)}
GAMMA = 0.01
RADIUS = math.sqrt(3.0 * D * FF * NE / (BLOCKS * EX_ROW))
EXPERT = ("y", "c")
BF = jnp.bfloat16
F32 = jnp.float32
MIB = 1 << 20
LANES = 128
TILE = NZ * SLOTS
MID = SLOTS // 2
COLS = 512
LEFT = D // 2


def shift(a, axis, step):
    n = SIZE[axis]
    return lax.ppermute(a, axis, [(i, (i + step) % n) for i in range(n)])


def ring_gather(a, axis):
    half = SIZE[axis] // 2
    mid = a.shape[-2] // 2
    pieces = [a]
    up = down = a
    for _ in range(1, half):
        up, down = shift(up, axis, 1), shift(down, axis, -1)
        pieces += [up, down]
    return pieces + [shift(up[..., :mid, :], axis, 1), shift(down[..., mid:, :], axis, -1)]


def line_of(pieces):
    return jnp.stack(pieces[:-2] + [jnp.concatenate(pieces[-2:], axis=-2)], axis=0)


def plus(a, b):
    return (a.astype(F32) + b.astype(F32)).astype(BF)


def ring_sum(far_up, far_down, parts, axis, hook):
    half = SIZE[axis] // 2
    place = ORDER[axis].index

    def get(k):
        return parts[place(k)]

    mid = far_up.shape[0]
    up, down = shift(far_up, axis, 1), shift(far_down, axis, -1)
    own_up, own_down = hook(1, (get(half - 1), get(1 - half)))
    up = jnp.concatenate([plus(up, own_up[:mid]), own_up[mid:]], axis=0)
    down = jnp.concatenate([own_down[:mid], plus(down, own_down[mid:])], axis=0)
    for k in range(half - 1, 0, -1):
        up, down = shift(up, axis, 1), shift(down, axis, -1)
        if k > 1:
            own_up, own_down = hook(half - k + 1, (get(k - 1), get(1 - k)))
            up, down = plus(up, own_up), plus(down, own_down)
    own = hook(half, get(0))
    return (up.astype(F32) + down.astype(F32) + own.astype(F32)).astype(BF)


def direct_sum(parts, axis):
    total = parts[0].astype(F32)
    for place, k in enumerate(ORDER[axis]):
        if k:
            total = total + shift(parts[place], axis, k).astype(F32)
    return total.astype(BF)


def spread(a, axes, n):
    return lax.all_to_all(jnp.broadcast_to(a[None], (n,) + a.shape), axes, 0, 0, tiled=True)


def dot(a, b, dims):
    return lax.dot_general(a, b, (dims, ((), ())), preferred_element_type=F32)


def forward_kernel(where_ref, *refs):
    a_refs, refs = refs[: NZ + 1], refs[NZ + 1 :]
    b_refs, refs = refs[: NX + 1], refs[NX + 1 :]
    wg_ref, wu_ref, wd_ref, x_out, gate_ref, up_ref, hidden_ref, far_up, far_down, left_ref, right_ref, rows_ref, wg, wu, wd, in_sems, w_sems, out_sems = refs
    step = pl.program_id(0)
    quarter = MID // 2
    arrivals = []
    for i in range(NX):
        moves = [(a_refs[j].at[i], rows_ref.at[i, j, pl.ds(0, MID)]) for j in range(NZ - 1)]
        moves += [(a_refs[NZ - 1 + h].at[i], rows_ref.at[i, NZ - 1, pl.ds(h * quarter, quarter)]) for h in range(2)]
        if i < NX - 1:
            moves += [(b_refs[i], rows_ref.at[i, :, pl.ds(MID, MID)])]
        else:
            moves += [(b_refs[i + h], rows_ref.at[i, :, pl.ds(MID + h * quarter, quarter)]) for h in range(2)]
        arrivals.append([pltpu.make_async_copy(s, d, in_sems.at[i, n]) for n, (s, d) in enumerate(moves)])
    leaving = [pltpu.make_async_copy(rows_ref.at[i], x_out.at[i], out_sems.at[i]) for i in range(NX)]

    weights = [
        pltpu.make_async_copy(s.at[0], d, w_sems.at[n]) for n, (s, d) in enumerate([(wg_ref, wg), (wu_ref, wu), (wd_ref, wd)])
    ]

    @pl.when(step == 0)
    def _():
        for copy in arrivals[0] + weights[:2] + arrivals[1] + weights[2:] + arrivals[2] + arrivals[3]:
            copy.start()
        for copy in weights[:2]:
            copy.wait()

    for i in range(NX):

        @pl.when(step == i)
        def _():
            for copy in arrivals[i]:
                copy.wait()
            leaving[i].start()

    x = rows_ref[step].reshape(TILE, D)
    gate = dot(x, wg[...], ((1,), (0,)))
    up = dot(x, wu[...], ((1,), (0,)))
    hidden = (gate * jax.nn.sigmoid(gate) * up).astype(BF)
    gate_ref[...] = gate
    up_ref[...] = up
    hidden_ref[...] = hidden

    @pl.when(step == 0)
    def _():
        weights[2].wait()

    out = dot(hidden, wd[:, :LEFT], ((1,), (0,))).astype(BF)
    left_ref[...] = out[: TILE - SLOTS].reshape(NZ - 1, 1, SLOTS, LEFT)

    @pl.when(step < NX // 2)
    def _():
        far_up[0] = out[TILE - SLOTS :]

    @pl.when(step >= NX // 2)
    def _():
        far_down[0] = out[TILE - SLOTS :]

    out = dot(hidden, wd[:, LEFT:], ((1,), (0,))).astype(BF)
    for j in range(NZ):
        right_ref[0, where_ref[NX + j]] = out[j * SLOTS : (j + 1) * SLOTS]

    @pl.when(step == NX - 1)
    def _():
        for copy in leaving:
            copy.wait()


def forward(where, a_pieces, b_pieces, w_gate, w_up, w_down):
    outside = pl.BlockSpec(memory_space=pltpu.HBM)

    def tall(n):
        return pl.BlockSpec((TILE, n), lambda i, where: (i, 0))

    return pl.pallas_call(
        forward_kernel,
        grid_spec=pltpu.PrefetchScalarGridSpec(
            num_scalar_prefetch=1,
            grid=(NX,),
            in_specs=[outside] * (NZ + NX + 5),
            out_specs=[
                outside,
                tall(HID),
                tall(HID),
                tall(HID),
                pl.BlockSpec((1, SLOTS, LEFT), lambda i, where: (jnp.minimum(i, NX // 2 - 1), 0, 0)),
                pl.BlockSpec((1, SLOTS, LEFT), lambda i, where: (jnp.maximum(i - NX // 2, 0), 0, 0)),
                pl.BlockSpec((NZ - 1, 1, SLOTS, LEFT), lambda i, where: (0, i, 0, 0)),
                pl.BlockSpec((1, NZ, SLOTS, D - LEFT), lambda i, where: (where[i], 0, 0, 0)),
            ],
            scratch_shapes=[
                pltpu.VMEM((NX, NZ, SLOTS, D), BF),
                pltpu.VMEM((D, HID), BF),
                pltpu.VMEM((D, HID), BF),
                pltpu.VMEM((HID, D), BF),
                pltpu.SemaphoreType.DMA((NX, NZ + 3)),
                pltpu.SemaphoreType.DMA((3,)),
                pltpu.SemaphoreType.DMA((NX,)),
            ],
        ),
        out_shape=[
            jax.ShapeDtypeStruct((NX, NZ, SLOTS, D), BF),
            jax.ShapeDtypeStruct((ROWS, HID), F32),
            jax.ShapeDtypeStruct((ROWS, HID), F32),
            jax.ShapeDtypeStruct((ROWS, HID), BF),
            jax.ShapeDtypeStruct((NX // 2, SLOTS, LEFT), BF),
            jax.ShapeDtypeStruct((NX // 2, SLOTS, LEFT), BF),
            jax.ShapeDtypeStruct((NZ - 1, NX, SLOTS, LEFT), BF),
            jax.ShapeDtypeStruct((NX, NZ, SLOTS, D - LEFT), BF),
        ],
        compiler_params=pltpu.CompilerParams(vmem_limit_bytes=60 * MIB),
        cost_estimate=pl.CostEstimate(flops=6 * ROWS * D * HID, bytes_accessed=20 * MIB, transcendentals=ROWS * HID),
        name="forward",
    )(where, *a_pieces, *b_pieces, w_gate, w_up, w_down)


def backward_kernel(where_ref, y_ref, note_ref, wd_ref, gate_ref, up_ref, hidden_ref, dg_ref, du_ref, spot_ref, sum_ref, y_rows):
    i = pl.program_id(0)
    at_x = where_ref[i]
    spots, notes = [], []
    for j in range(NZ):
        at_z = where_ref[NX + j]
        y_rows[j] = y_ref[at_z]
        note = note_ref[at_z].astype(F32)
        start = ((at_x * NZ + at_z) * 8).astype(F32)
        spots.append(jnp.where(note[:, :LANES] >= 0.0, note[:, :LANES] + start, -1.0))
        notes.append(note[:, LANES:])
    spot = jnp.concatenate(spots, axis=0)
    spot_ref[...] = spot[:, :1]
    notes = jnp.concatenate(notes, axis=0)
    xx = jnp.concatenate([notes[:, :SLOTS] + notes[:, SLOTS : 2 * SLOTS]] * NZ, axis=1)
    yy = jnp.concatenate([notes[:, 2 * SLOTS : 3 * SLOTS] + notes[:, 3 * SLOTS :]] * NZ, axis=1)
    back = dot(y_rows[...].reshape(TILE, D), wd_ref[0], ((1,), (1,)))
    gate, up, hidden = gate_ref[...], up_ref[...], hidden_ref[...]
    sig = jax.nn.sigmoid(gate)
    d_gate = (back * up * sig * (1.0 + gate * (1.0 - sig))).astype(BF)
    d_up = (back * (gate * sig)).astype(BF)
    dg_ref[...] = d_gate
    du_ref[...] = d_up
    last = ((1,), (1,))
    pair = xx * (dot(d_gate, d_gate, last) + dot(d_up, d_up, last)) + yy * dot(hidden, hidden, last)
    same = (spot[:, :1] == spot.T[:1, :]) & (spot[:, :1] >= 0.0)
    row_sums = jnp.sum(jnp.where(same, pair, 0.0), axis=1, keepdims=True)
    lane = lax.broadcasted_iota(jnp.int32, (TILE, LANES), 1).astype(F32)

    @pl.when(i == 0)
    def _():
        sum_ref[...] = jnp.zeros_like(sum_ref)

    for half in range(2):
        hot = spot == lane + half * LANES
        sum_ref[half : half + 1, :] += jnp.sum(jnp.where(hot, row_sums, 0.0), axis=0, keepdims=True)


def backward(where, wide_y, w_down, gate, up, hidden):
    def tall(n):
        return pl.BlockSpec((TILE, n), lambda i, where: (i, 0))

    return pl.pallas_call(
        backward_kernel,
        grid_spec=pltpu.PrefetchScalarGridSpec(
            num_scalar_prefetch=1,
            grid=(NX,),
            in_specs=[
                pl.BlockSpec((NZ, SLOTS, D), lambda i, where: (where[i], 0, 0)),
                pl.BlockSpec((NZ, SLOTS, 2 * LANES), lambda i, where: (where[i], 0, D // (2 * LANES))),
                pl.BlockSpec(w_down.shape, lambda i, where: (0, 0, 0), pipeline_mode=pl.Buffered(1)),
                tall(HID),
                tall(HID),
                tall(HID),
            ],
            out_specs=[tall(HID), tall(HID), tall(1), pl.BlockSpec((2, LANES), lambda i, where: (0, 0))],
            scratch_shapes=[pltpu.VMEM((NZ, SLOTS, D), BF)],
        ),
        out_shape=[
            jax.ShapeDtypeStruct((ROWS, HID), BF),
            jax.ShapeDtypeStruct((ROWS, HID), BF),
            jax.ShapeDtypeStruct((ROWS, 1), F32),
            jax.ShapeDtypeStruct((2, LANES), F32),
        ],
        compiler_params=pltpu.CompilerParams(vmem_limit_bytes=60 * MIB),
        cost_estimate=pl.CostEstimate(flops=3 * ROWS * D * HID, bytes_accessed=12 * MIB, transcendentals=ROWS * HID),
        name="backward",
    )(where, wide_y, wide_y, w_down, gate, up, hidden)


def factor_by_row(spot, factors):
    lane = lax.broadcasted_iota(jnp.int32, (ROWS, LANES), 1).astype(F32)
    factor = jnp.zeros((ROWS, 1), F32)
    for half in range(2):
        chosen = jnp.where(spot == lane + half * LANES, factors[half : half + 1, :], 0.0)
        factor = factor + jnp.sum(chosen, axis=1, keepdims=True)
    return factor


def wide_grads_kernel(x_ref, dg_ref, du_ref, spot_ref, factor_ref, gg_ref, gu_ref, scaled):
    @pl.when(pl.program_id(0) == 0)
    def _():
        factor = factor_by_row(spot_ref[...], factor_ref[...])
        scaled[:, :HID] = (factor * dg_ref[...].astype(F32)).astype(BF)
        scaled[:, HID:] = (factor * du_ref[...].astype(F32)).astype(BF)

    both = dot(x_ref[...].reshape(ROWS, COLS), scaled[...], ((0,), (0,))).astype(BF)
    gg_ref[0] = both[:, :HID]
    gu_ref[0] = both[:, HID:]


def wide_gradients(x, d_gate, d_up, spot, factors):
    def whole(a):
        return pl.BlockSpec(a.shape, lambda i: (0, 0), pipeline_mode=pl.Buffered(1))

    return pl.pallas_call(
        wide_grads_kernel,
        grid=(D // COLS,),
        in_specs=[
            pl.BlockSpec((NX, NZ, SLOTS, COLS), lambda i: (0, 0, 0, i)),
            whole(d_gate),
            whole(d_up),
            whole(spot),
            whole(factors),
        ],
        out_specs=[pl.BlockSpec((1, COLS, HID), lambda i: (0, i, 0))] * 2,
        out_shape=[jax.ShapeDtypeStruct((1, D, HID), BF)] * 2,
        scratch_shapes=[pltpu.VMEM((ROWS, 2 * HID), BF)],
        compiler_params=pltpu.CompilerParams(vmem_limit_bytes=60 * MIB),
        cost_estimate=pl.CostEstimate(flops=4 * ROWS * D * HID, bytes_accessed=11 * MIB, transcendentals=0),
        name="wide_gradients",
    )(x, d_gate, d_up, spot, factors)


def down_grad_kernel(where_ref, y_ref, hidden_ref, spot_ref, factor_ref, gd_ref, turned, moved, by_row):
    @pl.when(pl.program_id(0) == 0)
    def _():
        factor = factor_by_row(spot_ref[...], factor_ref[...])
        for i in range(NX):
            for j in range(NZ):
                block = where_ref[i] * NZ + where_ref[NX + j]
                first = (i * NZ + j) * SLOTS
                moved[block] = hidden_ref[first : first + SLOTS]
                by_row[block] = factor[first : first + SLOTS]
        turned[...] = moved[...].reshape(ROWS, HID).T

    cot = (by_row[...] * y_ref[...].astype(F32)).astype(BF).reshape(ROWS, COLS)
    gd_ref[0] = dot(turned[...], cot, ((1,), (0,))).astype(BF)


def down_gradient(where, wide_y, hidden, spot, factors):
    def whole(a):
        return pl.BlockSpec(a.shape, lambda i, where: (0, 0), pipeline_mode=pl.Buffered(1))

    return pl.pallas_call(
        down_grad_kernel,
        grid_spec=pltpu.PrefetchScalarGridSpec(
            num_scalar_prefetch=1,
            grid=(D // COLS,),
            in_specs=[
                pl.BlockSpec((BLOCKS, SLOTS, COLS), lambda i, where: (0, 0, i)),
                whole(hidden),
                whole(spot),
                whole(factors),
            ],
            out_specs=pl.BlockSpec((1, HID, COLS), lambda i, where: (0, 0, i)),
            scratch_shapes=[
                pltpu.VMEM((HID, ROWS), BF),
                pltpu.VMEM((BLOCKS, SLOTS, HID), BF),
                pltpu.VMEM((BLOCKS, SLOTS, 1), F32),
            ],
        ),
        out_shape=jax.ShapeDtypeStruct((1, HID, D), BF),
        compiler_params=pltpu.CompilerParams(vmem_limit_bytes=60 * MIB),
        cost_estimate=pl.CostEstimate(flops=2 * ROWS * D * HID, bytes_accessed=8 * MIB, transcendentals=0),
        name="down_gradient",
    )(where, wide_y, hidden, spot, factors)


def on_device(tokens, cotangent, routes, example_ids, w_gate, w_up, w_down):
    ix, iz = lax.axis_index("x"), lax.axis_index("z")
    where = jnp.concatenate([(ix + jnp.array(ORDER["x"])) % NX, (iz + jnp.array(ORDER["z"])) % NZ]).astype(jnp.int32)
    tok_count, width = tokens.shape
    flat_routes = routes.reshape(-1)
    owner_hot = (flat_routes[:, None] == jnp.arange(NE)[None, :]).astype(jnp.int32)
    before = jnp.cumsum(owner_hot, axis=0) - owner_hot
    slot_of = flat_routes * CAP + jnp.sum(before * owner_hot, axis=1)
    placed = (jnp.arange(SLOTS)[:, None] == slot_of[None, :]).astype(jnp.int32)
    placed = jnp.sum(placed.reshape(SLOTS, tok_count, 2), axis=2)
    placed_bf = placed.astype(BF)
    filled = jnp.sum(placed, axis=1) > 0
    send_ids = jnp.where(filled, jnp.sum(placed * example_ids.reshape(-1)[None, :], axis=1), -1)
    send_x = jnp.dot(placed_bf, tokens, preferred_element_type=F32).astype(BF)
    send_dy = jnp.dot(placed_bf, cotangent, preferred_element_type=F32).astype(BF)
    id_cols = jnp.broadcast_to(send_ids.astype(BF)[:, None], (SLOTS, LANES))
    send = jnp.concatenate(
        [
            jnp.concatenate([send_x, id_cols], axis=1).reshape(NE, CAP, width + LANES),
            jnp.concatenate([send_dy, id_cols], axis=1).reshape(NE, CAP, width + LANES),
        ],
        axis=1,
    )
    got = lax.all_to_all(send, EXPERT, split_axis=0, concat_axis=0, tiled=True)
    local_x = got[:, :CAP, :width].reshape(SLOTS, width)
    local_dy = got[:, CAP:].reshape(SLOTS, width + LANES)
    last = ((1,), (1,))
    parts = []
    for rows in (local_x, local_dy[:, :width]):
        gram = dot(rows, rows, last)
        high = lax.reduce_precision(gram, 8, 7)
        parts += [high.astype(BF), (gram - high).astype(BF)]
    wide_y = lax.all_gather(jnp.concatenate([local_dy] + parts, axis=1), ("x", "z"), axis=0)
    line_x = line_of(ring_gather(local_x[:MID], "x"))
    line_z = line_of(ring_gather(local_x[MID:], "z"))
    a_pieces = ring_gather(line_x, "z")
    b_pieces = ring_gather(line_z, "x")
    x, gate, up_part, hidden, far_up, far_down, left, right = forward(
        where, a_pieces, b_pieces, w_gate, w_up, w_down
    )
    right, wide_y = lax.optimization_barrier((right, wide_y))
    right_line = lax.psum_scatter(right.reshape(ROWS, D - LEFT), "x", scatter_dimension=0, tiled=True)
    kept = {}

    def hook(step, sent):
        if step == 1:
            kept["back"] = backward(where, wide_y, w_down, gate, up_part, hidden)
            sent, kept["sum"] = lax.optimization_barrier((sent, kept["back"][3]))
        elif step == 2:
            total = jnp.sum(spread(kept["sum"], ("x", "z"), BLOCKS).reshape(BLOCKS, 2, LANES), axis=0)
            sent, kept["sum"], line = lax.optimization_barrier((sent, total, right_line))
            line = lax.optimization_barrier(line.astype(F32))
            kept["line"] = lax.optimization_barrier(lax.psum_scatter(line, "z", scatter_dimension=0, tiled=True))
        elif step == 3:
            total = jnp.sum(spread(kept["sum"], EXPERT, NE).reshape(NE, 2, LANES), axis=0)
            sent, kept["norms"] = lax.optimization_barrier((sent, jnp.sqrt(total)))
        else:
            d_gate, d_up, spot, _ = kept["back"]
            kept["factors"] = RADIUS / (kept["norms"] + GAMMA)
            grads = wide_gradients(x, d_gate, d_up, spot, kept["factors"])
            sent, kept["grads"] = lax.optimization_barrier((sent, tuple(grads)))
        return sent

    left_line = ring_sum(far_up, far_down, left, "z", hook)
    right_out = kept["line"].astype(BF)
    left_out = direct_sum(left_line, "x")
    own_out = jnp.concatenate([left_out, right_out], axis=1)
    own_out, late = lax.optimization_barrier((own_out, hidden))
    grad_down = down_gradient(where, wide_y, late, kept["back"][2], kept["factors"])
    returned = lax.all_to_all(own_out.reshape(NE, CAP, width), EXPERT, split_axis=0, concat_axis=0, tiled=True)
    mixed = jnp.dot(placed_bf.T, returned.reshape(SLOTS, width), preferred_element_type=F32).astype(BF)
    norms = kept["norms"]
    own_norms = lax.dynamic_slice(norms.reshape(BLOCKS, 8), (ix * NZ + iz, 0), (1, EX_ROW))
    return (mixed, own_norms, *kept["grads"], grad_down)


def solution(mesh):
    mesh = Mesh(mesh.devices.reshape(NX, NZ, 4, 2), ("x", "z", "y", "c"))
    data, every = ("x", "z"), ("x", "z", "y", "c")
    return jax.shard_map(
        on_device,
        mesh=mesh,
        in_specs=(
            P(every, None),
            P(every, None),
            P(every, None),
            P(data, EXPERT),
            P(EXPERT, None, data),
            P(EXPERT, None, data),
            P(EXPERT, data, None),
        ),
        out_specs=(
            P(every, None),
            P(data, None),
            P(EXPERT, None, data),
            P(EXPERT, None, data),
            P(EXPERT, data, None),
        ),
        check_vma=False,
    )
```

```python
import math

import jax
import jax.numpy as jnp
from jax import lax
from jax.experimental import pallas as pl
from jax.experimental.pallas import tpu as pltpu
from jax.sharding import Mesh, PartitionSpec as P

D = 3072
FF = 8192
CAP = 4
EX_ROW = 6
NX, NZ, NE = 4, 8, 8
BLOCKS = NX * NZ
SLOTS = NE * CAP
ROWS = BLOCKS * SLOTS
HID = FF // BLOCKS
SIZE = {"x": NX, "z": NZ}
ORDER = {"x": (0, -1, 1, 2), "z": (0, -1, 1, -2, 2, -3, 3, 4)}
GAMMA = 0.01
RADIUS = math.sqrt(3.0 * D * FF * NE / (BLOCKS * EX_ROW))
EXPERT = ("y", "c")
BF = jnp.bfloat16
F32 = jnp.float32
MIB = 1 << 20
LANES = 128
TILE = NZ * SLOTS
MID = SLOTS // 2
COLS = 512
LEFT = D // 2


def shift(a, axis, step):
    n = SIZE[axis]
    return lax.ppermute(a, axis, [(i, (i + step) % n) for i in range(n)])


def ring_gather(a, axis, split):
    half = SIZE[axis] // 2
    mid = a.shape[-2] // 2
    pieces = [a]
    up = down = a
    for _ in range(1, half):
        up, down = shift(up, axis, 1), shift(down, axis, -1)
        pieces += [up, down]
    if split:
        return pieces + [shift(up[..., :mid, :], axis, 1), shift(down[..., mid:, :], axis, -1)]
    return pieces + [shift(up, axis, 1)]


def plus(a, b):
    return (a.astype(F32) + b.astype(F32)).astype(BF)


def ring_sum(far, parts, axis, hook):
    half = SIZE[axis] // 2
    place = ORDER[axis].index

    def get(k):
        return parts[place(k)]

    own_up, down = hook(1, (get(half - 1), get(1 - half)), far)
    up = plus(shift(far, axis, 1), own_up)
    for k in range(half - 1, 0, -1):
        going = up
        up, down = shift(up, axis, 1), shift(down, axis, -1)
        if k > 1:
            own_up, own_down = hook(half - k + 1, (get(k - 1), get(1 - k)), going)
            up, down = plus(up, own_up), plus(down, own_down)
    own = hook(half, get(0), going)
    return (up.astype(F32) + down.astype(F32) + own.astype(F32)).astype(BF)


def direct_sum(parts, axis):
    total = parts[0].astype(F32)
    for place, k in enumerate(ORDER[axis]):
        if k:
            total = total + shift(parts[place], axis, k).astype(F32)
    return total.astype(BF)


def spread(a, axes, n):
    return lax.all_to_all(jnp.broadcast_to(a[None], (n,) + a.shape), axes, 0, 0, tiled=True)


def dot(a, b, dims):
    return lax.dot_general(a, b, (dims, ((), ())), preferred_element_type=F32)


def forward_kernel(where_ref, *refs):
    a_refs, refs = refs[: NZ + 1], refs[NZ + 1 :]
    b_refs, refs = refs[: NX + 1], refs[NX + 1 :]
    wg_ref, wu_ref, wd_ref, x_out, gate_ref, up_ref, hidden_ref, far_ref, left_ref, right_ref, rows_ref, wg, wu, wd, in_sems, w_sems, out_sems = refs
    step = pl.program_id(0)
    quarter = MID // 2
    arrivals = []
    for i in range(NX):
        moves = [(a_refs[j].at[i], rows_ref.at[i, j, pl.ds(0, MID)]) for j in range(NZ - 1)]
        moves += [(a_refs[NZ - 1 + h].at[i], rows_ref.at[i, NZ - 1, pl.ds(h * quarter, quarter)]) for h in range(2)]
        if i < NX - 1:
            moves += [(b_refs[i], rows_ref.at[i, :, pl.ds(MID, MID)])]
        else:
            moves += [(b_refs[i + h], rows_ref.at[i, :, pl.ds(MID + h * quarter, quarter)]) for h in range(2)]
        arrivals.append([pltpu.make_async_copy(s, d, in_sems.at[i, n]) for n, (s, d) in enumerate(moves)])
    leaving = [pltpu.make_async_copy(rows_ref.at[i], x_out.at[i], out_sems.at[i]) for i in range(NX)]

    weights = [
        pltpu.make_async_copy(s.at[0], d, w_sems.at[n]) for n, (s, d) in enumerate([(wg_ref, wg), (wu_ref, wu), (wd_ref, wd)])
    ]

    @pl.when(step == 0)
    def _():
        for copy in arrivals[0] + weights[:2] + arrivals[1] + weights[2:] + arrivals[2] + arrivals[3]:
            copy.start()
        for copy in weights[:2]:
            copy.wait()

    for i in range(NX):

        @pl.when(step == i)
        def _():
            for copy in arrivals[i]:
                copy.wait()
            leaving[i].start()

    x = rows_ref[step].reshape(TILE, D)
    gate = dot(x, wg[...], ((1,), (0,)))
    up = dot(x, wu[...], ((1,), (0,)))
    hidden = (gate * jax.nn.sigmoid(gate) * up).astype(BF)
    gate_ref[...] = gate
    up_ref[...] = up
    hidden_ref[...] = hidden

    @pl.when(step == 0)
    def _():
        weights[2].wait()

    out = dot(hidden, wd[:, :LEFT], ((1,), (0,))).astype(BF)
    left_ref[...] = out[: TILE - SLOTS].reshape(NZ - 1, 1, SLOTS, LEFT)
    far_ref[0] = out[TILE - SLOTS :]
    out = dot(hidden, wd[:, LEFT:], ((1,), (0,))).astype(BF)
    for j in range(NZ):
        right_ref[0, where_ref[NX + j]] = out[j * SLOTS : (j + 1) * SLOTS]

    @pl.when(step == NX - 1)
    def _():
        for copy in leaving:
            copy.wait()


def forward(where, a_pieces, b_pieces, w_gate, w_up, w_down):
    outside = pl.BlockSpec(memory_space=pltpu.HBM)

    def tall(n):
        return pl.BlockSpec((TILE, n), lambda i, where: (i, 0))

    return pl.pallas_call(
        forward_kernel,
        grid_spec=pltpu.PrefetchScalarGridSpec(
            num_scalar_prefetch=1,
            grid=(NX,),
            in_specs=[outside] * (NZ + NX + 5),
            out_specs=[
                outside,
                tall(HID),
                tall(HID),
                tall(HID),
                pl.BlockSpec((1, SLOTS, LEFT), lambda i, where: (i, 0, 0)),
                pl.BlockSpec((NZ - 1, 1, SLOTS, LEFT), lambda i, where: (0, i, 0, 0)),
                pl.BlockSpec((1, NZ, SLOTS, D - LEFT), lambda i, where: (where[i], 0, 0, 0)),
            ],
            scratch_shapes=[
                pltpu.VMEM((NX, NZ, SLOTS, D), BF),
                pltpu.VMEM((D, HID), BF),
                pltpu.VMEM((D, HID), BF),
                pltpu.VMEM((HID, D), BF),
                pltpu.SemaphoreType.DMA((NX, NZ + 3)),
                pltpu.SemaphoreType.DMA((3,)),
                pltpu.SemaphoreType.DMA((NX,)),
            ],
        ),
        out_shape=[
            jax.ShapeDtypeStruct((NX, NZ, SLOTS, D), BF),
            jax.ShapeDtypeStruct((ROWS, HID), F32),
            jax.ShapeDtypeStruct((ROWS, HID), F32),
            jax.ShapeDtypeStruct((ROWS, HID), BF),
            jax.ShapeDtypeStruct((NX, SLOTS, LEFT), BF),
            jax.ShapeDtypeStruct((NZ - 1, NX, SLOTS, LEFT), BF),
            jax.ShapeDtypeStruct((NX, NZ, SLOTS, D - LEFT), BF),
        ],
        compiler_params=pltpu.CompilerParams(vmem_limit_bytes=60 * MIB),
        cost_estimate=pl.CostEstimate(flops=6 * ROWS * D * HID, bytes_accessed=20 * MIB, transcendentals=ROWS * HID),
        name="forward",
    )(where, *a_pieces, *b_pieces, w_gate, w_up, w_down)


def backward_kernel(where_ref, y_ref, note_ref, wd_ref, gate_ref, up_ref, hidden_ref, dg_ref, du_ref, spot_ref, sum_ref, y_rows):
    i = pl.program_id(0)
    at_x = where_ref[i]
    spots, notes = [], []
    for j in range(NZ):
        at_z = where_ref[NX + j]
        y_rows[j] = y_ref[at_z]
        note = note_ref[at_z].astype(F32)
        start = ((at_x * NZ + at_z) * 8).astype(F32)
        spots.append(jnp.where(note[:, :LANES] >= 0.0, note[:, :LANES] + start, -1.0))
        notes.append(note[:, LANES:])
    spot = jnp.concatenate(spots, axis=0)
    spot_ref[...] = spot[:, :1]
    notes = jnp.concatenate(notes, axis=0)
    xx = jnp.concatenate([notes[:, :SLOTS] + notes[:, SLOTS : 2 * SLOTS]] * NZ, axis=1)
    yy = jnp.concatenate([notes[:, 2 * SLOTS : 3 * SLOTS] + notes[:, 3 * SLOTS :]] * NZ, axis=1)
    back = dot(y_rows[...].reshape(TILE, D), wd_ref[0], ((1,), (1,)))
    gate, up, hidden = gate_ref[...], up_ref[...], hidden_ref[...]
    sig = jax.nn.sigmoid(gate)
    d_gate = (back * up * sig * (1.0 + gate * (1.0 - sig))).astype(BF)
    d_up = (back * (gate * sig)).astype(BF)
    dg_ref[...] = d_gate
    du_ref[...] = d_up
    last = ((1,), (1,))
    pair = xx * (dot(d_gate, d_gate, last) + dot(d_up, d_up, last)) + yy * dot(hidden, hidden, last)
    same = (spot[:, :1] == spot.T[:1, :]) & (spot[:, :1] >= 0.0)
    row_sums = jnp.sum(jnp.where(same, pair, 0.0), axis=1, keepdims=True)
    lane = lax.broadcasted_iota(jnp.int32, (TILE, LANES), 1).astype(F32)

    @pl.when(i == 0)
    def _():
        sum_ref[...] = jnp.zeros_like(sum_ref)

    for half in range(2):
        hot = spot == lane + half * LANES
        sum_ref[half : half + 1, :] += jnp.sum(jnp.where(hot, row_sums, 0.0), axis=0, keepdims=True)


def backward(where, wide_y, w_down, gate, up, hidden):
    def tall(n):
        return pl.BlockSpec((TILE, n), lambda i, where: (i, 0))

    return pl.pallas_call(
        backward_kernel,
        grid_spec=pltpu.PrefetchScalarGridSpec(
            num_scalar_prefetch=1,
            grid=(NX,),
            in_specs=[
                pl.BlockSpec((NZ, SLOTS, D), lambda i, where: (where[i], 0, 0)),
                pl.BlockSpec((NZ, SLOTS, 2 * LANES), lambda i, where: (where[i], 0, D // (2 * LANES))),
                pl.BlockSpec(w_down.shape, lambda i, where: (0, 0, 0), pipeline_mode=pl.Buffered(1)),
                tall(HID),
                tall(HID),
                tall(HID),
            ],
            out_specs=[tall(HID), tall(HID), tall(1), pl.BlockSpec((2, LANES), lambda i, where: (0, 0))],
            scratch_shapes=[pltpu.VMEM((NZ, SLOTS, D), BF)],
        ),
        out_shape=[
            jax.ShapeDtypeStruct((ROWS, HID), BF),
            jax.ShapeDtypeStruct((ROWS, HID), BF),
            jax.ShapeDtypeStruct((ROWS, 1), F32),
            jax.ShapeDtypeStruct((2, LANES), F32),
        ],
        compiler_params=pltpu.CompilerParams(vmem_limit_bytes=60 * MIB),
        cost_estimate=pl.CostEstimate(flops=3 * ROWS * D * HID, bytes_accessed=12 * MIB, transcendentals=ROWS * HID),
        name="backward",
    )(where, wide_y, wide_y, w_down, gate, up, hidden)


def factor_by_row(spot, factors):
    lane = lax.broadcasted_iota(jnp.int32, (ROWS, LANES), 1).astype(F32)
    factor = jnp.zeros((ROWS, 1), F32)
    for half in range(2):
        chosen = jnp.where(spot == lane + half * LANES, factors[half : half + 1, :], 0.0)
        factor = factor + jnp.sum(chosen, axis=1, keepdims=True)
    return factor


def wide_grads_kernel(x_ref, dg_ref, du_ref, spot_ref, factor_ref, gg_ref, gu_ref, scaled):
    @pl.when(pl.program_id(0) == 0)
    def _():
        factor = factor_by_row(spot_ref[...], factor_ref[...])
        scaled[:, :HID] = (factor * dg_ref[...].astype(F32)).astype(BF)
        scaled[:, HID:] = (factor * du_ref[...].astype(F32)).astype(BF)

    both = dot(x_ref[...].reshape(ROWS, COLS), scaled[...], ((0,), (0,))).astype(BF)
    gg_ref[0] = both[:, :HID]
    gu_ref[0] = both[:, HID:]


def wide_gradients(x, d_gate, d_up, spot, factors):
    def whole(a):
        return pl.BlockSpec(a.shape, lambda i: (0, 0), pipeline_mode=pl.Buffered(1))

    return pl.pallas_call(
        wide_grads_kernel,
        grid=(D // COLS,),
        in_specs=[
            pl.BlockSpec((NX, NZ, SLOTS, COLS), lambda i: (0, 0, 0, i)),
            whole(d_gate),
            whole(d_up),
            whole(spot),
            whole(factors),
        ],
        out_specs=[pl.BlockSpec((1, COLS, HID), lambda i: (0, i, 0))] * 2,
        out_shape=[jax.ShapeDtypeStruct((1, D, HID), BF)] * 2,
        scratch_shapes=[pltpu.VMEM((ROWS, 2 * HID), BF)],
        compiler_params=pltpu.CompilerParams(vmem_limit_bytes=60 * MIB),
        cost_estimate=pl.CostEstimate(flops=ROWS * D, bytes_accessed=MIB, transcendentals=0),
        name="wide_gradients",
    )(x, d_gate, d_up, spot, factors)


def down_grad_kernel(where_ref, y_ref, hidden_ref, spot_ref, factor_ref, gd_ref, turned, moved, by_row):
    @pl.when(pl.program_id(0) == 0)
    def _():
        factor = factor_by_row(spot_ref[...], factor_ref[...])
        for i in range(NX):
            for j in range(NZ):
                block = where_ref[i] * NZ + where_ref[NX + j]
                first = (i * NZ + j) * SLOTS
                moved[block] = hidden_ref[first : first + SLOTS]
                by_row[block] = factor[first : first + SLOTS]
        turned[...] = moved[...].reshape(ROWS, HID).T

    cot = (by_row[...] * y_ref[...].astype(F32)).astype(BF).reshape(ROWS, COLS)
    gd_ref[0] = dot(turned[...], cot, ((1,), (0,))).astype(BF)


def down_gradient(where, wide_y, hidden, spot, factors):
    def whole(a):
        return pl.BlockSpec(a.shape, lambda i, where: (0, 0), pipeline_mode=pl.Buffered(1))

    return pl.pallas_call(
        down_grad_kernel,
        grid_spec=pltpu.PrefetchScalarGridSpec(
            num_scalar_prefetch=1,
            grid=(D // COLS,),
            in_specs=[
                pl.BlockSpec((BLOCKS, SLOTS, COLS), lambda i, where: (0, 0, i)),
                whole(hidden),
                whole(spot),
                whole(factors),
            ],
            out_specs=pl.BlockSpec((1, HID, COLS), lambda i, where: (0, 0, i)),
            scratch_shapes=[
                pltpu.VMEM((HID, ROWS), BF),
                pltpu.VMEM((BLOCKS, SLOTS, HID), BF),
                pltpu.VMEM((BLOCKS, SLOTS, 1), F32),
            ],
        ),
        out_shape=jax.ShapeDtypeStruct((1, HID, D), BF),
        compiler_params=pltpu.CompilerParams(vmem_limit_bytes=60 * MIB),
        cost_estimate=pl.CostEstimate(flops=ROWS * D, bytes_accessed=MIB, transcendentals=0),
        name="down_gradient",
    )(where, wide_y, hidden, spot, factors)


def on_device(tokens, cotangent, routes, example_ids, w_gate, w_up, w_down):
    ix, iz = lax.axis_index("x"), lax.axis_index("z")
    where = jnp.concatenate([(ix + jnp.array(ORDER["x"])) % NX, (iz + jnp.array(ORDER["z"])) % NZ]).astype(jnp.int32)
    tok_count, width = tokens.shape
    flat_routes = routes.reshape(-1)
    owner_hot = (flat_routes[:, None] == jnp.arange(NE)[None, :]).astype(jnp.int32)
    before = jnp.cumsum(owner_hot, axis=0) - owner_hot
    slot_of = flat_routes * CAP + jnp.sum(before * owner_hot, axis=1)
    placed = (jnp.arange(SLOTS)[:, None] == slot_of[None, :]).astype(jnp.int32)
    placed = jnp.sum(placed.reshape(SLOTS, tok_count, 2), axis=2)
    placed_bf = placed.astype(BF)
    filled = jnp.sum(placed, axis=1) > 0
    send_ids = jnp.where(filled, jnp.sum(placed * example_ids.reshape(-1)[None, :], axis=1), -1)
    send_x = jnp.dot(placed_bf, tokens, preferred_element_type=F32).astype(BF)
    send_dy = jnp.dot(placed_bf, cotangent, preferred_element_type=F32).astype(BF)
    id_cols = jnp.broadcast_to(send_ids.astype(BF)[:, None], (SLOTS, LANES))
    send = jnp.concatenate(
        [
            jnp.concatenate([send_x, id_cols], axis=1).reshape(NE, CAP, width + LANES),
            jnp.concatenate([send_dy, id_cols], axis=1).reshape(NE, CAP, width + LANES),
        ],
        axis=1,
    )
    got = lax.all_to_all(send, EXPERT, split_axis=0, concat_axis=0, tiled=True)
    local_x = got[:, :CAP, :width].reshape(SLOTS, width)
    local_dy = got[:, CAP:].reshape(SLOTS, width + LANES)
    last = ((1,), (1,))
    parts = []
    for rows in (local_x, local_dy[:, :width]):
        gram = dot(rows, rows, last)
        high = lax.reduce_precision(gram, 8, 7)
        parts += [high.astype(BF), (gram - high).astype(BF)]
    wide_y = lax.all_gather(jnp.concatenate([local_dy] + parts, axis=1), ("x", "z"), axis=0)
    line_x = jnp.stack(ring_gather(local_x[:MID], "x", False))
    line_z = jnp.stack(ring_gather(local_x[MID:], "z", False))
    a_pieces = ring_gather(line_x, "z", True)
    b_pieces = ring_gather(line_z, "x", True)
    x, gate, up_part, hidden, far, left, right = forward(
        where, a_pieces, b_pieces, w_gate, w_up, w_down
    )
    right, wide_y = lax.optimization_barrier((right, wide_y))
    right_line = lax.psum_scatter(right.reshape(ROWS, D - LEFT), "x", scatter_dimension=0, tiled=True)
    kept = {}

    def hook(step, sent, going):
        if step == 1:
            kept["back"] = backward(where, wide_y, w_down, gate, up_part, hidden)
            sent, kept["sum"] = lax.optimization_barrier((sent, kept["back"][3]))
        elif step == 2:
            total, _ = lax.optimization_barrier((kept["sum"], going))
            total = jnp.sum(spread(total, ("x", "z"), BLOCKS).reshape(BLOCKS, 2, LANES), axis=0)
            total = jnp.sum(spread(total, EXPERT, NE).reshape(NE, 2, LANES), axis=0)
            sent, total, line = lax.optimization_barrier((sent, total, right_line))
            kept["line"] = lax.psum_scatter(line, "z", scatter_dimension=0, tiled=True)
            kept["norms"] = jnp.sqrt(total)
            kept["factors"] = RADIUS / (kept["norms"] + GAMMA)
        elif step == 3:
            factors, _ = lax.optimization_barrier((kept["factors"], going))
            grad = down_gradient(where, wide_y, hidden, kept["back"][2], factors)
            sent, kept["down"] = lax.optimization_barrier((sent, grad))
        else:
            d_gate, d_up, spot, _ = kept["back"]
            factors, _ = lax.optimization_barrier((kept["factors"], going))
            grads = wide_gradients(x, d_gate, d_up, spot, factors)
            sent, kept["grads"] = lax.optimization_barrier((sent, tuple(grads)))
        return sent

    left_line = ring_sum(far, left, "z", hook)
    right_out = kept["line"]
    left_out = direct_sum(left_line, "x")
    own_out = jnp.concatenate([left_out, right_out], axis=1)
    returned = lax.all_to_all(own_out.reshape(NE, CAP, width), EXPERT, split_axis=0, concat_axis=0, tiled=True)
    mixed = jnp.dot(placed_bf.T, returned.reshape(SLOTS, width), preferred_element_type=F32).astype(BF)
    norms = kept["norms"]
    own_norms = lax.dynamic_slice(norms.reshape(BLOCKS, 8), (ix * NZ + iz, 0), (1, EX_ROW))
    return (mixed, own_norms, *kept["grads"], kept["down"])


def solution(mesh):
    mesh = Mesh(mesh.devices.reshape(NX, NZ, 4, 2), ("x", "z", "y", "c"))
    data, every = ("x", "z"), ("x", "z", "y", "c")
    return jax.shard_map(
        on_device,
        mesh=mesh,
        in_specs=(
            P(every, None),
            P(every, None),
            P(every, None),
            P(data, EXPERT),
            P(EXPERT, None, data),
            P(EXPERT, None, data),
            P(EXPERT, data, None),
        ),
        out_specs=(
            P(every, None),
            P(data, None),
            P(EXPERT, None, data),
            P(EXPERT, None, data),
            P(EXPERT, data, None),
        ),
        check_vma=False,
    )
```

```python
import math

import jax
import jax.numpy as jnp
from jax import lax
from jax.experimental import pallas as pl
from jax.experimental.pallas import tpu as pltpu
from jax.sharding import Mesh, PartitionSpec as P

D = 3072
FF = 8192
CAP = 4
EX_ROW = 6
NX, NZ, NE = 4, 8, 8
BLOCKS = NX * NZ
SLOTS = NE * CAP
ROWS = BLOCKS * SLOTS
HID = FF // BLOCKS
SIZE = {"x": NX, "z": NZ}
ORDER = {"x": (0, -1, 1, 2), "z": (0, -1, 1, -2, 2, -3, 3, 4)}
GAMMA = 0.01
RADIUS = math.sqrt(3.0 * D * FF * NE / (BLOCKS * EX_ROW))
EXPERT = ("y", "c")
BF = jnp.bfloat16
F32 = jnp.float32
MIB = 1 << 20
LANES = 128
TILE = NZ * SLOTS
MID = SLOTS // 2
COLS = 512
LEFT = 1792


def shift(a, axis, step):
    n = SIZE[axis]
    return lax.ppermute(a, axis, [(i, (i + step) % n) for i in range(n)])


def ring_gather(a, axis, split):
    half = SIZE[axis] // 2
    mid = a.shape[-2] // 2
    pieces = [a]
    up = down = a
    for _ in range(1, half):
        up, down = shift(up, axis, 1), shift(down, axis, -1)
        pieces += [up, down]
    if split:
        return pieces + [shift(up[..., :mid, :], axis, 1), shift(down[..., mid:, :], axis, -1)]
    return pieces + [shift(up, axis, 1)]


def plus(a, b):
    return (a.astype(F32) + b.astype(F32)).astype(BF)


def ring_sum(far, parts, axis, hook):
    half = SIZE[axis] // 2
    place = ORDER[axis].index

    def get(k):
        return parts[place(k)]

    own_up, down = hook(1, (get(half - 1), get(1 - half)), far)
    up = plus(shift(far, axis, 1), own_up)
    for k in range(half - 1, 0, -1):
        going = up
        up, down = shift(up, axis, 1), shift(down, axis, -1)
        if k > 1:
            own_up, own_down = hook(half - k + 1, (get(k - 1), get(1 - k)), going)
            up, down = plus(up, own_up), plus(down, own_down)
    own = hook(half, get(0), going)
    return (up.astype(F32) + down.astype(F32) + own.astype(F32)).astype(BF)


def direct_sum(parts, axis):
    total = parts[0].astype(F32)
    for place, k in enumerate(ORDER[axis]):
        if k:
            total = total + shift(parts[place], axis, k).astype(F32)
    return total.astype(BF)


def spread(a, axes, n):
    return lax.all_to_all(jnp.broadcast_to(a[None], (n,) + a.shape), axes, 0, 0, tiled=True)


def dot(a, b, dims):
    return lax.dot_general(a, b, (dims, ((), ())), preferred_element_type=F32)


def forward_kernel(where_ref, *refs):
    a_refs, refs = refs[: NZ + 1], refs[NZ + 1 :]
    b_refs, refs = refs[: NX + 1], refs[NX + 1 :]
    wg_ref, wu_ref, wd_ref, x_out, gate_ref, up_ref, hidden_ref, far_ref, left_ref, right_ref, rows_ref, wg, wu, wd, in_sems, w_sems, out_sems = refs
    step = pl.program_id(0)
    quarter = MID // 2
    arrivals = []
    for i in range(NX):
        moves = [(a_refs[j].at[i], rows_ref.at[i, j, pl.ds(0, MID)]) for j in range(NZ - 1)]
        moves += [(a_refs[NZ - 1 + h].at[i], rows_ref.at[i, NZ - 1, pl.ds(h * quarter, quarter)]) for h in range(2)]
        if i < NX - 1:
            moves += [(b_refs[i], rows_ref.at[i, :, pl.ds(MID, MID)])]
        else:
            moves += [(b_refs[i + h], rows_ref.at[i, :, pl.ds(MID + h * quarter, quarter)]) for h in range(2)]
        arrivals.append([pltpu.make_async_copy(s, d, in_sems.at[i, n]) for n, (s, d) in enumerate(moves)])
    leaving = [pltpu.make_async_copy(rows_ref.at[i], x_out.at[i], out_sems.at[i]) for i in range(NX)]

    weights = [
        pltpu.make_async_copy(s.at[0], d, w_sems.at[n]) for n, (s, d) in enumerate([(wg_ref, wg), (wu_ref, wu), (wd_ref, wd)])
    ]

    @pl.when(step == 0)
    def _():
        for copy in arrivals[0] + weights[:2] + arrivals[1] + weights[2:] + arrivals[2] + arrivals[3]:
            copy.start()
        for copy in weights[:2]:
            copy.wait()

    for i in range(NX):

        @pl.when(step == i)
        def _():
            for copy in arrivals[i]:
                copy.wait()
            leaving[i].start()

    x = rows_ref[step].reshape(TILE, D)
    gate = dot(x, wg[...], ((1,), (0,)))
    up = dot(x, wu[...], ((1,), (0,)))
    hidden = (gate * jax.nn.sigmoid(gate) * up).astype(BF)
    gate_ref[...] = gate
    up_ref[...] = up
    hidden_ref[...] = hidden

    @pl.when(step == 0)
    def _():
        weights[2].wait()

    out = dot(hidden, wd[:, :LEFT], ((1,), (0,))).astype(BF)
    left_ref[...] = out[: TILE - SLOTS].reshape(NZ - 1, 1, SLOTS, LEFT)
    far_ref[0] = out[TILE - SLOTS :]
    out = dot(hidden, wd[:, LEFT:], ((1,), (0,))).astype(BF)
    for j in range(NZ):
        right_ref[0, where_ref[NX + j]] = out[j * SLOTS : (j + 1) * SLOTS]

    @pl.when(step == NX - 1)
    def _():
        for copy in leaving:
            copy.wait()


def forward(where, a_pieces, b_pieces, w_gate, w_up, w_down):
    outside = pl.BlockSpec(memory_space=pltpu.HBM)

    def tall(n):
        return pl.BlockSpec((TILE, n), lambda i, where: (i, 0))

    return pl.pallas_call(
        forward_kernel,
        grid_spec=pltpu.PrefetchScalarGridSpec(
            num_scalar_prefetch=1,
            grid=(NX,),
            in_specs=[outside] * (NZ + NX + 5),
            out_specs=[
                outside,
                tall(HID),
                tall(HID),
                tall(HID),
                pl.BlockSpec((1, SLOTS, LEFT), lambda i, where: (i, 0, 0)),
                pl.BlockSpec((NZ - 1, 1, SLOTS, LEFT), lambda i, where: (0, i, 0, 0)),
                pl.BlockSpec((1, NZ, SLOTS, D - LEFT), lambda i, where: (where[i], 0, 0, 0)),
            ],
            scratch_shapes=[
                pltpu.VMEM((NX, NZ, SLOTS, D), BF),
                pltpu.VMEM((D, HID), BF),
                pltpu.VMEM((D, HID), BF),
                pltpu.VMEM((HID, D), BF),
                pltpu.SemaphoreType.DMA((NX, NZ + 3)),
                pltpu.SemaphoreType.DMA((3,)),
                pltpu.SemaphoreType.DMA((NX,)),
            ],
        ),
        out_shape=[
            jax.ShapeDtypeStruct((NX, NZ, SLOTS, D), BF),
            jax.ShapeDtypeStruct((ROWS, HID), F32),
            jax.ShapeDtypeStruct((ROWS, HID), F32),
            jax.ShapeDtypeStruct((ROWS, HID), BF),
            jax.ShapeDtypeStruct((NX, SLOTS, LEFT), BF),
            jax.ShapeDtypeStruct((NZ - 1, NX, SLOTS, LEFT), BF),
            jax.ShapeDtypeStruct((NX, NZ, SLOTS, D - LEFT), BF),
        ],
        compiler_params=pltpu.CompilerParams(vmem_limit_bytes=60 * MIB),
        cost_estimate=pl.CostEstimate(flops=6 * ROWS * D * HID, bytes_accessed=20 * MIB, transcendentals=ROWS * HID),
        name="forward",
    )(where, *a_pieces, *b_pieces, w_gate, w_up, w_down)


def backward_kernel(where_ref, y_ref, note_ref, wd_ref, gate_ref, up_ref, hidden_ref, dg_ref, du_ref, spot_ref, sum_ref, y_rows):
    i = pl.program_id(0)
    at_x = where_ref[i]
    spots, notes = [], []
    for j in range(NZ):
        at_z = where_ref[NX + j]
        y_rows[j] = y_ref[at_z]
        note = note_ref[at_z].astype(F32)
        start = ((at_x * NZ + at_z) * 8).astype(F32)
        spots.append(jnp.where(note[:, :LANES] >= 0.0, note[:, :LANES] + start, -1.0))
        notes.append(note[:, LANES:])
    spot = jnp.concatenate(spots, axis=0)
    spot_ref[...] = spot[:, :1]
    notes = jnp.concatenate(notes, axis=0)
    xx = jnp.concatenate([notes[:, :SLOTS] + notes[:, SLOTS : 2 * SLOTS]] * NZ, axis=1)
    yy = jnp.concatenate([notes[:, 2 * SLOTS : 3 * SLOTS] + notes[:, 3 * SLOTS :]] * NZ, axis=1)
    back = dot(y_rows[...].reshape(TILE, D), wd_ref[0], ((1,), (1,)))
    gate, up, hidden = gate_ref[...], up_ref[...], hidden_ref[...]
    sig = jax.nn.sigmoid(gate)
    d_gate = (back * up * sig * (1.0 + gate * (1.0 - sig))).astype(BF)
    d_up = (back * (gate * sig)).astype(BF)
    dg_ref[...] = d_gate
    du_ref[...] = d_up
    last = ((1,), (1,))
    pair = xx * (dot(d_gate, d_gate, last) + dot(d_up, d_up, last)) + yy * dot(hidden, hidden, last)
    same = (spot[:, :1] == spot.T[:1, :]) & (spot[:, :1] >= 0.0)
    row_sums = jnp.sum(jnp.where(same, pair, 0.0), axis=1, keepdims=True)
    lane = lax.broadcasted_iota(jnp.int32, (TILE, LANES), 1).astype(F32)

    @pl.when(i == 0)
    def _():
        sum_ref[...] = jnp.zeros_like(sum_ref)

    for half in range(2):
        hot = spot == lane + half * LANES
        sum_ref[half : half + 1, :] += jnp.sum(jnp.where(hot, row_sums, 0.0), axis=0, keepdims=True)


def backward(where, wide_y, w_down, gate, up, hidden):
    def tall(n):
        return pl.BlockSpec((TILE, n), lambda i, where: (i, 0))

    return pl.pallas_call(
        backward_kernel,
        grid_spec=pltpu.PrefetchScalarGridSpec(
            num_scalar_prefetch=1,
            grid=(NX,),
            in_specs=[
                pl.BlockSpec((NZ, SLOTS, D), lambda i, where: (where[i], 0, 0)),
                pl.BlockSpec((NZ, SLOTS, 2 * LANES), lambda i, where: (where[i], 0, D // (2 * LANES))),
                pl.BlockSpec(w_down.shape, lambda i, where: (0, 0, 0), pipeline_mode=pl.Buffered(1)),
                tall(HID),
                tall(HID),
                tall(HID),
            ],
            out_specs=[tall(HID), tall(HID), tall(1), pl.BlockSpec((2, LANES), lambda i, where: (0, 0))],
            scratch_shapes=[pltpu.VMEM((NZ, SLOTS, D), BF)],
        ),
        out_shape=[
            jax.ShapeDtypeStruct((ROWS, HID), BF),
            jax.ShapeDtypeStruct((ROWS, HID), BF),
            jax.ShapeDtypeStruct((ROWS, 1), F32),
            jax.ShapeDtypeStruct((2, LANES), F32),
        ],
        compiler_params=pltpu.CompilerParams(vmem_limit_bytes=60 * MIB),
        cost_estimate=pl.CostEstimate(flops=3 * ROWS * D * HID, bytes_accessed=12 * MIB, transcendentals=ROWS * HID),
        name="backward",
    )(where, wide_y, wide_y, w_down, gate, up, hidden)


def factor_by_row(spot, factors):
    lane = lax.broadcasted_iota(jnp.int32, (ROWS, LANES), 1).astype(F32)
    factor = jnp.zeros((ROWS, 1), F32)
    for half in range(2):
        chosen = jnp.where(spot == lane + half * LANES, factors[half : half + 1, :], 0.0)
        factor = factor + jnp.sum(chosen, axis=1, keepdims=True)
    return factor


def wide_grads_kernel(x_ref, dg_ref, du_ref, spot_ref, factor_ref, gg_ref, gu_ref, scaled):
    @pl.when(pl.program_id(0) == 0)
    def _():
        factor = factor_by_row(spot_ref[...], factor_ref[...])
        scaled[:, :HID] = (factor * dg_ref[...].astype(F32)).astype(BF)
        scaled[:, HID:] = (factor * du_ref[...].astype(F32)).astype(BF)

    both = dot(x_ref[...].reshape(ROWS, COLS), scaled[...], ((0,), (0,))).astype(BF)
    gg_ref[0] = both[:, :HID]
    gu_ref[0] = both[:, HID:]


def wide_gradients(x, d_gate, d_up, spot, factors):
    def whole(a):
        return pl.BlockSpec(a.shape, lambda i: (0, 0), pipeline_mode=pl.Buffered(1))

    return pl.pallas_call(
        wide_grads_kernel,
        grid=(D // COLS,),
        in_specs=[
            pl.BlockSpec((NX, NZ, SLOTS, COLS), lambda i: (0, 0, 0, i)),
            whole(d_gate),
            whole(d_up),
            whole(spot),
            whole(factors),
        ],
        out_specs=[pl.BlockSpec((1, COLS, HID), lambda i: (0, i, 0))] * 2,
        out_shape=[jax.ShapeDtypeStruct((1, D, HID), BF)] * 2,
        scratch_shapes=[pltpu.VMEM((ROWS, 2 * HID), BF)],
        compiler_params=pltpu.CompilerParams(vmem_limit_bytes=60 * MIB),
        cost_estimate=pl.CostEstimate(flops=ROWS * D, bytes_accessed=MIB, transcendentals=0),
        name="wide_gradients",
    )(x, d_gate, d_up, spot, factors)


def down_grad_kernel(where_ref, y_ref, hidden_ref, spot_ref, factor_ref, gd_ref, turned, moved, by_row):
    @pl.when(pl.program_id(0) == 0)
    def _():
        factor = factor_by_row(spot_ref[...], factor_ref[...])
        for i in range(NX):
            for j in range(NZ):
                block = where_ref[i] * NZ + where_ref[NX + j]
                first = (i * NZ + j) * SLOTS
                moved[block] = hidden_ref[first : first + SLOTS]
                by_row[block] = factor[first : first + SLOTS]
        turned[...] = moved[...].reshape(ROWS, HID).T

    cot = (by_row[...] * y_ref[...].astype(F32)).astype(BF).reshape(ROWS, COLS)
    gd_ref[0] = dot(turned[...], cot, ((1,), (0,))).astype(BF)


def down_gradient(where, wide_y, hidden, spot, factors):
    def whole(a):
        return pl.BlockSpec(a.shape, lambda i, where: (0, 0), pipeline_mode=pl.Buffered(1))

    return pl.pallas_call(
        down_grad_kernel,
        grid_spec=pltpu.PrefetchScalarGridSpec(
            num_scalar_prefetch=1,
            grid=(D // COLS,),
            in_specs=[
                pl.BlockSpec((BLOCKS, SLOTS, COLS), lambda i, where: (0, 0, i)),
                whole(hidden),
                whole(spot),
                whole(factors),
            ],
            out_specs=pl.BlockSpec((1, HID, COLS), lambda i, where: (0, 0, i)),
            scratch_shapes=[
                pltpu.VMEM((HID, ROWS), BF),
                pltpu.VMEM((BLOCKS, SLOTS, HID), BF),
                pltpu.VMEM((BLOCKS, SLOTS, 1), F32),
            ],
        ),
        out_shape=jax.ShapeDtypeStruct((1, HID, D), BF),
        compiler_params=pltpu.CompilerParams(vmem_limit_bytes=60 * MIB),
        cost_estimate=pl.CostEstimate(flops=ROWS * D, bytes_accessed=MIB, transcendentals=0),
        name="down_gradient",
    )(where, wide_y, hidden, spot, factors)


def on_device(tokens, cotangent, routes, example_ids, w_gate, w_up, w_down):
    ix, iz = lax.axis_index("x"), lax.axis_index("z")
    where = jnp.concatenate([(ix + jnp.array(ORDER["x"])) % NX, (iz + jnp.array(ORDER["z"])) % NZ]).astype(jnp.int32)
    tok_count, width = tokens.shape
    flat_routes = routes.reshape(-1)
    owner_hot = (flat_routes[:, None] == jnp.arange(NE)[None, :]).astype(jnp.int32)
    before = jnp.cumsum(owner_hot, axis=0) - owner_hot
    slot_of = flat_routes * CAP + jnp.sum(before * owner_hot, axis=1)
    placed = (jnp.arange(SLOTS)[:, None] == slot_of[None, :]).astype(jnp.int32)
    placed = jnp.sum(placed.reshape(SLOTS, tok_count, 2), axis=2)
    placed_bf = placed.astype(BF)
    filled = jnp.sum(placed, axis=1) > 0
    send_ids = jnp.where(filled, jnp.sum(placed * example_ids.reshape(-1)[None, :], axis=1), -1)
    send_x = jnp.dot(placed_bf, tokens, preferred_element_type=F32).astype(BF)
    send_dy = jnp.dot(placed_bf, cotangent, preferred_element_type=F32).astype(BF)
    id_cols = jnp.broadcast_to(send_ids.astype(BF)[:, None], (SLOTS, LANES))
    send = jnp.concatenate(
        [
            jnp.concatenate([send_x, id_cols], axis=1).reshape(NE, CAP, width + LANES),
            jnp.concatenate([send_dy, id_cols], axis=1).reshape(NE, CAP, width + LANES),
        ],
        axis=1,
    )
    got = lax.all_to_all(send, EXPERT, split_axis=0, concat_axis=0, tiled=True)
    local_x = got[:, :CAP, :width].reshape(SLOTS, width)
    local_dy = got[:, CAP:].reshape(SLOTS, width + LANES)
    last = ((1,), (1,))
    parts = []
    for rows in (local_x, local_dy[:, :width]):
        gram = dot(rows, rows, last)
        high = lax.reduce_precision(gram, 8, 7)
        parts += [high.astype(BF), (gram - high).astype(BF)]
    wide_y = lax.all_gather(jnp.concatenate([local_dy] + parts, axis=1), ("x", "z"), axis=0)
    line_x = jnp.stack(ring_gather(local_x[:MID], "x", False))
    line_z = jnp.stack(ring_gather(local_x[MID:], "z", False))
    a_pieces = ring_gather(line_x, "z", True)
    b_pieces = ring_gather(line_z, "x", True)
    x, gate, up_part, hidden, far, left, right = forward(
        where, a_pieces, b_pieces, w_gate, w_up, w_down
    )
    right, wide_y = lax.optimization_barrier((right, wide_y))
    right_line = lax.psum_scatter(right.reshape(ROWS, D - LEFT), "x", scatter_dimension=0, tiled=True)
    kept = {}

    def hook(step, sent, going):
        if step == 1:
            kept["back"] = backward(where, wide_y, w_down, gate, up_part, hidden)
            sent, kept["sum"] = lax.optimization_barrier((sent, kept["back"][3]))
        elif step == 2:
            total, _ = lax.optimization_barrier((kept["sum"], going))
            total = jnp.sum(spread(total, ("x", "z"), BLOCKS).reshape(BLOCKS, 2, LANES), axis=0)
            sent, kept["sum"], line = lax.optimization_barrier((sent, total, right_line))
            kept["line"] = lax.psum_scatter(line, "z", scatter_dimension=0, tiled=True)
        elif step == 3:
            total, _ = lax.optimization_barrier((kept["sum"], going))
            total = jnp.sum(spread(total, EXPERT, NE).reshape(NE, 2, LANES), axis=0)
            sent, total = lax.optimization_barrier((sent, total))
            kept["norms"] = jnp.sqrt(total)
            kept["factors"] = RADIUS / (kept["norms"] + GAMMA)
        else:
            d_gate, d_up, spot, _ = kept["back"]
            factors, _ = lax.optimization_barrier((kept["factors"], going))
            grads = wide_gradients(x, d_gate, d_up, spot, factors)
            sent, kept["grads"], kept["line"] = lax.optimization_barrier((sent, tuple(grads), kept["line"]))
        return sent

    left_line = ring_sum(far, left, "z", hook)
    right_out = kept["line"]
    left_out = direct_sum(left_line, "x")
    own_out = jnp.concatenate([left_out, right_out], axis=1)
    own_out, late = lax.optimization_barrier((own_out, hidden))
    grad_down = down_gradient(where, wide_y, late, kept["back"][2], kept["factors"])
    returned = lax.all_to_all(own_out.reshape(NE, CAP, width), EXPERT, split_axis=0, concat_axis=0, tiled=True)
    mixed = jnp.dot(placed_bf.T, returned.reshape(SLOTS, width), preferred_element_type=F32).astype(BF)
    norms = kept["norms"]
    own_norms = lax.dynamic_slice(norms.reshape(BLOCKS, 8), (ix * NZ + iz, 0), (1, EX_ROW))
    return (mixed, own_norms, *kept["grads"], grad_down)


def solution(mesh):
    mesh = Mesh(mesh.devices.reshape(NX, NZ, 4, 2), ("x", "z", "y", "c"))
    data, every = ("x", "z"), ("x", "z", "y", "c")
    return jax.shard_map(
        on_device,
        mesh=mesh,
        in_specs=(
            P(every, None),
            P(every, None),
            P(every, None),
            P(data, EXPERT),
            P(EXPERT, None, data),
            P(EXPERT, None, data),
            P(EXPERT, data, None),
        ),
        out_specs=(
            P(every, None),
            P(data, None),
            P(EXPERT, None, data),
            P(EXPERT, None, data),
            P(EXPERT, data, None),
        ),
        check_vma=False,
    )
```

```python
import math

import jax
import jax.numpy as jnp
from jax import lax
from jax.experimental import pallas as pl
from jax.experimental.pallas import tpu as pltpu
from jax.sharding import Mesh, PartitionSpec as P

D = 3072
FF = 8192
CAP = 4
EX_ROW = 6
NX, NZ, NE = 4, 8, 8
BLOCKS = NX * NZ
SLOTS = NE * CAP
ROWS = BLOCKS * SLOTS
HID = FF // BLOCKS
SIZE = {"x": NX, "z": NZ}
ORDER = {"x": (0, -1, 1, 2), "z": (0, -1, 1, -2, 2, -3, 3, 4)}
GAMMA = 0.01
RADIUS = math.sqrt(3.0 * D * FF * NE / (BLOCKS * EX_ROW))
EXPERT = ("y", "c")
BF = jnp.bfloat16
F32 = jnp.float32
MIB = 1 << 20
LANES = 128
TILE = NZ * SLOTS
MID = SLOTS // 2
COLS = 512
LEFT = 2304


def shift(a, axis, step):
    n = SIZE[axis]
    return lax.ppermute(a, axis, [(i, (i + step) % n) for i in range(n)])


def ring_gather(a, axis, split):
    half = SIZE[axis] // 2
    mid = a.shape[-2] // 2
    pieces = [a]
    up = down = a
    for _ in range(1, half):
        up, down = shift(up, axis, 1), shift(down, axis, -1)
        pieces += [up, down]
    if split:
        return pieces + [shift(up[..., :mid, :], axis, 1), shift(down[..., mid:, :], axis, -1)]
    return pieces + [shift(up, axis, 1)]


def plus(a, b):
    return (a.astype(F32) + b.astype(F32)).astype(BF)


def ring_sum(far, parts, axis, hook):
    half = SIZE[axis] // 2
    place = ORDER[axis].index

    def get(k):
        return parts[place(k)]

    own_up, down = hook(1, (get(half - 1), get(1 - half)), far)
    up = plus(shift(far, axis, 1), own_up)
    for k in range(half - 1, 0, -1):
        going = up
        up, down = shift(up, axis, 1), shift(down, axis, -1)
        if k > 1:
            own_up, own_down = hook(half - k + 1, (get(k - 1), get(1 - k)), going)
            up, down = plus(up, own_up), plus(down, own_down)
    own = hook(half, get(0), going)
    return (up.astype(F32) + down.astype(F32) + own.astype(F32)).astype(BF)


def direct_sum(parts, axis):
    total = parts[0].astype(F32)
    for place, k in enumerate(ORDER[axis]):
        if k:
            total = total + shift(parts[place], axis, k).astype(F32)
    return total.astype(BF)


def spread(a, axes, n):
    return lax.all_to_all(jnp.broadcast_to(a[None], (n,) + a.shape), axes, 0, 0, tiled=True)


def dot(a, b, dims):
    return lax.dot_general(a, b, (dims, ((), ())), preferred_element_type=F32)


def forward_kernel(where_ref, *refs):
    a_refs, refs = refs[: NZ + 1], refs[NZ + 1 :]
    b_refs, refs = refs[: NX + 1], refs[NX + 1 :]
    wg_ref, wu_ref, wd_ref, x_out, gate_ref, up_ref, hidden_ref, far_ref, left_ref, right_ref, rows_ref, wg, wu, wd, in_sems, w_sems, out_sems = refs
    step = pl.program_id(0)
    quarter = MID // 2
    arrivals = []
    for i in range(NX):
        moves = [(a_refs[j].at[i], rows_ref.at[i, j, pl.ds(0, MID)]) for j in range(NZ - 1)]
        moves += [(a_refs[NZ - 1 + h].at[i], rows_ref.at[i, NZ - 1, pl.ds(h * quarter, quarter)]) for h in range(2)]
        if i < NX - 1:
            moves += [(b_refs[i], rows_ref.at[i, :, pl.ds(MID, MID)])]
        else:
            moves += [(b_refs[i + h], rows_ref.at[i, :, pl.ds(MID + h * quarter, quarter)]) for h in range(2)]
        arrivals.append([pltpu.make_async_copy(s, d, in_sems.at[i, n]) for n, (s, d) in enumerate(moves)])
    leaving = [pltpu.make_async_copy(rows_ref.at[i], x_out.at[i], out_sems.at[i]) for i in range(NX)]

    weights = [
        pltpu.make_async_copy(s.at[0], d, w_sems.at[n]) for n, (s, d) in enumerate([(wg_ref, wg), (wu_ref, wu), (wd_ref, wd)])
    ]

    @pl.when(step == 0)
    def _():
        for copy in arrivals[0] + weights[:2] + arrivals[1] + weights[2:] + arrivals[2] + arrivals[3]:
            copy.start()
        for copy in weights[:2]:
            copy.wait()

    for i in range(NX):

        @pl.when(step == i)
        def _():
            for copy in arrivals[i]:
                copy.wait()
            leaving[i].start()

    x = rows_ref[step].reshape(TILE, D)
    gate = dot(x, wg[...], ((1,), (0,)))
    up = dot(x, wu[...], ((1,), (0,)))
    hidden = (gate * jax.nn.sigmoid(gate) * up).astype(BF)
    gate_ref[...] = gate
    up_ref[...] = up
    hidden_ref[...] = hidden

    @pl.when(step == 0)
    def _():
        weights[2].wait()

    out = dot(hidden, wd[:, :LEFT], ((1,), (0,))).astype(BF)
    left_ref[...] = out[: TILE - SLOTS].reshape(NZ - 1, 1, SLOTS, LEFT)
    far_ref[0] = out[TILE - SLOTS :]
    out = dot(hidden, wd[:, LEFT:], ((1,), (0,))).astype(BF)
    for j in range(NZ):
        right_ref[0, where_ref[NX + j]] = out[j * SLOTS : (j + 1) * SLOTS]

    @pl.when(step == NX - 1)
    def _():
        for copy in leaving:
            copy.wait()


def forward(where, a_pieces, b_pieces, w_gate, w_up, w_down):
    outside = pl.BlockSpec(memory_space=pltpu.HBM)

    def tall(n):
        return pl.BlockSpec((TILE, n), lambda i, where: (i, 0))

    return pl.pallas_call(
        forward_kernel,
        grid_spec=pltpu.PrefetchScalarGridSpec(
            num_scalar_prefetch=1,
            grid=(NX,),
            in_specs=[outside] * (NZ + NX + 5),
            out_specs=[
                outside,
                tall(HID),
                tall(HID),
                tall(HID),
                pl.BlockSpec((1, SLOTS, LEFT), lambda i, where: (i, 0, 0)),
                pl.BlockSpec((NZ - 1, 1, SLOTS, LEFT), lambda i, where: (0, i, 0, 0)),
                pl.BlockSpec((1, NZ, SLOTS, D - LEFT), lambda i, where: (where[i], 0, 0, 0)),
            ],
            scratch_shapes=[
                pltpu.VMEM((NX, NZ, SLOTS, D), BF),
                pltpu.VMEM((D, HID), BF),
                pltpu.VMEM((D, HID), BF),
                pltpu.VMEM((HID, D), BF),
                pltpu.SemaphoreType.DMA((NX, NZ + 3)),
                pltpu.SemaphoreType.DMA((3,)),
                pltpu.SemaphoreType.DMA((NX,)),
            ],
        ),
        out_shape=[
            jax.ShapeDtypeStruct((NX, NZ, SLOTS, D), BF),
            jax.ShapeDtypeStruct((ROWS, HID), F32),
            jax.ShapeDtypeStruct((ROWS, HID), F32),
            jax.ShapeDtypeStruct((ROWS, HID), BF),
            jax.ShapeDtypeStruct((NX, SLOTS, LEFT), BF),
            jax.ShapeDtypeStruct((NZ - 1, NX, SLOTS, LEFT), BF),
            jax.ShapeDtypeStruct((NX, NZ, SLOTS, D - LEFT), BF),
        ],
        compiler_params=pltpu.CompilerParams(vmem_limit_bytes=60 * MIB),
        cost_estimate=pl.CostEstimate(flops=6 * ROWS * D * HID, bytes_accessed=20 * MIB, transcendentals=ROWS * HID),
        name="forward",
    )(where, *a_pieces, *b_pieces, w_gate, w_up, w_down)


def backward_kernel(where_ref, y_ref, note_ref, wd_ref, gate_ref, up_ref, hidden_ref, dg_ref, du_ref, spot_ref, sum_ref, y_rows):
    i = pl.program_id(0)
    at_x = where_ref[i]
    spots, notes = [], []
    for j in range(NZ):
        at_z = where_ref[NX + j]
        y_rows[j] = y_ref[at_z]
        note = note_ref[at_z].astype(F32)
        start = ((at_x * NZ + at_z) * 8).astype(F32)
        spots.append(jnp.where(note[:, :LANES] >= 0.0, note[:, :LANES] + start, -1.0))
        notes.append(note[:, LANES:])
    spot = jnp.concatenate(spots, axis=0)
    spot_ref[...] = spot[:, :1]
    notes = jnp.concatenate(notes, axis=0)
    xx = jnp.concatenate([notes[:, :SLOTS] + notes[:, SLOTS : 2 * SLOTS]] * NZ, axis=1)
    yy = jnp.concatenate([notes[:, 2 * SLOTS : 3 * SLOTS] + notes[:, 3 * SLOTS :]] * NZ, axis=1)
    back = dot(y_rows[...].reshape(TILE, D), wd_ref[0], ((1,), (1,)))
    gate, up, hidden = gate_ref[...], up_ref[...], hidden_ref[...]
    sig = jax.nn.sigmoid(gate)
    d_gate = (back * up * sig * (1.0 + gate * (1.0 - sig))).astype(BF)
    d_up = (back * (gate * sig)).astype(BF)
    dg_ref[...] = d_gate
    du_ref[...] = d_up
    last = ((1,), (1,))
    pair = xx * (dot(d_gate, d_gate, last) + dot(d_up, d_up, last)) + yy * dot(hidden, hidden, last)
    same = (spot[:, :1] == spot.T[:1, :]) & (spot[:, :1] >= 0.0)
    row_sums = jnp.sum(jnp.where(same, pair, 0.0), axis=1, keepdims=True)
    lane = lax.broadcasted_iota(jnp.int32, (TILE, LANES), 1).astype(F32)

    @pl.when(i == 0)
    def _():
        sum_ref[...] = jnp.zeros_like(sum_ref)

    for half in range(2):
        hot = spot == lane + half * LANES
        sum_ref[half : half + 1, :] += jnp.sum(jnp.where(hot, row_sums, 0.0), axis=0, keepdims=True)


def backward(where, wide_y, w_down, gate, up, hidden):
    def tall(n):
        return pl.BlockSpec((TILE, n), lambda i, where: (i, 0))

    return pl.pallas_call(
        backward_kernel,
        grid_spec=pltpu.PrefetchScalarGridSpec(
            num_scalar_prefetch=1,
            grid=(NX,),
            in_specs=[
                pl.BlockSpec((NZ, SLOTS, D), lambda i, where: (where[i], 0, 0)),
                pl.BlockSpec((NZ, SLOTS, 2 * LANES), lambda i, where: (where[i], 0, D // (2 * LANES))),
                pl.BlockSpec(w_down.shape, lambda i, where: (0, 0, 0), pipeline_mode=pl.Buffered(1)),
                tall(HID),
                tall(HID),
                tall(HID),
            ],
            out_specs=[tall(HID), tall(HID), tall(1), pl.BlockSpec((2, LANES), lambda i, where: (0, 0))],
            scratch_shapes=[pltpu.VMEM((NZ, SLOTS, D), BF)],
        ),
        out_shape=[
            jax.ShapeDtypeStruct((ROWS, HID), BF),
            jax.ShapeDtypeStruct((ROWS, HID), BF),
            jax.ShapeDtypeStruct((ROWS, 1), F32),
            jax.ShapeDtypeStruct((2, LANES), F32),
        ],
        compiler_params=pltpu.CompilerParams(vmem_limit_bytes=60 * MIB),
        cost_estimate=pl.CostEstimate(flops=3 * ROWS * D * HID, bytes_accessed=12 * MIB, transcendentals=ROWS * HID),
        name="backward",
    )(where, wide_y, wide_y, w_down, gate, up, hidden)


def factor_by_row(spot, factors):
    lane = lax.broadcasted_iota(jnp.int32, (ROWS, LANES), 1).astype(F32)
    factor = jnp.zeros((ROWS, 1), F32)
    for half in range(2):
        chosen = jnp.where(spot == lane + half * LANES, factors[half : half + 1, :], 0.0)
        factor = factor + jnp.sum(chosen, axis=1, keepdims=True)
    return factor


def wide_grads_kernel(x_ref, dg_ref, du_ref, spot_ref, factor_ref, gg_ref, gu_ref, scaled):
    @pl.when(pl.program_id(0) == 0)
    def _():
        factor = factor_by_row(spot_ref[...], factor_ref[...])
        scaled[:, :HID] = (factor * dg_ref[...].astype(F32)).astype(BF)
        scaled[:, HID:] = (factor * du_ref[...].astype(F32)).astype(BF)

    both = dot(x_ref[...].reshape(ROWS, COLS), scaled[...], ((0,), (0,))).astype(BF)
    gg_ref[0] = both[:, :HID]
    gu_ref[0] = both[:, HID:]


def wide_gradients(x, d_gate, d_up, spot, factors):
    def whole(a):
        return pl.BlockSpec(a.shape, lambda i: (0, 0), pipeline_mode=pl.Buffered(1))

    return pl.pallas_call(
        wide_grads_kernel,
        grid=(D // COLS,),
        in_specs=[
            pl.BlockSpec((NX, NZ, SLOTS, COLS), lambda i: (0, 0, 0, i)),
            whole(d_gate),
            whole(d_up),
            whole(spot),
            whole(factors),
        ],
        out_specs=[pl.BlockSpec((1, COLS, HID), lambda i: (0, i, 0))] * 2,
        out_shape=[jax.ShapeDtypeStruct((1, D, HID), BF)] * 2,
        scratch_shapes=[pltpu.VMEM((ROWS, 2 * HID), BF)],
        compiler_params=pltpu.CompilerParams(vmem_limit_bytes=60 * MIB),
        cost_estimate=pl.CostEstimate(flops=ROWS * D, bytes_accessed=MIB, transcendentals=0),
        name="wide_gradients",
    )(x, d_gate, d_up, spot, factors)


def down_grad_kernel(where_ref, y_ref, hidden_ref, spot_ref, factor_ref, gd_ref, turned, moved, by_row):
    @pl.when(pl.program_id(0) == 0)
    def _():
        factor = factor_by_row(spot_ref[...], factor_ref[...])
        for i in range(NX):
            for j in range(NZ):
                block = where_ref[i] * NZ + where_ref[NX + j]
                first = (i * NZ + j) * SLOTS
                moved[block] = hidden_ref[first : first + SLOTS]
                by_row[block] = factor[first : first + SLOTS]
        turned[...] = moved[...].reshape(ROWS, HID).T

    cot = (by_row[...] * y_ref[...].astype(F32)).astype(BF).reshape(ROWS, COLS)
    gd_ref[0] = dot(turned[...], cot, ((1,), (0,))).astype(BF)


def down_gradient(where, wide_y, hidden, spot, factors):
    def whole(a):
        return pl.BlockSpec(a.shape, lambda i, where: (0, 0), pipeline_mode=pl.Buffered(1))

    return pl.pallas_call(
        down_grad_kernel,
        grid_spec=pltpu.PrefetchScalarGridSpec(
            num_scalar_prefetch=1,
            grid=(D // COLS,),
            in_specs=[
                pl.BlockSpec((BLOCKS, SLOTS, COLS), lambda i, where: (0, 0, i)),
                whole(hidden),
                whole(spot),
                whole(factors),
            ],
            out_specs=pl.BlockSpec((1, HID, COLS), lambda i, where: (0, 0, i)),
            scratch_shapes=[
                pltpu.VMEM((HID, ROWS), BF),
                pltpu.VMEM((BLOCKS, SLOTS, HID), BF),
                pltpu.VMEM((BLOCKS, SLOTS, 1), F32),
            ],
        ),
        out_shape=jax.ShapeDtypeStruct((1, HID, D), BF),
        compiler_params=pltpu.CompilerParams(vmem_limit_bytes=60 * MIB),
        cost_estimate=pl.CostEstimate(flops=ROWS * D, bytes_accessed=MIB, transcendentals=0),
        name="down_gradient",
    )(where, wide_y, hidden, spot, factors)


def on_device(tokens, cotangent, routes, example_ids, w_gate, w_up, w_down):
    ix, iz = lax.axis_index("x"), lax.axis_index("z")
    where = jnp.concatenate([(ix + jnp.array(ORDER["x"])) % NX, (iz + jnp.array(ORDER["z"])) % NZ]).astype(jnp.int32)
    tok_count, width = tokens.shape
    flat_routes = routes.reshape(-1)
    owner_hot = (flat_routes[:, None] == jnp.arange(NE)[None, :]).astype(jnp.int32)
    before = jnp.cumsum(owner_hot, axis=0) - owner_hot
    slot_of = flat_routes * CAP + jnp.sum(before * owner_hot, axis=1)
    placed = (jnp.arange(SLOTS)[:, None] == slot_of[None, :]).astype(jnp.int32)
    placed = jnp.sum(placed.reshape(SLOTS, tok_count, 2), axis=2)
    placed_bf = placed.astype(BF)
    filled = jnp.sum(placed, axis=1) > 0
    send_ids = jnp.where(filled, jnp.sum(placed * example_ids.reshape(-1)[None, :], axis=1), -1)
    send_x = jnp.dot(placed_bf, tokens, preferred_element_type=F32).astype(BF)
    send_dy = jnp.dot(placed_bf, cotangent, preferred_element_type=F32).astype(BF)
    id_cols = jnp.broadcast_to(send_ids.astype(BF)[:, None], (SLOTS, LANES))
    send = jnp.concatenate(
        [
            jnp.concatenate([send_x, id_cols], axis=1).reshape(NE, CAP, width + LANES),
            jnp.concatenate([send_dy, id_cols], axis=1).reshape(NE, CAP, width + LANES),
        ],
        axis=1,
    )
    got = lax.all_to_all(send, EXPERT, split_axis=0, concat_axis=0, tiled=True)
    local_x = got[:, :CAP, :width].reshape(SLOTS, width)
    local_dy = got[:, CAP:].reshape(SLOTS, width + LANES)
    last = ((1,), (1,))
    parts = []
    for rows in (local_x, local_dy[:, :width]):
        gram = dot(rows, rows, last)
        high = lax.reduce_precision(gram, 8, 7)
        parts += [high.astype(BF), (gram - high).astype(BF)]
    wide_y = lax.all_gather(jnp.concatenate([local_dy] + parts, axis=1), ("x", "z"), axis=0)
    line_x = jnp.stack(ring_gather(local_x[:MID], "x", False))
    line_z = jnp.stack(ring_gather(local_x[MID:], "z", False))
    a_pieces = ring_gather(line_x, "z", True)
    b_pieces = ring_gather(line_z, "x", True)
    x, gate, up_part, hidden, far, left, right = forward(
        where, a_pieces, b_pieces, w_gate, w_up, w_down
    )
    right, wide_y = lax.optimization_barrier((right, wide_y))
    right_line = lax.psum_scatter(right.reshape(ROWS, D - LEFT), "x", scatter_dimension=0, tiled=True)
    kept = {}

    def hook(step, sent, going):
        if step == 1:
            kept["back"] = backward(where, wide_y, w_down, gate, up_part, hidden)
            sent, kept["sum"] = lax.optimization_barrier((sent, kept["back"][3]))
        elif step == 2:
            total, _ = lax.optimization_barrier((kept["sum"], going))
            total = jnp.sum(spread(total, ("x", "z"), BLOCKS).reshape(BLOCKS, 2, LANES), axis=0)
            sent, kept["sum"], line = lax.optimization_barrier((sent, total, right_line))
            kept["line"] = lax.psum_scatter(line, "z", scatter_dimension=0, tiled=True)
        elif step == 3:
            total, _ = lax.optimization_barrier((kept["sum"], going))
            total = jnp.sum(spread(total, EXPERT, NE).reshape(NE, 2, LANES), axis=0)
            sent, total = lax.optimization_barrier((sent, total))
            kept["norms"] = jnp.sqrt(total)
            kept["factors"] = RADIUS / (kept["norms"] + GAMMA)
        else:
            d_gate, d_up, spot, _ = kept["back"]
            factors, _ = lax.optimization_barrier((kept["factors"], going))
            grads = wide_gradients(x, d_gate, d_up, spot, factors)
            sent, kept["grads"], kept["line"] = lax.optimization_barrier((sent, tuple(grads), kept["line"]))
        return sent

    left_line = ring_sum(far, left, "z", hook)
    right_out = kept["line"]
    left_out = direct_sum(left_line, "x")
    own_out = jnp.concatenate([left_out, right_out], axis=1)
    own_out, late = lax.optimization_barrier((own_out, hidden))
    grad_down = down_gradient(where, wide_y, late, kept["back"][2], kept["factors"])
    returned = lax.all_to_all(own_out.reshape(NE, CAP, width), EXPERT, split_axis=0, concat_axis=0, tiled=True)
    mixed = jnp.dot(placed_bf.T, returned.reshape(SLOTS, width), preferred_element_type=F32).astype(BF)
    norms = kept["norms"]
    own_norms = lax.dynamic_slice(norms.reshape(BLOCKS, 8), (ix * NZ + iz, 0), (1, EX_ROW))
    return (mixed, own_norms, *kept["grads"], grad_down)


def solution(mesh):
    mesh = Mesh(mesh.devices.reshape(NX, NZ, 4, 2), ("x", "z", "y", "c"))
    data, every = ("x", "z"), ("x", "z", "y", "c")
    return jax.shard_map(
        on_device,
        mesh=mesh,
        in_specs=(
            P(every, None),
            P(every, None),
            P(every, None),
            P(data, EXPERT),
            P(EXPERT, None, data),
            P(EXPERT, None, data),
            P(EXPERT, data, None),
        ),
        out_specs=(
            P(every, None),
            P(data, None),
            P(EXPERT, None, data),
            P(EXPERT, None, data),
            P(EXPERT, data, None),
        ),
        check_vma=False,
    )
```

```python
import math

import jax
import jax.numpy as jnp
from jax import lax
from jax.experimental import pallas as pl
from jax.experimental.pallas import tpu as pltpu
from jax.sharding import Mesh, PartitionSpec as P

D = 3072
FF = 8192
CAP = 4
EX_ROW = 6
NX, NZ, NE = 4, 8, 8
BLOCKS = NX * NZ
SLOTS = NE * CAP
ROWS = BLOCKS * SLOTS
HID = FF // BLOCKS
SIZE = {"x": NX, "z": NZ}
ORDER = {"x": (0, -1, 1, 2), "z": (0, -1, 1, -2, 2, -3, 3, 4)}
GAMMA = 0.01
RADIUS = math.sqrt(3.0 * D * FF * NE / (BLOCKS * EX_ROW))
EXPERT = ("y", "c")
BF = jnp.bfloat16
F32 = jnp.float32
MIB = 1 << 20
LANES = 128
TILE = NZ * SLOTS
MID = SLOTS // 2
COLS = 512
LEFT = 2048


def shift(a, axis, step):
    n = SIZE[axis]
    return lax.ppermute(a, axis, [(i, (i + step) % n) for i in range(n)])


def ring_gather(a, axis, split):
    half = SIZE[axis] // 2
    mid = a.shape[-2] // 2
    pieces = [a]
    up = down = a
    for _ in range(1, half):
        up, down = shift(up, axis, 1), shift(down, axis, -1)
        pieces += [up, down]
    if split:
        return pieces + [shift(up[..., :mid, :], axis, 1), shift(down[..., mid:, :], axis, -1)]
    return pieces + [shift(up, axis, 1)]


def plus(a, b):
    return (a.astype(F32) + b.astype(F32)).astype(BF)


def ring_sum(far, parts, axis, hook):
    half = SIZE[axis] // 2
    place = ORDER[axis].index

    def get(k):
        return parts[place(k)]

    own_up, down = hook(1, (get(half - 1), get(1 - half)), far)
    up = plus(shift(far, axis, 1), own_up)
    for k in range(half - 1, 0, -1):
        going = up
        up, down = shift(up, axis, 1), shift(down, axis, -1)
        if k > 1:
            own_up, own_down = hook(half - k + 1, (get(k - 1), get(1 - k)), going)
            up, down = plus(up, own_up), plus(down, own_down)
    own = hook(half, get(0), going)
    return (up.astype(F32) + down.astype(F32) + own.astype(F32)).astype(BF)


def direct_sum(parts, axis):
    total = parts[0].astype(F32)
    for place, k in enumerate(ORDER[axis]):
        if k:
            total = total + shift(parts[place], axis, k).astype(F32)
    return total.astype(BF)


def spread(a, axes, n):
    return lax.all_to_all(jnp.broadcast_to(a[None], (n,) + a.shape), axes, 0, 0, tiled=True)


def dot(a, b, dims):
    return lax.dot_general(a, b, (dims, ((), ())), preferred_element_type=F32)


def forward_kernel(where_ref, *refs):
    a_refs, refs = refs[: NZ + 1], refs[NZ + 1 :]
    b_refs, refs = refs[: NX + 1], refs[NX + 1 :]
    wg_ref, wu_ref, wd_ref, x_out, gate_ref, up_ref, hidden_ref, far_ref, left_ref, right_ref, rows_ref, wg, wu, wd, in_sems, w_sems, out_sems = refs
    step = pl.program_id(0)
    quarter = MID // 2
    arrivals = []
    for i in range(NX):
        moves = [(a_refs[j].at[i], rows_ref.at[i, j, pl.ds(0, MID)]) for j in range(NZ - 1)]
        moves += [(a_refs[NZ - 1 + h].at[i], rows_ref.at[i, NZ - 1, pl.ds(h * quarter, quarter)]) for h in range(2)]
        if i < NX - 1:
            moves += [(b_refs[i], rows_ref.at[i, :, pl.ds(MID, MID)])]
        else:
            moves += [(b_refs[i + h], rows_ref.at[i, :, pl.ds(MID + h * quarter, quarter)]) for h in range(2)]
        arrivals.append([pltpu.make_async_copy(s, d, in_sems.at[i, n]) for n, (s, d) in enumerate(moves)])
    leaving = [pltpu.make_async_copy(rows_ref.at[i], x_out.at[i], out_sems.at[i]) for i in range(NX)]

    weights = [
        pltpu.make_async_copy(s.at[0], d, w_sems.at[n]) for n, (s, d) in enumerate([(wg_ref, wg), (wu_ref, wu), (wd_ref, wd)])
    ]

    @pl.when(step == 0)
    def _():
        for copy in arrivals[0] + weights[:2] + arrivals[1] + weights[2:] + arrivals[2] + arrivals[3]:
            copy.start()
        for copy in weights[:2]:
            copy.wait()

    for i in range(NX):

        @pl.when(step == i)
        def _():
            for copy in arrivals[i]:
                copy.wait()
            leaving[i].start()

    x = rows_ref[step].reshape(TILE, D)
    gate = dot(x, wg[...], ((1,), (0,)))
    up = dot(x, wu[...], ((1,), (0,)))
    hidden = (gate * jax.nn.sigmoid(gate) * up).astype(BF)
    gate_ref[...] = gate
    up_ref[...] = up
    hidden_ref[...] = hidden

    @pl.when(step == 0)
    def _():
        weights[2].wait()

    out = dot(hidden, wd[:, :LEFT], ((1,), (0,))).astype(BF)
    left_ref[...] = out[: TILE - SLOTS].reshape(NZ - 1, 1, SLOTS, LEFT)
    far_ref[0] = out[TILE - SLOTS :]
    out = dot(hidden, wd[:, LEFT:], ((1,), (0,))).astype(BF)
    for j in range(NZ):
        right_ref[0, where_ref[NX + j]] = out[j * SLOTS : (j + 1) * SLOTS]

    @pl.when(step == NX - 1)
    def _():
        for copy in leaving:
            copy.wait()


def forward(where, a_pieces, b_pieces, w_gate, w_up, w_down):
    outside = pl.BlockSpec(memory_space=pltpu.HBM)

    def tall(n):
        return pl.BlockSpec((TILE, n), lambda i, where: (i, 0))

    return pl.pallas_call(
        forward_kernel,
        grid_spec=pltpu.PrefetchScalarGridSpec(
            num_scalar_prefetch=1,
            grid=(NX,),
            in_specs=[outside] * (NZ + NX + 5),
            out_specs=[
                outside,
                tall(HID),
                tall(HID),
                tall(HID),
                pl.BlockSpec((1, SLOTS, LEFT), lambda i, where: (i, 0, 0)),
                pl.BlockSpec((NZ - 1, 1, SLOTS, LEFT), lambda i, where: (0, i, 0, 0)),
                pl.BlockSpec((1, NZ, SLOTS, D - LEFT), lambda i, where: (where[i], 0, 0, 0)),
            ],
            scratch_shapes=[
                pltpu.VMEM((NX, NZ, SLOTS, D), BF),
                pltpu.VMEM((D, HID), BF),
                pltpu.VMEM((D, HID), BF),
                pltpu.VMEM((HID, D), BF),
                pltpu.SemaphoreType.DMA((NX, NZ + 3)),
                pltpu.SemaphoreType.DMA((3,)),
                pltpu.SemaphoreType.DMA((NX,)),
            ],
        ),
        out_shape=[
            jax.ShapeDtypeStruct((NX, NZ, SLOTS, D), BF),
            jax.ShapeDtypeStruct((ROWS, HID), F32),
            jax.ShapeDtypeStruct((ROWS, HID), F32),
            jax.ShapeDtypeStruct((ROWS, HID), BF),
            jax.ShapeDtypeStruct((NX, SLOTS, LEFT), BF),
            jax.ShapeDtypeStruct((NZ - 1, NX, SLOTS, LEFT), BF),
            jax.ShapeDtypeStruct((NX, NZ, SLOTS, D - LEFT), BF),
        ],
        compiler_params=pltpu.CompilerParams(vmem_limit_bytes=60 * MIB),
        cost_estimate=pl.CostEstimate(flops=6 * ROWS * D * HID, bytes_accessed=20 * MIB, transcendentals=ROWS * HID),
        name="forward",
    )(where, *a_pieces, *b_pieces, w_gate, w_up, w_down)


def backward_kernel(where_ref, y_ref, note_ref, wd_ref, gate_ref, up_ref, hidden_ref, dg_ref, du_ref, spot_ref, sum_ref, y_rows):
    i = pl.program_id(0)
    at_x = where_ref[i]
    spots, notes = [], []
    for j in range(NZ):
        at_z = where_ref[NX + j]
        y_rows[j] = y_ref[at_z]
        note = note_ref[at_z].astype(F32)
        start = ((at_x * NZ + at_z) * 8).astype(F32)
        spots.append(jnp.where(note[:, :LANES] >= 0.0, note[:, :LANES] + start, -1.0))
        notes.append(note[:, LANES:])
    spot = jnp.concatenate(spots, axis=0)
    spot_ref[...] = spot[:, :1]
    notes = jnp.concatenate(notes, axis=0)
    xx = jnp.concatenate([notes[:, :SLOTS] + notes[:, SLOTS : 2 * SLOTS]] * NZ, axis=1)
    yy = jnp.concatenate([notes[:, 2 * SLOTS : 3 * SLOTS] + notes[:, 3 * SLOTS :]] * NZ, axis=1)
    back = dot(y_rows[...].reshape(TILE, D), wd_ref[0], ((1,), (1,)))
    gate, up, hidden = gate_ref[...], up_ref[...], hidden_ref[...]
    sig = jax.nn.sigmoid(gate)
    d_gate = (back * up * sig * (1.0 + gate * (1.0 - sig))).astype(BF)
    d_up = (back * (gate * sig)).astype(BF)
    dg_ref[...] = d_gate
    du_ref[...] = d_up
    last = ((1,), (1,))
    pair = xx * (dot(d_gate, d_gate, last) + dot(d_up, d_up, last)) + yy * dot(hidden, hidden, last)
    same = (spot[:, :1] == spot.T[:1, :]) & (spot[:, :1] >= 0.0)
    row_sums = jnp.sum(jnp.where(same, pair, 0.0), axis=1, keepdims=True)
    lane = lax.broadcasted_iota(jnp.int32, (TILE, LANES), 1).astype(F32)

    @pl.when(i == 0)
    def _():
        sum_ref[...] = jnp.zeros_like(sum_ref)

    for half in range(2):
        hot = spot == lane + half * LANES
        sum_ref[half : half + 1, :] += jnp.sum(jnp.where(hot, row_sums, 0.0), axis=0, keepdims=True)


def backward(where, wide_y, w_down, gate, up, hidden):
    def tall(n):
        return pl.BlockSpec((TILE, n), lambda i, where: (i, 0))

    return pl.pallas_call(
        backward_kernel,
        grid_spec=pltpu.PrefetchScalarGridSpec(
            num_scalar_prefetch=1,
            grid=(NX,),
            in_specs=[
                pl.BlockSpec((NZ, SLOTS, D), lambda i, where: (where[i], 0, 0)),
                pl.BlockSpec((NZ, SLOTS, 2 * LANES), lambda i, where: (where[i], 0, D // (2 * LANES))),
                pl.BlockSpec(w_down.shape, lambda i, where: (0, 0, 0), pipeline_mode=pl.Buffered(1)),
                tall(HID),
                tall(HID),
                tall(HID),
            ],
            out_specs=[tall(HID), tall(HID), tall(1), pl.BlockSpec((2, LANES), lambda i, where: (0, 0))],
            scratch_shapes=[pltpu.VMEM((NZ, SLOTS, D), BF)],
        ),
        out_shape=[
            jax.ShapeDtypeStruct((ROWS, HID), BF),
            jax.ShapeDtypeStruct((ROWS, HID), BF),
            jax.ShapeDtypeStruct((ROWS, 1), F32),
            jax.ShapeDtypeStruct((2, LANES), F32),
        ],
        compiler_params=pltpu.CompilerParams(vmem_limit_bytes=60 * MIB),
        cost_estimate=pl.CostEstimate(flops=3 * ROWS * D * HID, bytes_accessed=12 * MIB, transcendentals=ROWS * HID),
        name="backward",
    )(where, wide_y, wide_y, w_down, gate, up, hidden)


def factor_by_row(spot, factors):
    lane = lax.broadcasted_iota(jnp.int32, (ROWS, LANES), 1).astype(F32)
    factor = jnp.zeros((ROWS, 1), F32)
    for half in range(2):
        chosen = jnp.where(spot == lane + half * LANES, factors[half : half + 1, :], 0.0)
        factor = factor + jnp.sum(chosen, axis=1, keepdims=True)
    return factor


def wide_grads_kernel(x_ref, dg_ref, du_ref, spot_ref, factor_ref, gg_ref, gu_ref, scaled):
    @pl.when(pl.program_id(0) == 0)
    def _():
        factor = factor_by_row(spot_ref[...], factor_ref[...])
        scaled[:, :HID] = (factor * dg_ref[...].astype(F32)).astype(BF)
        scaled[:, HID:] = (factor * du_ref[...].astype(F32)).astype(BF)

    both = dot(x_ref[...].reshape(ROWS, COLS), scaled[...], ((0,), (0,))).astype(BF)
    gg_ref[0] = both[:, :HID]
    gu_ref[0] = both[:, HID:]


def wide_gradients(x, d_gate, d_up, spot, factors):
    def whole(a):
        return pl.BlockSpec(a.shape, lambda i: (0, 0), pipeline_mode=pl.Buffered(1))

    return pl.pallas_call(
        wide_grads_kernel,
        grid=(D // COLS,),
        in_specs=[
            pl.BlockSpec((NX, NZ, SLOTS, COLS), lambda i: (0, 0, 0, i)),
            whole(d_gate),
            whole(d_up),
            whole(spot),
            whole(factors),
        ],
        out_specs=[pl.BlockSpec((1, COLS, HID), lambda i: (0, i, 0))] * 2,
        out_shape=[jax.ShapeDtypeStruct((1, D, HID), BF)] * 2,
        scratch_shapes=[pltpu.VMEM((ROWS, 2 * HID), BF)],
        compiler_params=pltpu.CompilerParams(vmem_limit_bytes=60 * MIB),
        cost_estimate=pl.CostEstimate(flops=ROWS * D, bytes_accessed=MIB, transcendentals=0),
        name="wide_gradients",
    )(x, d_gate, d_up, spot, factors)


def down_grad_kernel(where_ref, y_ref, hidden_ref, spot_ref, factor_ref, gd_ref, turned, moved, by_row):
    @pl.when(pl.program_id(0) == 0)
    def _():
        factor = factor_by_row(spot_ref[...], factor_ref[...])
        for i in range(NX):
            for j in range(NZ):
                block = where_ref[i] * NZ + where_ref[NX + j]
                first = (i * NZ + j) * SLOTS
                moved[block] = hidden_ref[first : first + SLOTS]
                by_row[block] = factor[first : first + SLOTS]
        turned[...] = moved[...].reshape(ROWS, HID).T

    cot = (by_row[...] * y_ref[...].astype(F32)).astype(BF).reshape(ROWS, COLS)
    gd_ref[0] = dot(turned[...], cot, ((1,), (0,))).astype(BF)


def down_gradient(where, wide_y, hidden, spot, factors):
    def whole(a):
        return pl.BlockSpec(a.shape, lambda i, where: (0, 0), pipeline_mode=pl.Buffered(1))

    return pl.pallas_call(
        down_grad_kernel,
        grid_spec=pltpu.PrefetchScalarGridSpec(
            num_scalar_prefetch=1,
            grid=(D // COLS,),
            in_specs=[
                pl.BlockSpec((BLOCKS, SLOTS, COLS), lambda i, where: (0, 0, i)),
                whole(hidden),
                whole(spot),
                whole(factors),
            ],
            out_specs=pl.BlockSpec((1, HID, COLS), lambda i, where: (0, 0, i)),
            scratch_shapes=[
                pltpu.VMEM((HID, ROWS), BF),
                pltpu.VMEM((BLOCKS, SLOTS, HID), BF),
                pltpu.VMEM((BLOCKS, SLOTS, 1), F32),
            ],
        ),
        out_shape=jax.ShapeDtypeStruct((1, HID, D), BF),
        compiler_params=pltpu.CompilerParams(vmem_limit_bytes=60 * MIB),
        cost_estimate=pl.CostEstimate(flops=ROWS * D, bytes_accessed=MIB, transcendentals=0),
        name="down_gradient",
    )(where, wide_y, hidden, spot, factors)


def on_device(tokens, cotangent, routes, example_ids, w_gate, w_up, w_down):
    ix, iz = lax.axis_index("x"), lax.axis_index("z")
    where = jnp.concatenate([(ix + jnp.array(ORDER["x"])) % NX, (iz + jnp.array(ORDER["z"])) % NZ]).astype(jnp.int32)
    tok_count, width = tokens.shape
    flat_routes = routes.reshape(-1)
    owner_hot = (flat_routes[:, None] == jnp.arange(NE)[None, :]).astype(jnp.int32)
    before = jnp.cumsum(owner_hot, axis=0) - owner_hot
    slot_of = flat_routes * CAP + jnp.sum(before * owner_hot, axis=1)
    placed = (jnp.arange(SLOTS)[:, None] == slot_of[None, :]).astype(jnp.int32)
    placed = jnp.sum(placed.reshape(SLOTS, tok_count, 2), axis=2)
    placed_bf = placed.astype(BF)
    filled = jnp.sum(placed, axis=1) > 0
    send_ids = jnp.where(filled, jnp.sum(placed * example_ids.reshape(-1)[None, :], axis=1), -1)
    send_x = jnp.dot(placed_bf, tokens, preferred_element_type=F32).astype(BF)
    send_dy = jnp.dot(placed_bf, cotangent, preferred_element_type=F32).astype(BF)
    id_cols = jnp.broadcast_to(send_ids.astype(BF)[:, None], (SLOTS, LANES))
    send = jnp.concatenate(
        [
            jnp.concatenate([send_x, id_cols], axis=1).reshape(NE, CAP, width + LANES),
            jnp.concatenate([send_dy, id_cols], axis=1).reshape(NE, CAP, width + LANES),
        ],
        axis=1,
    )
    got = lax.all_to_all(send, EXPERT, split_axis=0, concat_axis=0, tiled=True)
    local_x = got[:, :CAP, :width].reshape(SLOTS, width)
    local_dy = got[:, CAP:].reshape(SLOTS, width + LANES)
    last = ((1,), (1,))
    parts = []
    for rows in (local_x, local_dy[:, :width]):
        gram = dot(rows, rows, last)
        high = lax.reduce_precision(gram, 8, 7)
        parts += [high.astype(BF), (gram - high).astype(BF)]
    wide_y = lax.all_gather(jnp.concatenate([local_dy] + parts, axis=1), ("x", "z"), axis=0)
    line_x = jnp.stack(ring_gather(local_x[:MID], "x", False))
    line_z = jnp.stack(ring_gather(local_x[MID:], "z", False))
    a_pieces = ring_gather(line_x, "z", True)
    b_pieces = ring_gather(line_z, "x", True)
    x, gate, up_part, hidden, far, left, right = forward(
        where, a_pieces, b_pieces, w_gate, w_up, w_down
    )
    right, wide_y = lax.optimization_barrier((right, wide_y))
    right_line = lax.psum_scatter(right.reshape(ROWS, D - LEFT), "x", scatter_dimension=0, tiled=True)
    kept = {}

    def hook(step, sent, going):
        if step == 1:
            kept["back"] = backward(where, wide_y, w_down, gate, up_part, hidden)
            sent, kept["sum"] = lax.optimization_barrier((sent, kept["back"][3]))
        elif step == 2:
            total, _ = lax.optimization_barrier((kept["sum"], going))
            total = jnp.sum(spread(total, ("x", "z"), BLOCKS).reshape(BLOCKS, 2, LANES), axis=0)
            sent, kept["sum"], line = lax.optimization_barrier((sent, total, right_line))
            kept["line"] = lax.psum_scatter(line, "z", scatter_dimension=0, tiled=True)
        elif step == 3:
            total, _ = lax.optimization_barrier((kept["sum"], going))
            total = jnp.sum(spread(total, EXPERT, NE).reshape(NE, 2, LANES), axis=0)
            kept["norms"] = jnp.sqrt(total)
            kept["factors"] = RADIUS / (kept["norms"] + GAMMA)
            grad = down_gradient(where, wide_y, hidden, kept["back"][2], kept["factors"])
            sent, kept["down"], kept["line"] = lax.optimization_barrier((sent, grad, kept["line"]))
        else:
            d_gate, d_up, spot, _ = kept["back"]
            factors, _ = lax.optimization_barrier((kept["factors"], going))
            grads = wide_gradients(x, d_gate, d_up, spot, factors)
            sent, kept["grads"] = lax.optimization_barrier((sent, tuple(grads)))
        return sent

    left_line = ring_sum(far, left, "z", hook)
    right_out = kept["line"]
    left_out = direct_sum(left_line, "x")
    own_out = jnp.concatenate([left_out, right_out], axis=1)
    returned = lax.all_to_all(own_out.reshape(NE, CAP, width), EXPERT, split_axis=0, concat_axis=0, tiled=True)
    mixed = jnp.dot(placed_bf.T, returned.reshape(SLOTS, width), preferred_element_type=F32).astype(BF)
    norms = kept["norms"]
    own_norms = lax.dynamic_slice(norms.reshape(BLOCKS, 8), (ix * NZ + iz, 0), (1, EX_ROW))
    return (mixed, own_norms, *kept["grads"], kept["down"])


def solution(mesh):
    mesh = Mesh(mesh.devices.reshape(NX, NZ, 4, 2), ("x", "z", "y", "c"))
    data, every = ("x", "z"), ("x", "z", "y", "c")
    return jax.shard_map(
        on_device,
        mesh=mesh,
        in_specs=(
            P(every, None),
            P(every, None),
            P(every, None),
            P(data, EXPERT),
            P(EXPERT, None, data),
            P(EXPERT, None, data),
            P(EXPERT, data, None),
        ),
        out_specs=(
            P(every, None),
            P(data, None),
            P(EXPERT, None, data),
            P(EXPERT, None, data),
            P(EXPERT, data, None),
        ),
        check_vma=False,
    )
```

```python
import math

import jax
import jax.numpy as jnp
from jax import lax
from jax.experimental import pallas as pl
from jax.experimental.pallas import tpu as pltpu
from jax.sharding import Mesh, PartitionSpec as P

D = 3072
FF = 8192
CAP = 4
EX_ROW = 6
NX, NZ, NE = 4, 8, 8
BLOCKS = NX * NZ
SLOTS = NE * CAP
ROWS = BLOCKS * SLOTS
HID = FF // BLOCKS
SIZE = {"x": NX, "z": NZ}
ORDER = {"x": (0, -1, 1, 2), "z": (0, -1, 1, -2, 2, -3, 3, 4)}
GAMMA = 0.01
RADIUS = math.sqrt(3.0 * D * FF * NE / (BLOCKS * EX_ROW))
EXPERT = ("y", "c")
BF = jnp.bfloat16
F32 = jnp.float32
MIB = 1 << 20
LANES = 128
TILE = NZ * SLOTS
MID = SLOTS // 2
COLS = 512
LEFT = 2048


def shift(a, axis, step):
    n = SIZE[axis]
    return lax.ppermute(a, axis, [(i, (i + step) % n) for i in range(n)])


def ring_gather(a, axis, split):
    half = SIZE[axis] // 2
    mid = a.shape[-2] // 2
    pieces = [a]
    up = down = a
    for _ in range(1, half):
        up, down = shift(up, axis, 1), shift(down, axis, -1)
        pieces += [up, down]
    if split:
        return pieces + [shift(up[..., :mid, :], axis, 1), shift(down[..., mid:, :], axis, -1)]
    return pieces + [shift(up, axis, 1)]


def plus(a, b):
    return (a.astype(F32) + b.astype(F32)).astype(BF)


def ring_sum(far, parts, axis, hook):
    half = SIZE[axis] // 2
    place = ORDER[axis].index

    def get(k):
        return parts[place(k)]

    up = plus(hook(1, shift(far, axis, 1), far), get(half - 1))
    down = get(1 - half)
    for k in range(half - 1, 0, -1):
        going = up
        up, down = shift(up, axis, 1), shift(down, axis, -1)
        if k > 1:
            up, down = hook(half - k + 1, (up, down), going)
            up, down = plus(up, get(k - 1)), plus(down, get(1 - k))
    up, down = hook(half, (up, down), going)
    own = get(0)
    return (up.astype(F32) + down.astype(F32) + own.astype(F32)).astype(BF)


def direct_sum(parts, axis):
    total = parts[0].astype(F32)
    for place, k in enumerate(ORDER[axis]):
        if k:
            total = total + shift(parts[place], axis, k).astype(F32)
    return total.astype(BF)


def spread(a, axes, n):
    return lax.all_to_all(jnp.broadcast_to(a[None], (n,) + a.shape), axes, 0, 0, tiled=True)


def dot(a, b, dims):
    return lax.dot_general(a, b, (dims, ((), ())), preferred_element_type=F32)


def forward_kernel(where_ref, *refs):
    a_refs, refs = refs[: NZ + 1], refs[NZ + 1 :]
    b_refs, refs = refs[: NX + 1], refs[NX + 1 :]
    wg_ref, wu_ref, wd_ref, x_out, gate_ref, up_ref, hidden_ref, far_ref, left_ref, right_ref, rows_ref, wg, wu, wd, in_sems, w_sems, out_sems = refs
    step = pl.program_id(0)
    quarter = MID // 2
    arrivals = []
    for i in range(NX):
        moves = [(a_refs[j].at[i], rows_ref.at[i, j, pl.ds(0, MID)]) for j in range(NZ - 1)]
        moves += [(a_refs[NZ - 1 + h].at[i], rows_ref.at[i, NZ - 1, pl.ds(h * quarter, quarter)]) for h in range(2)]
        if i < NX - 1:
            moves += [(b_refs[i], rows_ref.at[i, :, pl.ds(MID, MID)])]
        else:
            moves += [(b_refs[i + h], rows_ref.at[i, :, pl.ds(MID + h * quarter, quarter)]) for h in range(2)]
        arrivals.append([pltpu.make_async_copy(s, d, in_sems.at[i, n]) for n, (s, d) in enumerate(moves)])
    leaving = [pltpu.make_async_copy(rows_ref.at[i], x_out.at[i], out_sems.at[i]) for i in range(NX)]

    weights = [
        pltpu.make_async_copy(s.at[0], d, w_sems.at[n]) for n, (s, d) in enumerate([(wg_ref, wg), (wu_ref, wu), (wd_ref, wd)])
    ]

    @pl.when(step == 0)
    def _():
        for copy in arrivals[0] + weights[:2] + arrivals[1] + weights[2:] + arrivals[2] + arrivals[3]:
            copy.start()
        for copy in weights[:2]:
            copy.wait()

    for i in range(NX):

        @pl.when(step == i)
        def _():
            for copy in arrivals[i]:
                copy.wait()
            leaving[i].start()

    x = rows_ref[step].reshape(TILE, D)
    gate = dot(x, wg[...], ((1,), (0,)))
    up = dot(x, wu[...], ((1,), (0,)))
    hidden = (gate * jax.nn.sigmoid(gate) * up).astype(BF)
    gate_ref[...] = gate
    up_ref[...] = up
    hidden_ref[...] = hidden

    @pl.when(step == 0)
    def _():
        weights[2].wait()

    out = dot(hidden, wd[:, :LEFT], ((1,), (0,))).astype(BF)
    left_ref[...] = out[: TILE - SLOTS].reshape(NZ - 1, 1, SLOTS, LEFT)
    far_ref[0] = out[TILE - SLOTS :]
    out = dot(hidden, wd[:, LEFT:], ((1,), (0,))).astype(BF)
    for j in range(NZ):
        right_ref[0, where_ref[NX + j]] = out[j * SLOTS : (j + 1) * SLOTS]

    @pl.when(step == NX - 1)
    def _():
        for copy in leaving:
            copy.wait()


def forward(where, a_pieces, b_pieces, w_gate, w_up, w_down):
    outside = pl.BlockSpec(memory_space=pltpu.HBM)

    def tall(n):
        return pl.BlockSpec((TILE, n), lambda i, where: (i, 0))

    return pl.pallas_call(
        forward_kernel,
        grid_spec=pltpu.PrefetchScalarGridSpec(
            num_scalar_prefetch=1,
            grid=(NX,),
            in_specs=[outside] * (NZ + NX + 5),
            out_specs=[
                outside,
                tall(HID),
                tall(HID),
                tall(HID),
                pl.BlockSpec((1, SLOTS, LEFT), lambda i, where: (i, 0, 0)),
                pl.BlockSpec((NZ - 1, 1, SLOTS, LEFT), lambda i, where: (0, i, 0, 0)),
                pl.BlockSpec((1, NZ, SLOTS, D - LEFT), lambda i, where: (where[i], 0, 0, 0)),
            ],
            scratch_shapes=[
                pltpu.VMEM((NX, NZ, SLOTS, D), BF),
                pltpu.VMEM((D, HID), BF),
                pltpu.VMEM((D, HID), BF),
                pltpu.VMEM((HID, D), BF),
                pltpu.SemaphoreType.DMA((NX, NZ + 3)),
                pltpu.SemaphoreType.DMA((3,)),
                pltpu.SemaphoreType.DMA((NX,)),
            ],
        ),
        out_shape=[
            jax.ShapeDtypeStruct((NX, NZ, SLOTS, D), BF),
            jax.ShapeDtypeStruct((ROWS, HID), F32),
            jax.ShapeDtypeStruct((ROWS, HID), F32),
            jax.ShapeDtypeStruct((ROWS, HID), BF),
            jax.ShapeDtypeStruct((NX, SLOTS, LEFT), BF),
            jax.ShapeDtypeStruct((NZ - 1, NX, SLOTS, LEFT), BF),
            jax.ShapeDtypeStruct((NX, NZ, SLOTS, D - LEFT), BF),
        ],
        compiler_params=pltpu.CompilerParams(vmem_limit_bytes=60 * MIB),
        cost_estimate=pl.CostEstimate(flops=6 * ROWS * D * HID, bytes_accessed=20 * MIB, transcendentals=ROWS * HID),
        name="forward",
    )(where, *a_pieces, *b_pieces, w_gate, w_up, w_down)


def backward_kernel(where_ref, y_ref, note_ref, wd_ref, gate_ref, up_ref, hidden_ref, dg_ref, du_ref, spot_ref, sum_ref, y_rows):
    i = pl.program_id(0)
    at_x = where_ref[i]
    spots, notes = [], []
    for j in range(NZ):
        at_z = where_ref[NX + j]
        y_rows[j] = y_ref[at_z]
        note = note_ref[at_z].astype(F32)
        start = ((at_x * NZ + at_z) * 8).astype(F32)
        spots.append(jnp.where(note[:, :LANES] >= 0.0, note[:, :LANES] + start, -1.0))
        notes.append(note[:, LANES:])
    spot = jnp.concatenate(spots, axis=0)
    spot_ref[...] = spot[:, :1]
    notes = jnp.concatenate(notes, axis=0)
    xx = jnp.concatenate([notes[:, :SLOTS] + notes[:, SLOTS : 2 * SLOTS]] * NZ, axis=1)
    yy = jnp.concatenate([notes[:, 2 * SLOTS : 3 * SLOTS] + notes[:, 3 * SLOTS :]] * NZ, axis=1)
    back = dot(y_rows[...].reshape(TILE, D), wd_ref[0], ((1,), (1,)))
    gate, up, hidden = gate_ref[...], up_ref[...], hidden_ref[...]
    sig = jax.nn.sigmoid(gate)
    d_gate = (back * up * sig * (1.0 + gate * (1.0 - sig))).astype(BF)
    d_up = (back * (gate * sig)).astype(BF)
    dg_ref[...] = d_gate
    du_ref[...] = d_up
    last = ((1,), (1,))
    pair = xx * (dot(d_gate, d_gate, last) + dot(d_up, d_up, last)) + yy * dot(hidden, hidden, last)
    same = (spot[:, :1] == spot.T[:1, :]) & (spot[:, :1] >= 0.0)
    row_sums = jnp.sum(jnp.where(same, pair, 0.0), axis=1, keepdims=True)
    lane = lax.broadcasted_iota(jnp.int32, (TILE, LANES), 1).astype(F32)

    @pl.when(i == 0)
    def _():
        sum_ref[...] = jnp.zeros_like(sum_ref)

    for half in range(2):
        hot = spot == lane + half * LANES
        sum_ref[half : half + 1, :] += jnp.sum(jnp.where(hot, row_sums, 0.0), axis=0, keepdims=True)


def backward(where, wide_y, w_down, gate, up, hidden):
    def tall(n):
        return pl.BlockSpec((TILE, n), lambda i, where: (i, 0))

    return pl.pallas_call(
        backward_kernel,
        grid_spec=pltpu.PrefetchScalarGridSpec(
            num_scalar_prefetch=1,
            grid=(NX,),
            in_specs=[
                pl.BlockSpec((NZ, SLOTS, D), lambda i, where: (where[i], 0, 0)),
                pl.BlockSpec((NZ, SLOTS, 2 * LANES), lambda i, where: (where[i], 0, D // (2 * LANES))),
                pl.BlockSpec(w_down.shape, lambda i, where: (0, 0, 0), pipeline_mode=pl.Buffered(1)),
                tall(HID),
                tall(HID),
                tall(HID),
            ],
            out_specs=[tall(HID), tall(HID), tall(1), pl.BlockSpec((2, LANES), lambda i, where: (0, 0))],
            scratch_shapes=[pltpu.VMEM((NZ, SLOTS, D), BF)],
        ),
        out_shape=[
            jax.ShapeDtypeStruct((ROWS, HID), BF),
            jax.ShapeDtypeStruct((ROWS, HID), BF),
            jax.ShapeDtypeStruct((ROWS, 1), F32),
            jax.ShapeDtypeStruct((2, LANES), F32),
        ],
        compiler_params=pltpu.CompilerParams(vmem_limit_bytes=60 * MIB),
        cost_estimate=pl.CostEstimate(flops=3 * ROWS * D * HID, bytes_accessed=12 * MIB, transcendentals=ROWS * HID),
        name="backward",
    )(where, wide_y, wide_y, w_down, gate, up, hidden)


def factor_by_row(spot, factors):
    lane = lax.broadcasted_iota(jnp.int32, (ROWS, LANES), 1).astype(F32)
    factor = jnp.zeros((ROWS, 1), F32)
    for half in range(2):
        chosen = jnp.where(spot == lane + half * LANES, factors[half : half + 1, :], 0.0)
        factor = factor + jnp.sum(chosen, axis=1, keepdims=True)
    return factor


def wide_grads_kernel(x_ref, dg_ref, du_ref, spot_ref, factor_ref, gg_ref, gu_ref, scaled):
    @pl.when(pl.program_id(0) == 0)
    def _():
        factor = factor_by_row(spot_ref[...], factor_ref[...])
        scaled[:, :HID] = (factor * dg_ref[...].astype(F32)).astype(BF)
        scaled[:, HID:] = (factor * du_ref[...].astype(F32)).astype(BF)

    both = dot(x_ref[...].reshape(ROWS, COLS), scaled[...], ((0,), (0,))).astype(BF)
    gg_ref[0] = both[:, :HID]
    gu_ref[0] = both[:, HID:]


def wide_gradients(x, d_gate, d_up, spot, factors):
    def whole(a):
        return pl.BlockSpec(a.shape, lambda i: (0, 0), pipeline_mode=pl.Buffered(1))

    return pl.pallas_call(
        wide_grads_kernel,
        grid=(D // COLS,),
        in_specs=[
            pl.BlockSpec((NX, NZ, SLOTS, COLS), lambda i: (0, 0, 0, i)),
            whole(d_gate),
            whole(d_up),
            whole(spot),
            whole(factors),
        ],
        out_specs=[pl.BlockSpec((1, COLS, HID), lambda i: (0, i, 0))] * 2,
        out_shape=[jax.ShapeDtypeStruct((1, D, HID), BF)] * 2,
        scratch_shapes=[pltpu.VMEM((ROWS, 2 * HID), BF)],
        compiler_params=pltpu.CompilerParams(vmem_limit_bytes=60 * MIB),
        cost_estimate=pl.CostEstimate(flops=ROWS * D, bytes_accessed=MIB, transcendentals=0),
        name="wide_gradients",
    )(x, d_gate, d_up, spot, factors)


def down_grad_kernel(where_ref, y_ref, hidden_ref, spot_ref, factor_ref, gd_ref, turned, moved, by_row):
    @pl.when(pl.program_id(0) == 0)
    def _():
        factor = factor_by_row(spot_ref[...], factor_ref[...])
        for i in range(NX):
            for j in range(NZ):
                block = where_ref[i] * NZ + where_ref[NX + j]
                first = (i * NZ + j) * SLOTS
                moved[block] = hidden_ref[first : first + SLOTS]
                by_row[block] = factor[first : first + SLOTS]
        turned[...] = moved[...].reshape(ROWS, HID).T

    cot = (by_row[...] * y_ref[...].astype(F32)).astype(BF).reshape(ROWS, COLS)
    gd_ref[0] = dot(turned[...], cot, ((1,), (0,))).astype(BF)


def down_gradient(where, wide_y, hidden, spot, factors):
    def whole(a):
        return pl.BlockSpec(a.shape, lambda i, where: (0, 0), pipeline_mode=pl.Buffered(1))

    return pl.pallas_call(
        down_grad_kernel,
        grid_spec=pltpu.PrefetchScalarGridSpec(
            num_scalar_prefetch=1,
            grid=(D // COLS,),
            in_specs=[
                pl.BlockSpec((BLOCKS, SLOTS, COLS), lambda i, where: (0, 0, i)),
                whole(hidden),
                whole(spot),
                whole(factors),
            ],
            out_specs=pl.BlockSpec((1, HID, COLS), lambda i, where: (0, 0, i)),
            scratch_shapes=[
                pltpu.VMEM((HID, ROWS), BF),
                pltpu.VMEM((BLOCKS, SLOTS, HID), BF),
                pltpu.VMEM((BLOCKS, SLOTS, 1), F32),
            ],
        ),
        out_shape=jax.ShapeDtypeStruct((1, HID, D), BF),
        compiler_params=pltpu.CompilerParams(vmem_limit_bytes=60 * MIB),
        cost_estimate=pl.CostEstimate(flops=ROWS * D, bytes_accessed=MIB, transcendentals=0),
        name="down_gradient",
    )(where, wide_y, hidden, spot, factors)


def on_device(tokens, cotangent, routes, example_ids, w_gate, w_up, w_down):
    ix, iz = lax.axis_index("x"), lax.axis_index("z")
    where = jnp.concatenate([(ix + jnp.array(ORDER["x"])) % NX, (iz + jnp.array(ORDER["z"])) % NZ]).astype(jnp.int32)
    tok_count, width = tokens.shape
    flat_routes = routes.reshape(-1)
    owner_hot = (flat_routes[:, None] == jnp.arange(NE)[None, :]).astype(jnp.int32)
    before = jnp.cumsum(owner_hot, axis=0) - owner_hot
    slot_of = flat_routes * CAP + jnp.sum(before * owner_hot, axis=1)
    placed = (jnp.arange(SLOTS)[:, None] == slot_of[None, :]).astype(jnp.int32)
    placed = jnp.sum(placed.reshape(SLOTS, tok_count, 2), axis=2)
    placed_bf = placed.astype(BF)
    filled = jnp.sum(placed, axis=1) > 0
    send_ids = jnp.where(filled, jnp.sum(placed * example_ids.reshape(-1)[None, :], axis=1), -1)
    send_x = jnp.dot(placed_bf, tokens, preferred_element_type=F32).astype(BF)
    send_dy = jnp.dot(placed_bf, cotangent, preferred_element_type=F32).astype(BF)
    id_cols = jnp.broadcast_to(send_ids.astype(BF)[:, None], (SLOTS, LANES))
    send = jnp.concatenate(
        [
            jnp.concatenate([send_x, id_cols], axis=1).reshape(NE, CAP, width + LANES),
            jnp.concatenate([send_dy, id_cols], axis=1).reshape(NE, CAP, width + LANES),
        ],
        axis=1,
    )
    got = lax.all_to_all(send, EXPERT, split_axis=0, concat_axis=0, tiled=True)
    local_x = got[:, :CAP, :width].reshape(SLOTS, width)
    local_dy = got[:, CAP:].reshape(SLOTS, width + LANES)
    last = ((1,), (1,))
    parts = []
    for rows in (local_x, local_dy[:, :width]):
        gram = dot(rows, rows, last)
        high = lax.reduce_precision(gram, 8, 7)
        parts += [high.astype(BF), (gram - high).astype(BF)]
    wide_y = lax.all_gather(jnp.concatenate([local_dy] + parts, axis=1), ("x", "z"), axis=0)
    line_x = jnp.stack(ring_gather(local_x[:MID], "x", False))
    line_z = jnp.stack(ring_gather(local_x[MID:], "z", False))
    a_pieces = ring_gather(line_x, "z", True)
    b_pieces = ring_gather(line_z, "x", True)
    x, gate, up_part, hidden, far, left, right = forward(
        where, a_pieces, b_pieces, w_gate, w_up, w_down
    )
    right, wide_y = lax.optimization_barrier((right, wide_y))
    right_line = lax.psum_scatter(right.reshape(ROWS, D - LEFT), "x", scatter_dimension=0, tiled=True)
    kept = {}

    def hook(step, sent, going):
        if step == 1:
            kept["back"] = backward(where, wide_y, w_down, gate, up_part, hidden)
            sent, kept["sum"] = lax.optimization_barrier((sent, kept["back"][3]))
        elif step == 2:
            total, _ = lax.optimization_barrier((kept["sum"], going))
            total = jnp.sum(spread(total, ("x", "z"), BLOCKS).reshape(BLOCKS, 2, LANES), axis=0)
            sent, kept["sum"], line = lax.optimization_barrier((sent, total, right_line))
            kept["line"] = lax.psum_scatter(line, "z", scatter_dimension=0, tiled=True)
        elif step == 3:
            total, _ = lax.optimization_barrier((kept["sum"], going))
            total = jnp.sum(spread(total, EXPERT, NE).reshape(NE, 2, LANES), axis=0)
            kept["norms"] = jnp.sqrt(total)
            kept["factors"] = RADIUS / (kept["norms"] + GAMMA)
            grad = down_gradient(where, wide_y, hidden, kept["back"][2], kept["factors"])
            sent, kept["down"], kept["line"] = lax.optimization_barrier((sent, grad, kept["line"]))
        else:
            d_gate, d_up, spot, _ = kept["back"]
            factors, _ = lax.optimization_barrier((kept["factors"], going))
            grads = wide_gradients(x, d_gate, d_up, spot, factors)
            sent, kept["grads"] = lax.optimization_barrier((sent, tuple(grads)))
        return sent

    left_line = ring_sum(far, left, "z", hook)
    right_out = kept["line"]
    left_out = direct_sum(left_line, "x")
    own_out = jnp.concatenate([left_out, right_out], axis=1)
    returned = lax.all_to_all(own_out.reshape(NE, CAP, width), EXPERT, split_axis=0, concat_axis=0, tiled=True)
    mixed = jnp.dot(placed_bf.T, returned.reshape(SLOTS, width), preferred_element_type=F32).astype(BF)
    norms = kept["norms"]
    own_norms = lax.dynamic_slice(norms.reshape(BLOCKS, 8), (ix * NZ + iz, 0), (1, EX_ROW))
    return (mixed, own_norms, *kept["grads"], kept["down"])


def solution(mesh):
    mesh = Mesh(mesh.devices.reshape(NX, NZ, 4, 2), ("x", "z", "y", "c"))
    data, every = ("x", "z"), ("x", "z", "y", "c")
    return jax.shard_map(
        on_device,
        mesh=mesh,
        in_specs=(
            P(every, None),
            P(every, None),
            P(every, None),
            P(data, EXPERT),
            P(EXPERT, None, data),
            P(EXPERT, None, data),
            P(EXPERT, data, None),
        ),
        out_specs=(
            P(every, None),
            P(data, None),
            P(EXPERT, None, data),
            P(EXPERT, None, data),
            P(EXPERT, data, None),
        ),
        check_vma=False,
    )
```
